32 devices in a mesh: groups: 2 (over y), mesh: 4 (over z), feat: 4 (over x, core).
Axes of the slice: x: 2, y: 2, z: 4, core: 2. Of those that a mesh axis runs over, the one named last changes fastest.
Arguments:
- nodes: bfloat16 [8192, 512], P(('groups', 'mesh')), parts along dimension 0, may hold values from -6 to 6
- fine_edges: bfloat16 [49152, 512], P(('groups', 'mesh', 'feat')), parts along dimension 0, may hold values from -6 to 6
- fine_send: int32 [49152], P(('groups', 'mesh', 'feat')), parts along dimension 0, may hold values from 0 to 1279, as said below
- fine_recv: int32 [49152], P(('groups', 'mesh', 'feat')), parts along dimension 0, may hold values from 0 to 1024, as said below
- halo_send: int32 [2048], P(('groups', 'mesh')), parts along dimension 0, may hold values from 0 to 1023, as said below
- coarse_edges: bfloat16 [3072, 512], P(('groups', 'mesh', 'feat')), parts along dimension 0, may hold values from -6 to 6
- coarse_send: int32 [3072], P(('groups', 'mesh', 'feat')), parts along dimension 0, may hold values from 0 to 511
- coarse_recv: int32 [3072], P(('groups', 'mesh', 'feat')), parts along dimension 0, may hold values from 0 to 511
- edge_w1: bfloat16 [2, 512, 1536], P(None, 'feat'), may hold values from -0.15625 to 0.15625
- edge_b1: bfloat16 [2, 512], P(None, 'feat'), may hold values from -3 to 3
- edge_w2: bfloat16 [2, 512, 512], P(None, 'feat'), may hold values from -0.25 to 0.25
- edge_gain: bfloat16 [2, 512], replicated, may hold values from 0.25 to 1.75
- node_w1: bfloat16 [2, 512, 1024], P(None, 'feat'), may hold values from -0.1875 to 0.1875
- node_b1: bfloat16 [2, 512], P(None, 'feat'), may hold values from -3 to 3
- node_w2: bfloat16 [2, 512, 512], P(None, 'feat'), may hold values from -0.25 to 0.25
- node_gain: bfloat16 [2, 512], replicated, may hold values from 0.25 to 1.75
Outputs:
- nodes_out: bfloat16 [8192, 512], P(('groups', 'mesh')), parts along dimension 0
The draws below stay inside these ranges and needn't reach their ends.
There are 2 independent parts, one for each index of `groups`. The reference program is written for one: setup_inputs(seed, part) draws one part's arguments, and reference() takes and returns one part's arrays. A program takes and returns all parts, laid end to end along the dimension named above; an argument that names none is the same for every part. Nothing has to cross between parts.
Inputs may be any that keep to these rules, and one draw needn't show every extreme that they name: `fine_send`: values index the extended table of the slot's partition: its 1024 nodes, then 128 rows from the previous and 128 from the next partition. `fine_recv`: the value 1024 marks an unused slot; each partition has from half to all of its 6144 slots in use, and some partition all. `halo_send`: each partition's 2 * 128 entries are distinct rows of that partition: first those for the previous partition, then those for the next.
All inputs are finite; a program needn't handle non-finite values.
Results may differ from the reference program's by a relative error of at most 0.0085.
Values may be sent and summed in bfloat16 or wider, within the bound.
No kernel may reach another device: no remote copies, remote signals or barrier semaphores. Data moves between devices by JAX's collectives and lax.ppermute only.
A program may use at most 64 MiB of HBM per device.

```python
import jax
import jax.numpy as jnp
from jax import lax

D = 512
H = 512
STEPS = 2
NODES_DEV = 1024
HALO = 128
EDGES_DEV = 6144
NODES = 4096
COARSE = 512
EDGES = 24576
CEDGES = 1536
N_MESH = 4


def edge_tables(key):
    part_count = EDGES // EDGES_DEV
    slot_count = NODES_DEV + 2 * HALO
    fullest = jax.random.randint(jax.random.fold_in(key, 7), (), 0, part_count)

    def one_part(part_index):
        part_key = jax.random.fold_in(jax.random.fold_in(key, 9), part_index)
        live_count = jax.random.randint(jax.random.fold_in(part_key, 1), (), EDGES_DEV // 2, EDGES_DEV)
        live_count = jnp.where(part_index == fullest, EDGES_DEV, live_count)
        placing = jax.random.permutation(jax.random.fold_in(part_key, 2), EDGES_DEV)
        rank_list = jnp.arange(EDGES_DEV, dtype=jnp.int32)
        extra_send = jax.random.randint(jax.random.fold_in(part_key, 3), (EDGES_DEV,), 0, slot_count)
        send_rank = jnp.where(rank_list < slot_count, rank_list, extra_send).astype(jnp.int32)
        recv_pick = jax.random.randint(jax.random.fold_in(part_key, 4), (EDGES_DEV,), 0, NODES_DEV)
        recv_rank = jnp.where(rank_list < live_count, recv_pick, NODES_DEV).astype(jnp.int32)
        senders = jnp.zeros((EDGES_DEV,), jnp.int32).at[placing].set(send_rank)
        receivers = jnp.zeros((EDGES_DEV,), jnp.int32).at[placing].set(recv_rank)
        return (senders, receivers)
    senders, receivers = jax.vmap(one_part)(jnp.arange(part_count))
    return (senders.reshape(EDGES), receivers.reshape(EDGES))


def draw_fine_send(key, part):
    return edge_tables(key)[0]


def draw_fine_recv(key, part):
    return edge_tables(key)[1]


def draw_halo_send(key, part):
    key = jax.random.fold_in(key, 5)
    part_count = NODES // NODES_DEV

    def one_part(part_index):
        chosen = jax.random.permutation(jax.random.fold_in(key, part_index), NODES_DEV)
        return chosen[:2 * HALO].astype(jnp.int32)
    return jax.vmap(one_part)(jnp.arange(part_count)).reshape(part_count * 2 * HALO)


def set_ends(drawn, own_key, smallest, largest):
    longest = drawn.shape.index(max(drawn.shape))
    spots = []
    for shift in (0, 1):
        where = [jax.random.randint(jax.random.fold_in(own_key, axis), (), 0, length) for axis, length in enumerate(drawn.shape)]
        where[longest] = (where[longest] + shift) % drawn.shape[longest]
        spots.append(tuple(where))
    return drawn.at[spots[0]].set(smallest).at[spots[1]].set(largest)


def level_of(rng, shape, cuts, smallest, top_value):
    def one(position, parts):
        heights = jax.random.uniform(jax.random.fold_in(jax.random.fold_in(rng, 6), position), (parts,), jnp.float32, smallest / len(cuts), top_value / len(cuts))
        return jnp.repeat(jnp.exp(heights), shape[position] // parts).reshape((-1,) + (1,) * (len(shape) - position - 1))

    level = one(*cuts[0])
    for cut in cuts[1:]:
        level = level * one(*cut)
    return level


def scatter_about(rng, shape, width, limit, pieces=(), kind=jnp.bfloat16):
    entries = width * jax.random.normal(rng, shape, jnp.float32)
    if pieces:
        entries = entries * level_of(rng, shape, pieces, -0.22, 0.18)
    return jnp.clip(entries, -limit, limit).astype(kind)


def setup_inputs(seed: int = 0, part: int = 0) -> dict:
    key_list = jax.random.split(jax.random.key(seed), 17)
    part_keys = jax.random.split(jax.random.fold_in(key_list[16], part), 17)
    nodes = scatter_about(part_keys[0], (NODES, D), 1.0, 6.0, ((0, 4),))
    fine_edges = scatter_about(part_keys[1], (EDGES, D), 1.0, 6.0, ((0, 16),))
    fine_send = draw_fine_send(jax.random.fold_in(jax.random.fold_in(key_list[16], part), 71), part)
    fine_recv = draw_fine_recv(jax.random.fold_in(jax.random.fold_in(key_list[16], part), 71), part)
    halo_send = draw_halo_send(jax.random.fold_in(jax.random.fold_in(key_list[16], part), 71), part)
    coarse_edges = scatter_about(part_keys[5], (CEDGES, D), 1.0, 6.0, ((0, 16),))
    coarse_send = set_ends(jax.random.randint(part_keys[6], (CEDGES,), 0, COARSE), jax.random.fold_in(part_keys[6], 1), 0, COARSE - 1).astype(jnp.int32)
    coarse_recv = set_ends(jax.random.randint(part_keys[7], (CEDGES,), 0, COARSE), jax.random.fold_in(part_keys[7], 1), 0, COARSE - 1).astype(jnp.int32)
    edge_w1 = scatter_about(key_list[8], (STEPS, H, 3 * D), (3 * D) ** -0.5, 0.15625, ((1, 4),))
    edge_b1 = scatter_about(key_list[9], (STEPS, H), 0.5, 3.0, ((1, 4),))
    edge_w2 = scatter_about(key_list[10], (STEPS, H, D), H ** -0.5, 0.25, ((1, 4),))
    edge_gain = jnp.clip(1.0 + 0.15 * jax.random.normal(key_list[11], (STEPS, D), jnp.float32), 0.25, 1.75).astype(jnp.bfloat16)
    node_w1 = scatter_about(key_list[12], (STEPS, H, 2 * D), (2 * D) ** -0.5, 0.1875, ((1, 4),))
    node_b1 = scatter_about(key_list[13], (STEPS, H), 0.5, 3.0, ((1, 4),))
    node_w2 = scatter_about(key_list[14], (STEPS, H, D), H ** -0.5, 0.25, ((1, 4),))
    node_gain = jnp.clip(1.0 + 0.15 * jax.random.normal(key_list[15], (STEPS, D), jnp.float32), 0.25, 1.75).astype(jnp.bfloat16)
    return dict(nodes=nodes, fine_edges=fine_edges, fine_send=fine_send, fine_recv=fine_recv, halo_send=halo_send, coarse_edges=coarse_edges, coarse_send=coarse_send, coarse_recv=coarse_recv, edge_w1=edge_w1, edge_b1=edge_b1, edge_w2=edge_w2, edge_gain=edge_gain, node_w1=node_w1, node_b1=node_b1, node_w2=node_w2, node_gain=node_gain)


def layer_norm(values, gain):
    row_mean = lax.optimization_barrier(jnp.mean(values, axis=-1, keepdims=True))
    centred = values - row_mean
    row_var = lax.optimization_barrier(jnp.mean(centred * centred, axis=-1, keepdims=True))
    return centred * lax.rsqrt(row_var + 1e-05) * gain.astype(jnp.float32)

def apply_mlp(inputs, w_in, hidden_bias, w_out, gain):
    pre_act = lax.dot_general(inputs, w_in, (((1,), (1,)), ((), ())), preferred_element_type=jnp.float32)
    activated = jax.nn.silu(pre_act + hidden_bias.astype(jnp.float32)).astype(jnp.bfloat16)
    return layer_norm(jnp.dot(activated, w_out, preferred_element_type=jnp.float32), gain)

def take_rows(source, indices):
    return jnp.take_along_axis(source, indices[:, :, None].astype(jnp.int32), axis=1)

def reference(nodes, fine_edges, fine_send, fine_recv, halo_send, coarse_edges, coarse_send, coarse_recv, edge_w1, edge_b1, edge_w2, edge_gain, node_w1, node_b1, node_w2, node_gain):
    blocks = halo_send.reshape(N_MESH, 2 * HALO)
    send_grid = fine_send.reshape(N_MESH, EDGES_DEV)
    recv_grid = fine_recv.reshape(N_MESH, EDGES_DEV)
    offsets = (jnp.arange(N_MESH, dtype=jnp.int32) * NODES_DEV)[:, None]
    segment_ids = jnp.where(recv_grid < NODES_DEV, recv_grid + offsets, NODES).reshape(EDGES).astype(jnp.int32)
    recv_safe = jnp.minimum(recv_grid, NODES_DEV - 1)
    for layer_index in range(STEPS):
        node_grid = nodes.reshape(N_MESH, NODES_DEV, D)
        from_prev = take_rows(jnp.roll(node_grid, 1, 0), jnp.roll(blocks, 1, 0)[:, HALO:])
        from_next = take_rows(jnp.roll(node_grid, -1, 0), jnp.roll(blocks, -1, 0)[:, :HALO])
        node_table = jnp.concatenate([node_grid, from_prev, from_next], axis=1)
        senders = take_rows(node_table, send_grid).reshape(EDGES, D)
        receivers = take_rows(node_grid, recv_safe).reshape(EDGES, D)
        coarse_nodes = nodes.reshape(COARSE, 8, D)[:, 0]
        fine_in = jnp.concatenate([fine_edges, senders, receivers], axis=1)
        coarse_in = jnp.concatenate([coarse_edges, coarse_nodes[coarse_send], coarse_nodes[coarse_recv]], axis=1)
        inputs = jnp.concatenate([fine_in, coarse_in], axis=0)
        update_term = apply_mlp(inputs, edge_w1[layer_index], edge_b1[layer_index], edge_w2[layer_index], edge_gain[layer_index])
        all_edges = jnp.concatenate([fine_edges, coarse_edges], axis=0)
        all_edges = (all_edges.astype(jnp.float32) + update_term).astype(jnp.bfloat16)
        fine_edges = all_edges[:EDGES]
        coarse_edges = all_edges[EDGES:]
        fine_sum = jax.ops.segment_sum(fine_edges.astype(jnp.float32), segment_ids, NODES)
        coarse_sum = jax.ops.segment_sum(coarse_edges.astype(jnp.float32), coarse_recv, COARSE)
        summed = fine_sum.reshape(COARSE, 8, D).at[:, 0].add(coarse_sum).reshape(NODES, D)
        node_in = jnp.concatenate([nodes, summed.astype(jnp.bfloat16)], axis=1)
        node_term = apply_mlp(node_in, node_w1[layer_index], node_b1[layer_index], node_w2[layer_index], node_gain[layer_index])
        nodes = (nodes.astype(jnp.float32) + node_term).astype(jnp.bfloat16)
    return nodes
```

```python
import functools

import jax
import jax.numpy as jnp
from jax import lax
from jax.experimental import pallas as pl
from jax.experimental.pallas import tpu as pltpu
from jax.sharding import PartitionSpec as P

STEPS = 2
STRIDE = 8
LANES = 128
DIGIT = 64
VMEM_BYTES = 32 * 1024 * 1024


def dot(a, b):
    return jnp.dot(a, b, preferred_element_type=jnp.float32)


def dot_t(a, b):
    return lax.dot_general(a, b, (((1,), (1,)), ((), ())), preferred_element_type=jnp.float32)


def pick_rows(index, count):
    spots = lax.broadcasted_iota(jnp.int32, (index.shape[0], count), 1)
    return (spots == index).astype(jnp.bfloat16)


def silu(x):
    return x * (0.5 * jnp.tanh(0.5 * x) + 0.5)


def layer_norm(values, gain):
    centred = values - jnp.mean(values, axis=-1, keepdims=True)
    row_var = jnp.mean(centred * centred, axis=-1, keepdims=True)
    return centred * lax.rsqrt(row_var + 1e-05) * gain


def mlp(x, groups, biases, gain, k):
    width = gain.shape[-1]
    total = None
    for packs, bias in zip(groups, biases):
        w_in = jnp.concatenate([p[:, :k] for p in packs], axis=0)
        w_out = jnp.concatenate([p[:, k : k + width] for p in packs], axis=0)
        act = silu(dot_t(x, w_in) + bias).astype(jnp.bfloat16)
        part = dot(act, w_out)
        total = part if total is None else total + part
    return layer_norm(total, gain)


def call(kernel, out_shape, args, scratch=(), flops=0, nbytes=0, name=None):
    vmem = pl.BlockSpec(memory_space=pltpu.VMEM)
    out_specs = jax.tree.map(lambda _: vmem, out_shape)
    return pl.pallas_call(
        kernel,
        out_shape=out_shape,
        in_specs=[vmem] * len(args),
        out_specs=out_specs,
        scratch_shapes=list(scratch),
        compiler_params=pltpu.CompilerParams(vmem_limit_bytes=VMEM_BYTES),
        cost_estimate=pl.CostEstimate(flops=flops, bytes_accessed=nbytes, transcendentals=0),
        name=name,
    )(*args)


def bf16(*shape):
    return jax.ShapeDtypeStruct(shape, jnp.bfloat16)


def core_index():
    return lax.rem(lax.axis_index("feat"), 2)


def pack_kernel(nodes, halo, to_prev, to_next, coarse_half, coarse):
    core = core_index()
    count, hr, cp = nodes.shape[0], halo.shape[0] // 2, coarse.shape[0]
    hh, ch = hr // 2, cp // 2
    prev = halo[pl.ds(pl.multiple_of(core * hh, hh), hh), :]
    nxt = halo[pl.ds(pl.multiple_of(hr + core * hh, hh), hh), :]
    table = nodes[...]
    rows = dot(pick_rows(jnp.concatenate([prev, nxt], axis=0), count), table).astype(jnp.bfloat16)
    every = STRIDE * lax.broadcasted_iota(jnp.int32, (cp, 1), 0)
    coarse[...] = dot(pick_rows(every, count), table).astype(jnp.bfloat16)
    mine = coarse[pl.ds(pl.multiple_of(core * ch, ch), ch), :]
    to_prev[pl.ds(0, hh), :] = rows[:hh]
    to_prev[pl.ds(hh, ch), :] = mine
    to_next[pl.ds(0, hh), :] = rows[hh:]
    to_next[pl.ds(hh, ch), :] = mine
    coarse_half[...] = mine


def gather_kernel(tile, nodes, send, recv, sent, received):
    count = nodes.shape[0]

    def body(t, carry):
        rows = pl.ds(pl.multiple_of(t * tile, tile), tile)
        table = nodes[...]
        sent[rows, :] = dot(pick_rows(send[rows, :], count), table).astype(jnp.bfloat16)
        safe = jnp.minimum(recv[rows, :], count - 1)
        received[rows, :] = dot(pick_rows(safe, count), table).astype(jnp.bfloat16)
        return carry

    lax.fori_loop(0, send.shape[0] // tile, body, 0)


def edge_kernel(tile, ctile, sizes, first, *refs):
    count, hr, cp, parts, cores = sizes
    it = iter(refs)
    fine, sent, received, send, recv_row, coarse_own, coarse_edges, coarse_index, gain_ref = (
        next(it) for _ in range(9)
    )
    arrived = [(next(it), next(it)) for _ in range(parts - 1)]
    groups = [[next(it) for _ in range(2)] for _ in range(cores // 2)]
    bias_in = None if first else next(it)
    new_fine, new_coarse, agg_own, agg_other = (next(it) for _ in range(4))
    bias_out = next(it) if first else None
    halo_tab, coarse_tab, latents = (next(it) for _ in range(3))

    core, me = core_index(), lax.axis_index("mesh")
    width = gain_ref.shape[-1]
    k = 3 * width
    hh, ch, nh = hr // 2, cp // 2, count // 2
    fine_count, coarse_count = fine.shape[0], coarse_edges.shape[0]

    coarse_tab[pl.ds(pl.multiple_of(me * cp, cp), cp), :] = coarse_own[...]
    for i, pair in enumerate(arrived):
        owner = lax.rem(me + parts - 1 - i, parts)
        side = {0: 0, parts - 2: hr}.get(i)
        for who, ref in zip((core, 1 - core), pair):
            skip = 0
            if side is not None:
                halo_tab[pl.ds(pl.multiple_of(side + who * hh, hh), hh), :] = ref[pl.ds(0, hh), :]
                skip = hh
            spot = pl.multiple_of(owner * cp + who * ch, ch)
            coarse_tab[pl.ds(spot, ch), :] = ref[pl.ds(skip, ch), :]

    layer = 0 if first else 1
    lane = lax.broadcasted_iota(jnp.int32, (8, LANES), 1)
    row = lax.broadcasted_iota(jnp.int32, (8, LANES), 0)
    if first:
        unit = (lane == row).astype(jnp.bfloat16)
        for g, packs in enumerate(groups):
            for j, p in enumerate(packs):
                hidden = p.shape[0]
                spot = (2 * g + j) * hidden
                bias_out[:, spot : spot + hidden] = dot_t(unit, p[:, k + width :])
        bias_ref = bias_out
    else:
        bias_ref = bias_in
    per = bias_ref.shape[1] // len(groups)
    biases = [bias_ref[layer : layer + 1, g * per : (g + 1) * per] for g in range(len(groups))]
    gain = gain_ref[layer : layer + 1, :].astype(jnp.float32)

    def update(x, old):
        return (old.astype(jnp.float32) + mlp(x, groups, biases, gain, k)).astype(jnp.bfloat16)

    def fine_body(t, carry):
        rows = pl.ds(pl.multiple_of(t * tile, tile), tile)
        border = dot(pick_rows(send[rows, :] - count, 2 * hr), halo_tab[...])
        senders = (sent[rows, :].astype(jnp.float32) + border).astype(jnp.bfloat16)
        old = fine[rows, :]
        new = update(jnp.concatenate([old, senders, received[rows, :]], axis=1), old)
        latents[rows, :] = new
        new_fine[rows, :] = new
        return carry

    lax.fori_loop(0, fine_count // tile, fine_body, 0)

    def digits(at):
        c = coarse_index[at, :].astype(jnp.float32)
        return [(DIGIT * c[:, 2 * j : 2 * j + 1] + c[:, 2 * j + 1 : 2 * j + 2]).astype(jnp.int32) for j in range(2)]

    def coarse_body(t, carry):
        rows = pl.ds(pl.multiple_of(t * ctile, ctile), ctile)
        old = coarse_edges[rows, :]
        ends = [
            dot(pick_rows(d, coarse_tab.shape[0]), coarse_tab[...]).astype(jnp.bfloat16)
            for d in digits(rows)
        ]
        new = update(jnp.concatenate([old] + ends, axis=1), old)
        latents[pl.ds(pl.multiple_of(fine_count + t * ctile, ctile), ctile), :] = new
        new_coarse[rows, :] = new
        return carry

    lax.fori_loop(0, coarse_count // ctile, coarse_body, 0)

    weights = jnp.where(lane == 2, float(DIGIT), jnp.where(lane == 3, 1.0, 0.0)).astype(jnp.bfloat16)
    near = dot_t(weights, coarse_index[...])[:1, :].astype(jnp.int32) - me * cp
    target = jnp.where((near >= 0) & (near < cp), near * STRIDE, -1)
    targets = jnp.concatenate([recv_row[...], target], axis=1)
    block = min(256, nh)

    def aggregate(base, spot):
        spots = lax.broadcasted_iota(jnp.int32, (block, targets.shape[1]), 0) + (base + spot)
        return dot((spots == targets).astype(jnp.bfloat16), latents[...])

    for spot in range(0, nh, block):
        agg_other[pl.ds(spot, block), :] = aggregate((1 - core) * nh, spot).astype(jnp.bfloat16)
    for spot in range(0, nh, block):
        agg_own[pl.ds(spot, block), :] = aggregate(core * nh, spot)


def node_kernel(tile, layer, cores, n_sums, *refs):
    it = iter(refs)
    nodes, bias_ref, gain_ref = (next(it) for _ in range(3))
    sums = [next(it) for _ in range(n_sums)]
    groups = [[next(it) for _ in range(2)] for _ in range(cores // 2)]
    out = next(it)
    width = gain_ref.shape[-1]
    nh = out.shape[0]
    per = bias_ref.shape[1] // len(groups)
    line = STEPS + layer
    biases = [bias_ref[line : line + 1, g * per : (g + 1) * per] for g in range(len(groups))]
    gain = gain_ref[layer : layer + 1, :].astype(jnp.float32)
    core = core_index()
    for t in range(nh // tile):
        rows = pl.ds(t * tile, tile)
        old = nodes[pl.ds(pl.multiple_of(core * nh + t * tile, tile), tile), :]
        agg = sums[0][rows, :].astype(jnp.float32)
        for more in sums[1:]:
            agg = agg + more[rows, :].astype(jnp.float32)
        x = jnp.concatenate([old, agg.astype(jnp.bfloat16)], axis=1)
        y = mlp(x, groups, biases, gain, 2 * width)
        out[rows, :] = (old.astype(jnp.float32) + y).astype(jnp.bfloat16)


def divisor(count, most, unit=16):
    best = unit
    for size in range(unit, min(most, count) + 1, unit):
        if count % size == 0:
            best = size
    return best


def local(
    nodes,
    fine_edges,
    fine_send,
    fine_recv,
    halo_send,
    coarse_edges,
    coarse_send,
    coarse_recv,
    edge_w1,
    edge_b1,
    edge_w2,
    edge_gain,
    node_w1,
    node_b1,
    node_w2,
    node_gain,
):
    count, width = nodes.shape
    hr = halo_send.shape[0] // 2
    cp = count // STRIDE
    nh = count // 2
    fine_count = fine_edges.shape[0]
    parts = lax.axis_size("mesh")
    cores = lax.axis_size("feat")
    core = core_index()

    def swap(x):
        return lax.ppermute(x, "feat", [(i, i ^ 1) for i in range(cores)])

    def across(x):
        return lax.ppermute(x, "feat", [(i, i ^ 2) for i in range(cores)])

    def shift(x, by):
        return lax.ppermute(x, "mesh", [(i, (i + by) % parts) for i in range(parts)])

    def spread(pack):
        if cores != 4:
            every = lax.all_gather(pack, "feat", axis=0)
            return [every[i] for i in range(cores)]
        far = across(pack)
        return [pack, swap(pack), far, swap(far)]

    bias = jnp.concatenate([edge_b1, node_b1], axis=0).T
    bias = jnp.pad(bias, ((0, 0), (0, LANES - bias.shape[1])))
    edge_packs = [
        spread(jnp.concatenate([edge_w1[s], edge_w2[s]] + ([bias] if s == 0 else []), axis=1))
        for s in range(STEPS)
    ]
    node_packs = [
        spread(jnp.concatenate([node_w1[s], node_w2[s]], axis=1)) for s in range(STEPS)
    ]

    digits = [coarse_send // DIGIT, coarse_send % DIGIT, coarse_recv // DIGIT, coarse_recv % DIGIT]
    digits = jnp.stack(digits, axis=1).astype(jnp.bfloat16)
    digits = jnp.pad(digits, ((0, 0), (0, LANES - digits.shape[1])))
    coarse_pack = jnp.concatenate([coarse_edges, digits], axis=1)
    coarse_all = jnp.concatenate(
        [coarse_pack] + [shift(coarse_pack, by) for by in range(1, parts)], axis=0
    )
    coarse_state = coarse_all[:, :width]
    coarse_index = coarse_all[:, width:]
    coarse_count = coarse_all.shape[0]

    send_col = fine_send.reshape(fine_count, 1)
    recv_col = fine_recv.reshape(fine_count, 1)
    recv_row = fine_recv.reshape(1, fine_count)
    halo_col = halo_send.reshape(2 * hr, 1)
    tile = divisor(fine_count, 256)
    ctile = divisor(coarse_count, 256)
    hidden = edge_w1.shape[1] * cores
    sizes = (count, hr, cp, parts, cores)
    bias_rows = None

    for s in range(STEPS):
        half = hr // 2 + cp // 2
        to_prev, to_next, coarse_half, coarse_own = call(
            pack_kernel,
            (bf16(half, width), bf16(half, width), bf16(cp // 2, width), bf16(cp, width)),
            [nodes, halo_col],
            flops=2 * (hr + cp) * count * width,
            name="halo_rows",
        )
        arrived = []
        for by in range(1, parts):
            moved = shift({1: to_next, parts - 1: to_prev}.get(by, coarse_half), by)
            arrived += [moved, swap(moved)]
        sent, received = call(
            functools.partial(gather_kernel, tile),
            (bf16(fine_count, width), bf16(fine_count, width)),
            [nodes, send_col, recv_col],
            flops=4 * fine_count * count * width,
            name="gather_rows",
        )
        first = s == 0
        outs = [
            bf16(fine_count, width),
            bf16(coarse_count, width),
            jax.ShapeDtypeStruct((nh, width), jnp.float32),
            bf16(nh, width),
        ]
        if first:
            outs.append(jax.ShapeDtypeStruct((8, hidden), jnp.float32))
        rows = fine_count + coarse_count
        result = call(
            functools.partial(edge_kernel, tile, ctile, sizes, first),
            tuple(outs),
            [fine_edges, sent, received, send_col, recv_row, coarse_own, coarse_state, coarse_index, edge_gain]
            + arrived
            + edge_packs[s]
            + ([] if first else [bias_rows]),
            scratch=[
                pltpu.VMEM((2 * hr, width), jnp.bfloat16),
                pltpu.VMEM((parts * cp, width), jnp.bfloat16),
                pltpu.VMEM((rows, width), jnp.bfloat16),
            ],
            flops=2 * rows * width * (4 * hidden + count),
            name="edge_update",
        )
        fine_edges, coarse_state, agg_own, agg_other = result[:4]
        if first:
            bias_rows = result[4]
        partial = agg_own + swap(agg_other).astype(jnp.float32)
        if cores == 4:
            partial = partial.astype(jnp.bfloat16)
            sums = [partial, across(partial)]
        else:
            every = lax.all_gather(partial.astype(jnp.bfloat16), "feat", axis=0)
            every = every.reshape(cores // 2, 2, nh, width).astype(jnp.float32)
            sums = [lax.dynamic_index_in_dim(every.sum(axis=0), core, 0, keepdims=False)]
        new_half = call(
            functools.partial(node_kernel, divisor(nh, 256), s, cores, len(sums)),
            bf16(nh, width),
            [nodes, bias_rows, node_gain] + sums + node_packs[s],
            flops=2 * nh * width * 3 * hidden,
            name="node_update",
        )
        other_half = swap(new_half)
        nodes = jnp.where(
            core == 0,
            jnp.concatenate([new_half, other_half], axis=0),
            jnp.concatenate([other_half, new_half], axis=0),
        )
    return nodes


def solution(mesh):
    placed = (
        P(("groups", "mesh"), None),
        P(("groups", "mesh", "feat"), None),
        P(("groups", "mesh", "feat")),
        P(("groups", "mesh", "feat")),
        P(("groups", "mesh")),
        P(("groups", "mesh", "feat"), None),
        P(("groups", "mesh", "feat")),
        P(("groups", "mesh", "feat")),
        P(None, "feat", None),
        P(None, "feat"),
        P(None, "feat", None),
        P(),
        P(None, "feat", None),
        P(None, "feat"),
        P(None, "feat", None),
        P(),
    )
    return jax.shard_map(
        local, mesh=mesh, in_specs=placed, out_specs=P(("groups", "mesh"), None), check_vma=False
    )
```

```python
import functools

import jax
import jax.numpy as jnp
from jax import lax
from jax.experimental import pallas as pl
from jax.experimental.pallas import tpu as pltpu
from jax.sharding import PartitionSpec as P

STEPS = 2
STRIDE = 8
LANES = 128
PART = 768
DIGIT = 64
VMEM_BYTES = 20 * 1024 * 1024


def dot(a, b):
    return jnp.dot(a, b, preferred_element_type=jnp.float32)


def dot_t(a, b):
    return lax.dot_general(a, b, (((1,), (1,)), ((), ())), preferred_element_type=jnp.float32)


def pick_rows(index, count):
    spots = lax.broadcasted_iota(jnp.int32, (index.shape[0], count), 1)
    return (spots == index).astype(jnp.bfloat16)


def silu(x):
    return x * (0.5 * jnp.tanh(0.5 * x) + 0.5)


def layer_norm(values, gain):
    centred = values - jnp.mean(values, axis=-1, keepdims=True)
    row_var = jnp.mean(centred * centred, axis=-1, keepdims=True)
    return centred * lax.rsqrt(row_var + 1e-05) * gain


def along_lanes(pieces):
    return jnp.concatenate([pack[:, at:to] for pack, at, to in pieces], axis=1)


def mlp(x, groups, biases, gain):
    total = None
    for shards, bias in zip(groups, biases):
        w_in = jnp.concatenate([along_lanes(pieces) for pieces, _ in shards])
        w_out = jnp.concatenate([along_lanes(pieces) for _, pieces in shards])
        act = silu(dot_t(x, w_in) + bias).astype(jnp.bfloat16)
        part = dot(act, w_out)
        total = part if total is None else total + part
    return layer_norm(total, gain)


def take_groups(it, spots, cores):
    n_packs = 1 + max(pack for pieces in spots for pack, _, _ in pieces)
    groups = []
    for _ in range(cores // 2):
        shards = []
        for _ in range(2):
            refs = [next(it) for _ in range(n_packs)]
            shards.append([[(refs[pack], at, to) for pack, at, to in pieces] for pieces in spots])
        groups.append(shards)
    return groups


def loop(steps, body):
    lax.fori_loop(0, steps, body, 0, unroll=2 if steps % 2 == 0 else 1)


def call(kernel, out_shape, args, scratch=(), flops=0, nbytes=0, memory=None, limit=VMEM_BYTES, name=None):
    in_specs = [pl.BlockSpec(memory_space=m) for m in memory or [pltpu.VMEM] * len(args)]
    out_specs = jax.tree.map(lambda _: pl.BlockSpec(memory_space=pltpu.VMEM), out_shape)
    return pl.pallas_call(
        kernel,
        out_shape=out_shape,
        in_specs=in_specs,
        out_specs=out_specs,
        scratch_shapes=list(scratch),
        compiler_params=pltpu.CompilerParams(vmem_limit_bytes=limit),
        cost_estimate=pl.CostEstimate(flops=flops, bytes_accessed=nbytes, transcendentals=0),
        name=name,
    )(*args)


def bf16(*shape):
    return jax.ShapeDtypeStruct(shape, jnp.bfloat16)


def core_index():
    return lax.rem(lax.axis_index("feat"), 2)


def join_halves(out, own, other):
    core, nh = core_index(), own.shape[0]
    out[pl.ds(pl.multiple_of(core * nh, nh), nh), :] = own[...]
    out[pl.ds(pl.multiple_of((1 - core) * nh, nh), nh), :] = other[...]


def join_kernel(own, other, out):
    join_halves(out, own, other)


def add_kernel(own, arrived, out):
    out[...] = (own[...] + arrived[...].astype(jnp.float32)).astype(out.dtype)


def halo_kernel(first, *refs):
    if first:
        nodes, halo, to_prev, to_next, to_far, coarse = refs
    else:
        own, other, halo, to_prev, to_next, to_far, coarse, nodes = refs
        join_halves(nodes, own, other)
    core = core_index()
    count = nodes.shape[0]
    hr, cp = halo.shape[0] // 2, coarse.shape[0]
    hh, ch = hr // 2, cp // 2
    prev = halo[pl.ds(pl.multiple_of(core * hh, hh), hh), :]
    nxt = halo[pl.ds(pl.multiple_of(hr + core * hh, hh), hh), :]
    table = nodes[...]
    rows = dot(pick_rows(jnp.concatenate([prev, nxt], axis=0), count), table).astype(jnp.bfloat16)
    every = STRIDE * lax.broadcasted_iota(jnp.int32, (cp, 1), 0)
    coarse[...] = dot(pick_rows(every, count), table).astype(jnp.bfloat16)
    mine = coarse[pl.ds(pl.multiple_of(core * ch, ch), ch), :]
    to_prev[pl.ds(0, hh), :] = rows[:hh]
    to_prev[pl.ds(hh, ch), :] = mine
    to_next[pl.ds(0, hh), :] = rows[hh:]
    to_next[pl.ds(hh, ch), :] = mine
    to_far[...] = mine


def gather_kernel(tile, nodes, send, recv, sent, received):
    count = nodes.shape[0]

    def body(t, carry):
        rows = pl.ds(pl.multiple_of(t * tile, tile), tile)
        table = nodes[...]
        sent[rows, :] = dot(pick_rows(send[rows, :], count), table).astype(jnp.bfloat16)
        safe = jnp.minimum(recv[rows, :], count - 1)
        received[rows, :] = dot(pick_rows(safe, count), table).astype(jnp.bfloat16)
        return carry

    loop(send.shape[0] // tile, body)


def bias_rows_of(bias_ref, line, n_groups):
    per = bias_ref.shape[1] // n_groups
    return [bias_ref[line : line + 1, g * per : (g + 1) * per] for g in range(n_groups)]


def weight_kernel(plans, n_in, *refs):
    source, outs, sems = refs[:n_in], refs[n_in:-1], refs[-1]
    copies = []
    for plan, out in zip(plans, outs):
        at = 0
        for which, layer, first, last in plan:
            part = source[which].at[layer, :, first:last]
            spot = out.at[:, at : at + last - first]
            copies.append(pltpu.make_async_copy(part, spot, sems.at[len(copies)]))
            at += last - first
    for copy in copies:
        copy.start()
    for copy in copies:
        copy.wait()


def first_kernel(edge_w1, edge_w2, edge_b1, node_b1, out, sems):
    k, width, hidden = edge_w1.shape[2], edge_w2.shape[2], edge_b1.shape[1]
    copies = [
        pltpu.make_async_copy(edge_w1.at[0], out.at[:, 0:k], sems.at[0]),
        pltpu.make_async_copy(edge_w2.at[0], out.at[:, k : k + width], sems.at[1]),
    ]
    for copy in copies:
        copy.start()
    rows = [edge_b1[...].astype(jnp.float32), node_b1[...].astype(jnp.float32)]
    rows.append(jnp.zeros((16 - 2 * STEPS, hidden), jnp.float32))
    out[0:16, k + width : k + width + hidden] = jnp.concatenate(rows).astype(jnp.bfloat16)
    for copy in copies:
        copy.wait()


def coarse_pack_kernel(edges, send, recv, pack):
    width = edges.shape[1]
    pack[:, :width] = edges[...]
    lane = lax.broadcasted_iota(jnp.int32, (edges.shape[0], LANES), 1)
    digits = jnp.zeros(lane.shape, jnp.int32)
    for j, ref in enumerate((send, recv)):
        index = ref[...]
        high = lax.shift_right_logical(index, DIGIT.bit_length() - 1)
        low = index & (DIGIT - 1)
        digits = jnp.where(lane == 2 * j, high, jnp.where(lane == 2 * j + 1, low, digits))
    pack[:, width:] = digits.astype(jnp.float32).astype(jnp.bfloat16)


def fine_kernel(tile, sizes, spots, layer, *refs):
    count, hr, cp, parts, cores = sizes
    it = iter(refs)
    fine, sent, received, send, gain_ref = (next(it) for _ in range(5))
    prev, nxt = ((next(it), next(it)) for _ in range(2))
    groups = take_groups(it, spots, cores)
    bias_in = None if layer == 0 else next(it)
    new_fine = next(it)
    bias_out = next(it) if layer == 0 else None
    halo_tab = next(it)

    core = core_index()
    width = gain_ref.shape[-1]
    hh = hr // 2
    for side, pair in ((0, prev), (hr, nxt)):
        for who, ref in zip((core, 1 - core), pair):
            halo_tab[pl.ds(pl.multiple_of(side + who * hh, hh), hh), :] = ref[pl.ds(0, hh), :]

    if layer == 0:
        spot = 0
        for shards in groups:
            for _, [(pack, _, at)] in shards:
                hidden = pack.shape[0]
                rows = pack[0:16, at : at + hidden].astype(jnp.float32)
                bias_out[:, spot : spot + hidden] = rows[:8]
                spot += hidden
    biases = bias_rows_of(bias_out if layer == 0 else bias_in, layer, len(groups))
    gain = gain_ref[layer : layer + 1, :].astype(jnp.float32)

    def body(t, carry):
        rows = pl.ds(pl.multiple_of(t * tile, tile), tile)
        border = dot(pick_rows(send[rows, :] - count, 2 * hr), halo_tab[...])
        senders = (sent[rows, :].astype(jnp.float32) + border).astype(jnp.bfloat16)
        old = fine[rows, :]
        x = jnp.concatenate([old, senders, received[rows, :]], axis=1)
        y = mlp(x, groups, biases, gain)
        new_fine[rows, :] = (old.astype(jnp.float32) + y).astype(jnp.bfloat16)
        return carry

    loop(fine.shape[0] // tile, body)


def coarse_target(state, width, me, cp):
    lane = lax.broadcasted_iota(jnp.int32, (8, LANES), 1)
    weights = jnp.where(lane == 2, float(DIGIT), jnp.where(lane == 3, 1.0, 0.0)).astype(jnp.bfloat16)
    near = dot_t(weights, state[:, width : width + LANES])[:1, :].astype(jnp.int32) - me * cp
    return jnp.where((near >= 0) & (near < cp), near * STRIDE, -1)


def row_sums(base, out, new_fine, recv_row, state, target):
    width = out.shape[1]
    block = min(256, out.shape[0])
    for spot in range(0, out.shape[0], block):
        total = None
        for places, latents in ((recv_row[...], new_fine[...]), (target, state[:, :width])):
            rows = lax.broadcasted_iota(jnp.int32, (block, places.shape[1]), 0) + (base + spot)
            part = dot((rows == places).astype(jnp.bfloat16), latents)
            total = part if total is None else total + part
        out[pl.ds(spot, block), :] = total.astype(out.dtype)


def coarse_kernel(tile, sizes, spots, layer, *refs):
    count, hr, cp, parts, cores = sizes
    it = iter(refs)
    new_fine, recv_row, coarse_own, gain_ref, bias_ref = (next(it) for _ in range(5))
    states = [next(it) for _ in range(parts if layer == 0 else 1)]
    arrived = [(next(it), next(it)) for _ in range(parts - 1)]
    groups = take_groups(it, spots, cores)
    state, agg_other, coarse_tab = (next(it) for _ in range(3))

    core, me = core_index(), lax.axis_index("mesh")
    width = gain_ref.shape[-1]
    hh, ch, nh = hr // 2, cp // 2, count // 2

    coarse_tab[pl.ds(pl.multiple_of(me * cp, cp), cp), :] = coarse_own[...]
    for i, pair in enumerate(arrived):
        owner = lax.rem(me + parts - 1 - i, parts)
        skip = hh if i in (0, parts - 2) else 0
        for who, ref in zip((core, 1 - core), pair):
            spot = pl.multiple_of(owner * cp + who * ch, ch)
            coarse_tab[pl.ds(spot, ch), :] = ref[pl.ds(skip, ch), 0:width]
    at = 0
    for one in states:
        state[pl.ds(at, one.shape[0]), :] = one[...]
        at += one.shape[0]

    biases = bias_rows_of(bias_ref, layer, len(groups))
    gain = gain_ref[layer : layer + 1, :].astype(jnp.float32)

    def body(t, carry):
        rows = pl.ds(pl.multiple_of(t * tile, tile), tile)
        old = state[rows, :width]
        digits = state[rows, width : width + LANES].astype(jnp.float32)
        ends = []
        for j in range(2):
            index = DIGIT * digits[:, 2 * j : 2 * j + 1] + digits[:, 2 * j + 1 : 2 * j + 2]
            picked = pick_rows(index.astype(jnp.int32), coarse_tab.shape[0])
            ends.append(dot(picked, coarse_tab[...]).astype(jnp.bfloat16))
        y = mlp(jnp.concatenate([old] + ends, axis=1), groups, biases, gain)
        state[rows, :width] = (old.astype(jnp.float32) + y).astype(jnp.bfloat16)
        return carry

    loop(state.shape[0] // tile, body)
    target = coarse_target(state, width, me, cp)
    row_sums((1 - core) * nh, agg_other, new_fine, recv_row, state, target)


def own_kernel(cp, new_fine, recv_row, state, agg_own):
    core, me = core_index(), lax.axis_index("mesh")
    nh, width = agg_own.shape
    target = coarse_target(state, width, me, cp)
    row_sums(core * nh, agg_own, new_fine, recv_row, state, target)


def node_kernel(tile, layer, cores, spots, n_sums, *refs):
    it = iter(refs)
    nodes, bias_ref, gain_ref = (next(it) for _ in range(3))
    sums = [next(it) for _ in range(n_sums)]
    groups = take_groups(it, spots, cores)
    out = next(it)
    nh = out.shape[0]
    biases = bias_rows_of(bias_ref, STEPS + layer, len(groups))
    gain = gain_ref[layer : layer + 1, :].astype(jnp.float32)
    core = core_index()
    for t in range(nh // tile):
        rows = pl.ds(t * tile, tile)
        old = nodes[pl.ds(pl.multiple_of(core * nh + t * tile, tile), tile), :]
        agg = sums[0][rows, :].astype(jnp.float32)
        for more in sums[1:]:
            agg = agg + more[rows, :].astype(jnp.float32)
        x = jnp.concatenate([old, agg.astype(jnp.bfloat16)], axis=1)
        y = mlp(x, groups, biases, gain)
        out[rows, :] = (old.astype(jnp.float32) + y).astype(jnp.bfloat16)


def divisor(count, most, unit=16):
    best = unit
    for size in range(unit, min(most, count) + 1, unit):
        if count % size == 0:
            best = size
    return best


def local(
    nodes,
    fine_edges,
    fine_send,
    fine_recv,
    halo_send,
    coarse_edges,
    coarse_send,
    coarse_recv,
    edge_w1,
    edge_b1,
    edge_w2,
    edge_gain,
    node_w1,
    node_b1,
    node_w2,
    node_gain,
):
    count, width = nodes.shape
    hr = halo_send.shape[0] // 2
    cp = count // STRIDE
    nh = count // 2
    fine_count = fine_edges.shape[0]
    parts = lax.axis_size("mesh")
    cores = lax.axis_size("feat")
    core = core_index()

    def swap(x):
        return lax.ppermute(x, "feat", [(i, i ^ 1) for i in range(cores)])

    def across(x):
        return lax.ppermute(x, "feat", [(i, i ^ 2) for i in range(cores)])

    def shift(x, by):
        return lax.ppermute(x, "mesh", [(i, (i + by) % parts) for i in range(parts)])

    def both(x):
        return [x, swap(x)]

    def after(x, *earlier):
        return lax.optimization_barrier((x, earlier))[0]

    two = cores == 4

    def spread(pack, *earlier):
        if two:
            return across(after(pack, *earlier) if earlier else pack)
        return lax.all_gather(pack, "feat", axis=0)

    def shards(pack, far):
        if two:
            return both(pack) + both(far)
        return [far[i] for i in range(cores)]

    k, kn = edge_w1.shape[2], node_w1.shape[2]
    w_hidden = edge_w1.shape[1]
    first_pack = call(
        first_kernel,
        bf16(w_hidden, k + width + LANES),
        [edge_w1, edge_w2, edge_b1, node_b1],
        scratch=[pltpu.SemaphoreType.DMA((2,))],
        memory=[pl.ANY, pl.ANY, pltpu.VMEM, pltpu.VMEM],
        limit=3 * VMEM_BYTES,
        name="first_weights",
    )
    stream = ((2, 0, kn), (3, 0, width), (1, 1, width), (0, 1, k), (2, 1, kn), (3, 1, width))
    starts = [0]
    for _, _, lanes in stream:
        starts.append(starts[-1] + lanes)
    cuts = [0, starts[2], starts[3], starts[4] + PART, starts[-1]]

    def pieces(which):
        first, last = starts[which], starts[which + 1]
        found = []
        for pack, (lo, hi) in enumerate(zip(cuts, cuts[1:])):
            if max(lo, first) < min(hi, last):
                found.append((pack, max(lo, first) - lo, min(hi, last) - lo))
        return found

    plans = [[] for _ in cuts[1:]]
    for which, (source, layer, _) in enumerate(stream):
        done = 0
        for pack, at, to in pieces(which):
            plans[pack].append((source, layer, done, done + to - at))
            done += to - at
    packs = call(
        functools.partial(weight_kernel, plans, 4),
        tuple(bf16(w_hidden, hi - lo) for lo, hi in zip(cuts, cuts[1:])),
        [edge_w1, edge_w2, node_w1, node_w2],
        scratch=[pltpu.SemaphoreType.DMA((sum(len(p) for p in plans),))],
        memory=[pl.ANY] * 4,
        limit=3 * VMEM_BYTES,
        name="later_weights",
    )

    def choose(shards_of, w_in, w_out):
        used = sorted({pack for which in (w_in, w_out) for pack, _, _ in pieces(which)})
        spots = [[(used.index(p), at, to) for p, at, to in pieces(w)] for w in (w_in, w_out)]
        return [x for shard in zip(*(shards_of[p] for p in used)) for x in shard], spots

    own_coarse = coarse_edges.shape[0]
    coarse_pack = call(
        coarse_pack_kernel,
        bf16(own_coarse, width + LANES),
        [coarse_edges, coarse_send.reshape(own_coarse, 1), coarse_recv.reshape(own_coarse, 1)],
        name="coarse_pack",
    )
    coarse_count = own_coarse * parts

    send_col = fine_send.reshape(fine_count, 1)
    recv_col = fine_recv.reshape(fine_count, 1)
    recv_row = fine_recv.reshape(1, fine_count)
    halo_col = halo_send.reshape(2 * hr, 1)
    tile = divisor(fine_count, 768)
    ctile = divisor(coarse_count, 384)
    hidden = w_hidden * cores
    sizes = (count, hr, cp, parts, cores)
    bias_rows = None

    def node_rows_out(*given):
        half = hr // 2 + cp // 2
        first = len(given) == 1
        outs = [bf16(half, width), bf16(half, width), bf16(cp // 2, width), bf16(cp, width)]
        return call(
            functools.partial(halo_kernel, first),
            tuple(outs if first else outs + [bf16(count, width)]),
            [*given, halo_col],
            name="halo_rows",
        )

    def exchange(to_prev, to_next, coarse_half):
        return [
            shift({1: to_next, parts - 1: to_prev}.get(by, coarse_half), by)
            for by in range(1, parts)
        ]

    def gather(nodes):
        return call(
            functools.partial(gather_kernel, tile),
            (bf16(fine_count, width), bf16(fine_count, width)),
            [nodes, send_col, recv_col],
            flops=4 * fine_count * count * width,
            name="gather_rows",
        )

    def fine_update(s, fine, sent, received, halo, weights, spots):
        outs = [bf16(fine_count, width)]
        if s == 0:
            outs.append(jax.ShapeDtypeStruct((8, hidden), jnp.float32))
        return call(
            functools.partial(fine_kernel, tile, sizes, spots, s),
            tuple(outs),
            [fine, sent, received, send_col, edge_gain] + halo + weights + ([bias_rows] if s else []),
            scratch=[pltpu.VMEM((2 * hr, width), jnp.bfloat16)],
            flops=8 * fine_count * width * hidden,
            name="fine_edges",
        )

    def coarse_update(s, new_fine, coarse_own, states, arrived, weights, spots):
        return call(
            functools.partial(coarse_kernel, ctile, sizes, spots, s),
            (bf16(coarse_count, width + LANES), bf16(nh, width)),
            [new_fine, recv_row, coarse_own, edge_gain, bias_rows] + states + arrived + weights,
            scratch=[pltpu.VMEM((parts * cp, width), jnp.bfloat16)],
            name="coarse_edges_and_sums",
        )

    def own_sums(new_fine, state):
        return call(
            functools.partial(own_kernel, cp),
            jax.ShapeDtypeStruct((nh, width), jnp.float32),
            [new_fine, recv_row, state],
            name="own_sums",
        )

    def node_update(s, nodes, sums, weights, spots):
        return both(
            call(
                functools.partial(node_kernel, divisor(nh, 256), s, cores, spots, len(sums)),
                bf16(nh, width),
                [nodes, bias_rows, node_gain] + sums + weights,
                name="node_update",
            )
        )

    def core_sum(agg_own, agg_other):
        return call(add_kernel, bf16(nh, width), [agg_own, swap(agg_other)], name="core_sum")

    def chip_sums(partial):
        if two:
            return [partial, across(partial)]
        every = lax.all_gather(partial, "feat", axis=0)
        every = every.reshape(cores // 2, 2, nh, width).astype(jnp.float32)
        return [lax.dynamic_index_in_dim(every.sum(axis=0), core, 0, keepdims=False)]

    def halo_of(moved, swapped):
        return [moved[0], swapped[0], moved[-1], swapped[-1]]

    def pairs(moved, swapped):
        return [x for pair in zip(moved, swapped) for x in pair]

    far_first = spread(first_pack)
    to_prev, to_next, to_far, coarse_own = node_rows_out(nodes)
    moved = exchange(to_prev, to_next, to_far)
    send_col, recv_col, recv_row, coarse_pack, *packs = after(
        (send_col, recv_col, recv_row, coarse_pack, *packs), to_prev
    )
    sent, received = gather(nodes)
    coarse_pack = after(coarse_pack, sent)
    states = [coarse_pack] + [shift(coarse_pack, by) for by in range(1, parts)]
    *moved, far_first = after((*moved, far_first), sent)
    swapped = [swap(m) for m in moved]
    weights, spots = shards(first_pack, far_first), (((0, 0, k),), ((0, k, k + width),))
    far = spread(packs[0], far_first)
    fine_edges, bias_rows = fine_update(
        0, fine_edges, sent, received, halo_of(moved, swapped), weights, spots
    )
    states, fine_edges, far = after((states, fine_edges, far))
    packs_of = [shards(packs[0], far)]
    far = spread(packs[1], far)
    state, agg_other = coarse_update(
        0, fine_edges, coarse_own, states, pairs(moved, swapped), weights, spots
    )
    state, agg_other, far = after((state, agg_other, far))
    packs_of.append(shards(packs[1], far))
    agg_own = own_sums(fine_edges, state)
    sums = chip_sums(core_sum(agg_own, agg_other))
    far = spread(packs[2], sums)
    halves = node_update(0, nodes, sums, *choose(packs_of, 0, 1))

    to_prev, to_next, to_far, coarse_own, nodes = node_rows_out(*halves)
    moved = exchange(to_prev, to_next, to_far)
    sent, received = gather(nodes)
    *moved, far = after((*moved, far), sent)
    packs_of.append(shards(packs[2], far))
    swapped = [swap(m) for m in moved]
    far = spread(packs[3], far)
    weights, spots = choose(packs_of, 3, 2)
    (fine_edges,) = fine_update(
        1, fine_edges, sent, received, halo_of(moved, swapped), weights, spots
    )
    fine_edges, far = after((fine_edges, far))
    packs_of.append(shards(packs[3], far))
    state, agg_other = coarse_update(
        1, fine_edges, coarse_own, [state], pairs(moved, swapped), weights, spots
    )
    agg_own = own_sums(fine_edges, state)
    sums = chip_sums(core_sum(agg_own, agg_other))
    halves = node_update(1, nodes, sums, *choose(packs_of, 4, 5))
    return call(join_kernel, bf16(count, width), halves, name="nodes_out")


def solution(mesh):
    placed = (
        P(("groups", "mesh"), None),
        P(("groups", "mesh", "feat"), None),
        P(("groups", "mesh", "feat")),
        P(("groups", "mesh", "feat")),
        P(("groups", "mesh")),
        P(("groups", "mesh", "feat"), None),
        P(("groups", "mesh", "feat")),
        P(("groups", "mesh", "feat")),
        P(None, "feat", None),
        P(None, "feat"),
        P(None, "feat", None),
        P(),
        P(None, "feat", None),
        P(None, "feat"),
        P(None, "feat", None),
        P(),
    )
    return jax.shard_map(
        local, mesh=mesh, in_specs=placed, out_specs=P(("groups", "mesh"), None), check_vma=False
    )
```

```python
import functools

import jax
import jax.numpy as jnp
from jax import lax
from jax.experimental import pallas as pl
from jax.experimental.pallas import tpu as pltpu
from jax.sharding import PartitionSpec as P

STEPS = 2
STRIDE = 8
LANES = 128
PART = 256
COARSE_FLOPS = (0, 0)
DIGIT = 64
VMEM_BYTES = 20 * 1024 * 1024


def dot(a, b):
    return jnp.dot(a, b, preferred_element_type=jnp.float32)


def dot_t(a, b):
    return lax.dot_general(a, b, (((1,), (1,)), ((), ())), preferred_element_type=jnp.float32)


def pick_rows(index, count):
    spots = lax.broadcasted_iota(jnp.int32, (index.shape[0], count), 1)
    return (spots == index).astype(jnp.bfloat16)


def silu(x):
    return x * (0.5 * jnp.tanh(0.5 * x) + 0.5)


def layer_norm(values, gain):
    centred = values - jnp.mean(values, axis=-1, keepdims=True)
    row_var = jnp.mean(centred * centred, axis=-1, keepdims=True)
    return centred * lax.rsqrt(row_var + 1e-05) * gain


def along_lanes(pieces):
    return jnp.concatenate([pack[:, at:to] for pack, at, to in pieces], axis=1)


def mlp(x, groups, biases, gain):
    total = None
    for shards, bias in zip(groups, biases):
        w_in = jnp.concatenate([along_lanes(pieces) for pieces, _ in shards])
        w_out = jnp.concatenate([along_lanes(pieces) for _, pieces in shards])
        act = silu(dot_t(x, w_in) + bias).astype(jnp.bfloat16)
        part = dot(act, w_out)
        total = part if total is None else total + part
    return layer_norm(total, gain)


def take_groups(it, spots, cores):
    n_packs = 1 + max(pack for pieces in spots for pack, _, _ in pieces)
    groups = []
    for _ in range(cores // 2):
        shards = []
        for _ in range(2):
            refs = [next(it) for _ in range(n_packs)]
            shards.append([[(refs[pack], at, to) for pack, at, to in pieces] for pieces in spots])
        groups.append(shards)
    return groups


def loop(steps, body):
    lax.fori_loop(0, steps, body, 0, unroll=2 if steps % 2 == 0 else 1)


def call(kernel, out_shape, args, scratch=(), flops=0, nbytes=0, memory=None, limit=VMEM_BYTES, name=None):
    in_specs = [pl.BlockSpec(memory_space=m) for m in memory or [pltpu.VMEM] * len(args)]
    out_specs = jax.tree.map(lambda _: pl.BlockSpec(memory_space=pltpu.VMEM), out_shape)
    return pl.pallas_call(
        kernel,
        out_shape=out_shape,
        in_specs=in_specs,
        out_specs=out_specs,
        scratch_shapes=list(scratch),
        compiler_params=pltpu.CompilerParams(vmem_limit_bytes=limit),
        cost_estimate=pl.CostEstimate(flops=flops, bytes_accessed=nbytes, transcendentals=0),
        name=name,
    )(*args)


def bf16(*shape):
    return jax.ShapeDtypeStruct(shape, jnp.bfloat16)


def core_index():
    return lax.rem(lax.axis_index("feat"), 2)


def join_halves(out, own, other):
    core, nh = core_index(), own.shape[0]
    out[pl.ds(pl.multiple_of(core * nh, nh), nh), :] = own[...]
    out[pl.ds(pl.multiple_of((1 - core) * nh, nh), nh), :] = other[...]


def join_kernel(*refs):
    out = refs[-1]
    core, at = core_index(), 0
    for own, other in zip(refs[:-1:2], refs[1:-1:2]):
        rows = own.shape[0]
        for who, ref in ((core, own), (1 - core, other)):
            spot = pl.multiple_of(who * (out.shape[0] // 2) + at, rows)
            out[pl.ds(spot, rows), :] = ref[...]
        at += rows


def add_kernel(own, arrived, *outs):
    at = 0
    for out in outs:
        rows = pl.ds(at, out.shape[0])
        out[...] = (own[rows, :] + arrived[rows, :].astype(jnp.float32)).astype(out.dtype)
        at += out.shape[0]


def index_digits(ref, lanes):
    index = ref[...]
    high = lax.shift_right_logical(index, DIGIT.bit_length() - 1)
    rows = jnp.concatenate([high, index & (DIGIT - 1)]).astype(jnp.float32)
    if lanes == index.shape[1]:
        return rows
    return jnp.concatenate([rows, jnp.zeros((2, lanes - index.shape[1]), jnp.float32)], axis=1)


def to_column(ref):
    count = ref.shape[1]
    rows = jnp.concatenate([index_digits(ref, count), jnp.zeros((6, count), jnp.float32)])
    unit = lax.broadcasted_iota(jnp.int32, (count, count), 0)
    unit = unit == lax.broadcasted_iota(jnp.int32, (count, count), 1)
    digits = dot_t(unit.astype(jnp.bfloat16), rows.astype(jnp.bfloat16))
    return (DIGIT * digits[:, 0:1] + digits[:, 1:2]).astype(jnp.int32)


def halo_kernel(first, *refs):
    if first:
        nodes, halo, edges, send, recv, *outs, coarse, block = refs
        count, width = edges.shape
        block[0:count, :] = edges[...]
        digits = [index_digits(ref, width) for ref in (send, recv)]
        digits.append(jnp.zeros((16 - 4, width), jnp.float32))
        block[count : count + 16, :] = jnp.concatenate(digits).astype(jnp.bfloat16)
    else:
        own, other, halo, *outs, coarse, nodes = refs
        join_halves(nodes, own, other)
    to_prev, to_next, to_far = outs
    core = core_index()
    count = nodes.shape[0]
    hr, cp = halo.shape[1] // 2, coarse.shape[0]
    hh, ch = hr // 2, cp // 2
    index = to_column(halo)
    mine = [jnp.where(core == 0, x[:hh], x[hh:]) for x in (index[:hr], index[hr:])]
    table = nodes[...]
    rows = dot(pick_rows(jnp.concatenate(mine), count), table).astype(jnp.bfloat16)
    every = STRIDE * lax.broadcasted_iota(jnp.int32, (cp, 1), 0)
    coarse[...] = dot(pick_rows(every, count), table).astype(jnp.bfloat16)
    mine = coarse[pl.ds(pl.multiple_of(core * ch, ch), ch), :]
    to_prev[pl.ds(0, hh), :] = rows[:hh]
    to_next[pl.ds(0, hh), :] = rows[hh:]
    for out, skip in ((to_prev, hh), (to_next, hh), (to_far, 0)):
        out[pl.ds(skip, ch), :] = mine
        if first:
            out[pl.ds(skip + ch, block.shape[0]), :] = block[...]


def prepare_kernel(plans, cut, *refs):
    source, (edge_b1, node_b1, nodes, halo, edges, send, recv) = refs[:4], refs[4:11]
    packs, rest = refs[11 : 11 + len(plans)], refs[11 + len(plans) :]
    *rest, sems = rest
    copies = []
    for plan, out in zip(plans, packs):
        at = 0
        for which, layer, first, last in plan:
            part = source[which].at[layer, :, first:last]
            spot = out.at[:, at : at + last - first]
            copies.append(pltpu.make_async_copy(part, spot, sems.at[len(copies)]))
            at += last - first
    for copy in copies:
        copy.start()
    hidden = edge_b1.shape[1]
    rows = [edge_b1[...].astype(jnp.float32), node_b1[...].astype(jnp.float32)]
    rows.append(jnp.zeros((16 - 2 * STEPS, hidden), jnp.float32))
    at = packs[0].shape[1] - LANES
    packs[0][0:16, at : at + hidden] = jnp.concatenate(rows).astype(jnp.bfloat16)
    if cut:
        part, *rest = rest
    halo_kernel(True, nodes, halo, edges, send, recv, *rest)
    for copy in copies:
        copy.wait()
    if cut:
        last = packs[-1]
        group = lax.axis_index("groups")
        part[...] = jnp.where(group == 0, last[:, :cut], last[:, cut:])


def gather_kernel(tile, nodes, send, recv, sent, received):
    count = nodes.shape[0]

    def body(t, carry):
        rows = pl.ds(pl.multiple_of(t * tile, tile), tile)
        table = nodes[...]
        sent[rows, :] = dot(pick_rows(send[rows, :], count), table).astype(jnp.bfloat16)
        safe = jnp.minimum(recv[rows, :], count - 1)
        received[rows, :] = dot(pick_rows(safe, count), table).astype(jnp.bfloat16)
        return carry

    loop(send.shape[0] // tile, body)


def bias_rows_of(bias_ref, line, n_groups):
    per = bias_ref.shape[1] // n_groups
    return [bias_ref[line : line + 1, g * per : (g + 1) * per] for g in range(n_groups)]


def fine_kernel(tile, sizes, spots, layer, *refs):
    count, hr, cp, parts, cores = sizes
    it = iter(refs)
    fine, sent, received, send, recv_row, gain_ref = (next(it) for _ in range(6))
    prev, nxt = ((next(it), next(it)) for _ in range(2))
    groups = take_groups(it, spots, cores)
    bias_in = None if layer == 0 else next(it)
    new_fine = next(it)
    bias_out, aggs = (next(it), [next(it), next(it)]) if layer == 0 else (None, None)
    halo_tab = next(it)

    core = core_index()
    width = gain_ref.shape[-1]
    hh = hr // 2
    for side, pair in ((0, prev), (hr, nxt)):
        for who, ref in zip((core, 1 - core), pair):
            halo_tab[pl.ds(pl.multiple_of(side + who * hh, hh), hh), :] = ref[pl.ds(0, hh), :]

    if layer == 0:
        spot = 0
        for shards in groups:
            for _, [(pack, _, at)] in shards:
                hidden = pack.shape[0]
                rows = pack[0:16, at : at + hidden].astype(jnp.float32)
                bias_out[:, spot : spot + hidden] = rows[:8]
                spot += hidden
    biases = bias_rows_of(bias_out if layer == 0 else bias_in, layer, len(groups))
    gain = gain_ref[layer : layer + 1, :].astype(jnp.float32)

    def body(t, carry):
        rows = pl.ds(pl.multiple_of(t * tile, tile), tile)
        border = dot(pick_rows(send[rows, :] - count, 2 * hr), halo_tab[...])
        senders = (sent[rows, :].astype(jnp.float32) + border).astype(jnp.bfloat16)
        old = fine[rows, :]
        x = jnp.concatenate([old, senders, received[rows, :]], axis=1)
        y = mlp(x, groups, biases, gain)
        new_fine[rows, :] = (old.astype(jnp.float32) + y).astype(jnp.bfloat16)
        return carry

    loop(fine.shape[0] // tile, body)
    if layer == 0:
        for out, half in zip(aggs, (1 - core, core)):
            place = place_in_half((count // 2, recv_row[...] - half * (count // 2)))
            sum_rows(out, 0, [place], [new_fine[...]])


def coarse_target(state, width, me, cp):
    lane = lax.broadcasted_iota(jnp.int32, (8, LANES), 1)
    weights = jnp.where(lane == 2, float(DIGIT), jnp.where(lane == 3, 1.0, 0.0)).astype(jnp.bfloat16)
    near = dot_t(weights, state[:, width : width + LANES])[:1, :].astype(jnp.int32) - me * cp
    return jnp.where((near >= 0) & (near < cp), near * STRIDE, -1)


def row_sums(base, out, new_fine, recv_row, state, target):
    width = out.shape[1]
    block = min(256, out.shape[0])
    for spot in range(0, out.shape[0], block):
        total = None
        for places, latents in ((recv_row[...], new_fine[...]), (target, state[:, :width])):
            rows = lax.broadcasted_iota(jnp.int32, (block, places.shape[1]), 0) + (base + spot)
            part = dot((rows == places).astype(jnp.bfloat16), latents)
            total = part if total is None else total + part
        out[pl.ds(spot, block), :] = total.astype(out.dtype)


def place_in_half(row):
    count, row = row
    group, rest = lax.shift_right_logical(row, 3), row & (STRIDE - 1)
    fine_rows = count - count // STRIDE
    place = jnp.where(rest == 0, fine_rows + group, (STRIDE - 1) * group + rest - 1)
    return jnp.where((row >= 0) & (row < count), place, -1)


def sum_rows(out, first, places, latents):
    total = None
    for place, latent in zip(places, latents):
        rows = lax.broadcasted_iota(jnp.int32, (out.shape[0], place.shape[1]), 0) + first
        part = dot((rows == place).astype(jnp.bfloat16), latent)
        total = part if total is None else total + part
    out[...] = total.astype(out.dtype)


def coarse_kernel(tile, sizes, spots, layer, *refs):
    count, hr, cp, parts, cores = sizes
    it = iter(refs)
    new_fine, recv_row, coarse_own, gain_ref, bias_ref = (next(it) for _ in range(5))
    given = next(it)
    arrived = [(next(it), next(it)) for _ in range(parts - 1)]
    groups = take_groups(it, spots, cores)
    state, *aggs, coarse_tab = it

    core, me = core_index(), lax.axis_index("mesh")
    width = gain_ref.shape[-1]
    hh, ch, nh = hr // 2, cp // 2, count // 2

    coarse_tab[pl.ds(pl.multiple_of(me * cp, cp), cp), :] = coarse_own[...]
    for i, pair in enumerate(arrived):
        owner = lax.rem(me + parts - 1 - i, parts)
        skip = hh if i in (0, parts - 2) else 0
        for who, ref in zip((core, 1 - core), pair):
            spot = pl.multiple_of(owner * cp + who * ch, ch)
            coarse_tab[pl.ds(spot, ch), :] = ref[pl.ds(skip, ch), 0:width]
    if layer == 0:
        per = given.shape[0] - 16
        lane = lax.broadcasted_iota(jnp.int32, (per, width), 1)
        unit = (lane == lax.broadcasted_iota(jnp.int32, (per, width), 0)).astype(jnp.bfloat16)
        blocks = [(given, 0)]
        for i, (ref, _) in enumerate(arrived):
            blocks.append((ref, ch + (hh if i in (0, parts - 2) else 0)))
        for i, (ref, skip) in enumerate(blocks):
            rows = pl.ds(i * per, per)
            state[rows, :width] = ref[pl.ds(skip, per), :]
            digits = ref[pl.ds(skip + per, 16), :].astype(jnp.float32)
            digits = jnp.concatenate([digits, jnp.zeros((LANES - 16, width), jnp.float32)])
            state[rows, width:] = dot_t(unit, digits.astype(jnp.bfloat16)).astype(jnp.bfloat16)
    else:
        state[...] = given[...]

    biases = bias_rows_of(bias_ref, layer, len(groups))
    gain = gain_ref[layer : layer + 1, :].astype(jnp.float32)

    def body(t, carry):
        rows = pl.ds(pl.multiple_of(t * tile, tile), tile)
        old = state[rows, :width]
        digits = state[rows, width : width + LANES].astype(jnp.float32)
        ends = []
        for j in range(2):
            index = DIGIT * digits[:, 2 * j : 2 * j + 1] + digits[:, 2 * j + 1 : 2 * j + 2]
            picked = pick_rows(index.astype(jnp.int32), coarse_tab.shape[0])
            ends.append(dot(picked, coarse_tab[...]).astype(jnp.bfloat16))
        y = mlp(jnp.concatenate([old] + ends, axis=1), groups, biases, gain)
        state[rows, :width] = (old.astype(jnp.float32) + y).astype(jnp.bfloat16)
        return carry

    loop(state.shape[0] // tile, body)
    target = coarse_target(state, width, me, cp)
    if layer > 0:
        row_sums((1 - core) * nh, aggs[0], new_fine, recv_row, state, target)
        return
    latents = [new_fine[...], state[:, :width]]
    for out, half in zip(aggs, (1 - core, core)):
        places = [place_in_half((nh, at - half * nh)) for at in (recv_row[...], target)]
        sum_rows(out, nh - ch, places, latents)


def own_kernel(cp, new_fine, recv_row, state, agg_own):
    core, me = core_index(), lax.axis_index("mesh")
    nh, width = agg_own.shape
    target = coarse_target(state, width, me, cp)
    row_sums(core * nh, agg_own, new_fine, recv_row, state, target)


def node_kernel(tile, layer, cores, spots, n_sums, cut, start, *refs):
    it = iter(refs)
    nodes, bias_ref, gain_ref = (next(it) for _ in range(3))
    sums = [[next(it) for _ in range(n)] for n in n_sums]
    if cut:
        groups = take_groups(it, spots, 2)
        parts = [(next(it), next(it)) for _ in range(2)]
    else:
        groups = take_groups(it, spots, cores)
    out, agg_ref, *far = it
    if cut:
        group = lax.axis_index("groups")
        for ref, (mine, other) in zip(far, parts):
            ref[:, pl.ds(pl.multiple_of(group * cut, LANES), cut)] = mine[...]
            ref[:, pl.ds(pl.multiple_of((1 - group) * cut, LANES), cut)] = other[...]
        groups.append([[[(ref, at, to) for _, at, to in pieces] for pieces in spots] for ref in far])
    nh = out.shape[0]
    agg = []
    for terms in sums:
        total = terms[0][...].astype(jnp.float32)
        for more in terms[1:]:
            total = total + more[...].astype(jnp.float32)
        agg.append(total.astype(jnp.bfloat16))
    if len(agg) > 1:
        row = lax.broadcasted_iota(jnp.int32, (nh, 1), 0)
        order = pick_rows(place_in_half((nh, row)), nh)
        agg = [dot(order, jnp.concatenate(agg)).astype(jnp.bfloat16)]
    agg_ref[...] = agg[0]
    biases = bias_rows_of(bias_ref, STEPS + layer, len(groups))
    gain = gain_ref[layer : layer + 1, :].astype(jnp.float32)
    core = core_index()
    half = nodes.shape[0] // 2
    for t in range(nh // tile):
        rows = pl.ds(t * tile, tile)
        old = nodes[pl.ds(pl.multiple_of(core * half + start + t * tile, tile), tile), :]
        x = jnp.concatenate([old, agg_ref[rows, :]], axis=1)
        y = mlp(x, groups, biases, gain)
        out[rows, :] = (old.astype(jnp.float32) + y).astype(jnp.bfloat16)


def divisor(count, most, unit=16):
    best = unit
    for size in range(unit, min(most, count) + 1, unit):
        if count % size == 0:
            best = size
    return best


def local(
    nodes,
    fine_edges,
    fine_send,
    fine_recv,
    halo_send,
    coarse_edges,
    coarse_send,
    coarse_recv,
    edge_w1,
    edge_b1,
    edge_w2,
    edge_gain,
    node_w1,
    node_b1,
    node_w2,
    node_gain,
):
    count, width = nodes.shape
    hr = halo_send.shape[0] // 2
    cp = count // STRIDE
    nh = count // 2
    fine_count = fine_edges.shape[0]
    parts = lax.axis_size("mesh")
    cores = lax.axis_size("feat")
    core = core_index()

    def swap(x):
        return lax.ppermute(x, "feat", [(i, i ^ 1) for i in range(cores)])

    def across(x):
        return lax.ppermute(x, "feat", [(i, i ^ 2) for i in range(cores)])

    def shift(x, by):
        return lax.ppermute(x, "mesh", [(i, (i + by) % parts) for i in range(parts)])

    def both(x):
        return [x, swap(x)]

    def after(x, *earlier):
        return lax.optimization_barrier((x, earlier))[0]

    two = cores == 4

    def spread(pack, *earlier):
        if two:
            return across(after(pack, *earlier) if earlier else pack)
        return lax.all_gather(pack, "feat", axis=0)

    def shards(pack, far):
        if two:
            return both(pack) + both(far)
        return [far[i] for i in range(cores)]

    k, kn = edge_w1.shape[2], node_w1.shape[2]
    w_hidden = edge_w1.shape[1]
    stream = ((2, 0, kn), (3, 0, width), (1, 1, width), (0, 1, k), (2, 1, kn), (3, 1, width))
    starts = [0]
    for _, _, lanes in stream:
        starts.append(starts[-1] + lanes)
    cuts = [0, starts[2] + PART, starts[4], starts[-1]]

    def pieces(which):
        first, last = starts[which], starts[which + 1]
        found = []
        for pack, (lo, hi) in enumerate(zip(cuts, cuts[1:])):
            if max(lo, first) < min(hi, last):
                found.append((pack, max(lo, first) - lo, min(hi, last) - lo))
        return found

    plans = [[] for _ in cuts[1:]]
    for which, (source, layer, _) in enumerate(stream):
        done = 0
        for pack, at, to in pieces(which):
            plans[pack].append((source, layer, done, done + to - at))
            done += to - at
    halo_row = halo_send.reshape(1, 2 * hr)
    own_coarse = coarse_edges.shape[0]
    coarse_count = own_coarse * parts
    plans = [[(0, 0, 0, k), (1, 0, 0, width)], *plans]
    lanes = [k + width + LANES] + [hi - lo for lo, hi in zip(cuts, cuts[1:])]
    cut = lanes[-1] // 2 if two and lax.axis_size("groups") == 2 else 0
    block = own_coarse + 16
    near, far = hr // 2 + cp // 2 + block, cp // 2 + block
    shapes = [(w_hidden, n) for n in lanes] + ([(w_hidden, cut)] if cut else [])
    shapes += [(near, width), (near, width), (far, width), (cp, width), (block, width)]
    first_pack, *packs = call(
        functools.partial(prepare_kernel, plans, cut),
        tuple(bf16(*shape) for shape in shapes),
        [edge_w1, edge_w2, node_w1, node_w2, edge_b1, node_b1, nodes, halo_row, coarse_edges]
        + [x.reshape(1, own_coarse) for x in (coarse_send, coarse_recv)],
        scratch=[pltpu.SemaphoreType.DMA((sum(len(p) for p in plans),))],
        memory=[pl.ANY] * 4 + [pltpu.VMEM] * 7,
        limit=3 * VMEM_BYTES,
        name="weights_and_halo_rows",
    )
    to_prev, to_next, to_far, coarse_own, block = packs[-5:]
    cut_part = packs[-6] if cut else None
    packs = packs[: len(plans) - 1]

    def choose(shards_of, w_in, w_out):
        used = sorted({pack for which in (w_in, w_out) for pack, _, _ in pieces(which)})
        spots = [[(used.index(p), at, to) for p, at, to in pieces(w)] for w in (w_in, w_out)]
        return [x for shard in zip(*(shards_of[p] for p in used)) for x in shard], spots

    send_col = fine_send.reshape(fine_count, 1)
    recv_col = fine_recv.reshape(fine_count, 1)
    recv_row = fine_recv.reshape(1, fine_count)
    tile = divisor(fine_count, 768)
    ctile = divisor(coarse_count, 384)
    hidden = w_hidden * cores
    sizes = (count, hr, cp, parts, cores)
    bias_rows = None

    def node_rows_out(own, other):
        near, far = hr // 2 + cp // 2, cp // 2
        return call(
            functools.partial(halo_kernel, False),
            (bf16(near, width), bf16(near, width), bf16(far, width), bf16(cp, width), bf16(count, width)),
            [own, other, halo_row],
            name="halo_rows",
        )

    def exchange(to_prev, to_next, coarse_half):
        return [
            shift({1: to_next, parts - 1: to_prev}.get(by, coarse_half), by)
            for by in range(1, parts)
        ]

    def gather(nodes):
        return call(
            functools.partial(gather_kernel, tile),
            (bf16(fine_count, width), bf16(fine_count, width)),
            [nodes, send_col, recv_col],
            flops=4 * fine_count * count * width,
            name="gather_rows",
        )

    def fine_update(s, fine, sent, received, halo, weights, spots):
        outs = [bf16(fine_count, width)]
        if s == 0:
            fine_rows = nh - cp // 2
            outs.append(jax.ShapeDtypeStruct((8, hidden), jnp.float32))
            outs += [bf16(fine_rows, width), jax.ShapeDtypeStruct((fine_rows, width), jnp.float32)]
        return call(
            functools.partial(fine_kernel, tile, sizes, spots, s),
            tuple(outs),
            [fine, sent, received, send_col, recv_row, edge_gain] + halo + weights + ([bias_rows] if s else []),
            scratch=[pltpu.VMEM((2 * hr, width), jnp.bfloat16)],
            flops=8 * fine_count * width * hidden,
            name="fine_edges",
        )

    def coarse_update(s, new_fine, coarse_own, state, arrived, weights, spots):
        aggs = [bf16(nh, width)] if s else [bf16(cp // 2, width), jax.ShapeDtypeStruct((cp // 2, width), jnp.float32)]
        return call(
            functools.partial(coarse_kernel, ctile, sizes, spots, s),
            (bf16(coarse_count, width + LANES), *aggs),
            [new_fine, recv_row, coarse_own, edge_gain, bias_rows, state] + arrived + weights,
            scratch=[pltpu.VMEM((parts * cp, width), jnp.bfloat16)],
            flops=COARSE_FLOPS[s],
            name="coarse_edges_and_sums",
        )

    def own_sums(new_fine, state):
        return call(
            functools.partial(own_kernel, cp),
            jax.ShapeDtypeStruct((nh, width), jnp.float32),
            [new_fine, recv_row, state],
            name="own_sums",
        )

    def node_update(s, nodes, sums, weights, spots, cut=0, start=0):
        far = [pltpu.VMEM((w_hidden, 2 * cut), jnp.bfloat16)] * 2 if cut else []
        rows = sum(part[0].shape[0] for part in sums)
        return both(
            call(
                functools.partial(node_kernel, rows, s, cores, spots, [len(part) for part in sums], cut, start),
                bf16(rows, width),
                [nodes, bias_rows, node_gain] + [x for part in sums for x in part] + weights,
                scratch=[pltpu.VMEM((rows, width), jnp.bfloat16), *far],
                name="node_update",
            )
        )

    def core_sum(agg_own, agg_other, cuts=1):
        rows = agg_own.shape[0] // cuts
        parts = call(
            add_kernel, (bf16(rows, width),) * cuts, [agg_own, swap(agg_other)], name="core_sum"
        )
        return parts if cuts > 1 else parts[0]

    def chip_sums(partial):
        if two:
            return [partial, across(partial)]
        every = lax.all_gather(partial, "feat", axis=0)
        every = every.reshape(cores // 2, 2, *partial.shape).astype(jnp.float32)
        return [lax.dynamic_index_in_dim(every.sum(axis=0), core, 0, keepdims=False)]

    def halo_of(moved, swapped):
        return [moved[0], swapped[0], moved[-1], swapped[-1]]

    def pairs(moved, swapped):
        return [x for pair in zip(moved, swapped) for x in pair]

    far_first = spread(first_pack)
    moved = exchange(to_prev, to_next, to_far)
    send_col, recv_col, recv_row, *packs = after(
        (send_col, recv_col, recv_row, *packs), to_prev
    )
    sent, received = gather(nodes)
    moved[0], moved[-1], far_first = after((moved[0], moved[-1], far_first), sent)
    swapped = {i: swap(moved[i]) for i in (0, -1)}
    weights, spots = shards(first_pack, far_first), (((0, 0, k),), ((0, k, k + width),))
    far = spread(packs[0], far_first)
    fine_edges, bias_rows, other, own = fine_update(
        0, fine_edges, sent, received, halo_of(moved, swapped), weights, spots
    )
    other, far, *moved[1:-1] = after((other, far, *moved[1:-1]))
    swapped = [swapped[0], *(swap(m) for m in moved[1:-1]), swapped[-1]]
    partial = core_sum(own, other)
    fine_edges, far = after((fine_edges, far), partial)
    packs_of = [shards(packs[0], far)]
    fine_part = chip_sums(partial)
    state, other, own = coarse_update(
        0, fine_edges, coarse_own, block, pairs(moved, swapped), weights, spots
    )
    sums = [fine_part, chip_sums(core_sum(own, other))]
    far = spread(packs[1], sums)
    halves = node_update(0, nodes, sums, *choose(packs_of, 0, 1))

    to_prev, to_next, to_far, coarse_own, nodes = node_rows_out(*halves)
    moved = exchange(to_prev, to_next, to_far)
    sent, received = gather(nodes)
    *moved, far = after((*moved, far), sent)
    packs_of.append(shards(packs[1], far))
    swapped = [swap(m) for m in moved]
    far = across(after(cut_part, far)) if cut else spread(packs[2], far)
    weights, spots = choose(packs_of, 3, 2)
    (fine_edges,) = fine_update(
        1, fine_edges, sent, received, halo_of(moved, swapped), weights, spots
    )
    fine_edges, far = after((fine_edges, far))
    state, agg_other = coarse_update(
        1, fine_edges, coarse_own, state, pairs(moved, swapped), weights, spots
    )
    agg_own = own_sums(fine_edges, state)
    partial = core_sum(agg_own, agg_other, 2)
    sums = [chip_sums(part) for part in partial]
    if cut:
        mine = both(far)
        others = both(lax.ppermute(after(far, partial), "groups", [(0, 1), (1, 0)]))
        weights = both(packs[2]) + pairs(mine, others)
        spots = [[(0, at - starts[4], at - starts[4] + n)] for at, n in zip(starts[4:], (kn, width))]
    else:
        packs_of.append(shards(packs[2], far))
        weights, spots = choose(packs_of, 4, 5)
    halves = [
        half
        for i, part in enumerate(sums)
        for half in node_update(1, nodes, [part], weights, spots, cut, i * nh // 2)
    ]
    return call(join_kernel, bf16(count, width), halves, name="nodes_out")


def solution(mesh):
    placed = (
        P(("groups", "mesh"), None),
        P(("groups", "mesh", "feat"), None),
        P(("groups", "mesh", "feat")),
        P(("groups", "mesh", "feat")),
        P(("groups", "mesh")),
        P(("groups", "mesh", "feat"), None),
        P(("groups", "mesh", "feat")),
        P(("groups", "mesh", "feat")),
        P(None, "feat", None),
        P(None, "feat"),
        P(None, "feat", None),
        P(),
        P(None, "feat", None),
        P(None, "feat"),
        P(None, "feat", None),
        P(),
    )
    return jax.shard_map(
        local, mesh=mesh, in_specs=placed, out_specs=P(("groups", "mesh"), None), check_vma=False
    )
```

```python
import functools

import jax
import jax.numpy as jnp
from jax import lax
from jax.experimental import pallas as pl
from jax.experimental.pallas import tpu as pltpu
from jax.sharding import PartitionSpec as P

STEPS = 2
STRIDE = 8
LANES = 128
COARSE_FLOPS = (0, 0)
RELAYED = 4
DIGIT = 64
VMEM_BYTES = 20 * 1024 * 1024


def dot(a, b):
    return jnp.dot(a, b, preferred_element_type=jnp.float32)


def dot_t(a, b):
    return lax.dot_general(a, b, (((1,), (1,)), ((), ())), preferred_element_type=jnp.float32)


def pick_rows(index, count):
    spots = lax.broadcasted_iota(jnp.int32, (index.shape[0], count), 1)
    return (spots == index).astype(jnp.bfloat16)


def silu(x):
    return x * (0.5 * jnp.tanh(0.5 * x) + 0.5)


def layer_norm(values, gain):
    centred = values - jnp.mean(values, axis=-1, keepdims=True)
    row_var = jnp.mean(centred * centred, axis=-1, keepdims=True)
    return centred * lax.rsqrt(row_var + 1e-05) * gain


def along_lanes(pieces):
    return jnp.concatenate([pack[:, at:to] for pack, at, to in pieces], axis=1)


def mlp(x, groups, biases, gain):
    total = None
    for shards, bias in zip(groups, biases):
        w_in = jnp.concatenate([along_lanes(pieces) for pieces, _ in shards])
        w_out = jnp.concatenate([along_lanes(pieces) for _, pieces in shards])
        act = silu(dot_t(x, w_in) + bias).astype(jnp.bfloat16)
        part = dot(act, w_out)
        total = part if total is None else total + part
    return layer_norm(total, gain)


def take_groups(it, spots, cores):
    n_packs = 1 + max(pack for pieces in spots for pack, _, _ in pieces)
    groups = []
    for _ in range(cores // 2):
        shards = []
        for _ in range(2):
            refs = [next(it) for _ in range(n_packs)]
            shards.append([[(refs[pack], at, to) for pack, at, to in pieces] for pieces in spots])
        groups.append(shards)
    return groups


def loop(steps, body):
    lax.fori_loop(0, steps, body, 0, unroll=2 if steps % 2 == 0 else 1)


def call(kernel, out_shape, args, scratch=(), flops=0, nbytes=0, memory=None, out_memory=pltpu.VMEM, limit=VMEM_BYTES, name=None):
    in_specs = [pl.BlockSpec(memory_space=m) for m in memory or [pltpu.VMEM] * len(args)]
    out_specs = jax.tree.map(lambda _: pl.BlockSpec(memory_space=out_memory), out_shape)
    return pl.pallas_call(
        kernel,
        out_shape=out_shape,
        in_specs=in_specs,
        out_specs=out_specs,
        scratch_shapes=list(scratch),
        compiler_params=pltpu.CompilerParams(vmem_limit_bytes=limit),
        cost_estimate=pl.CostEstimate(flops=flops, bytes_accessed=nbytes, transcendentals=0),
        name=name,
    )(*args)


def bf16(*shape):
    return jax.ShapeDtypeStruct(shape, jnp.bfloat16)


def core_index():
    return lax.rem(lax.axis_index("feat"), 2)


def join_halves(out, own, other):
    core, nh = core_index(), own.shape[0]
    out[pl.ds(pl.multiple_of(core * nh, nh), nh), :] = own[...]
    out[pl.ds(pl.multiple_of((1 - core) * nh, nh), nh), :] = other[...]


def join_kernel(own, other, out):
    join_halves(out, own, other)


def add_kernel(own, arrived, out):
    out[...] = (own[...] + arrived[...].astype(jnp.float32)).astype(out.dtype)


def index_digits(ref, lanes):
    index = ref[...]
    high = lax.shift_right_logical(index, DIGIT.bit_length() - 1)
    rows = jnp.concatenate([high, index & (DIGIT - 1)]).astype(jnp.float32)
    if lanes == index.shape[1]:
        return rows
    return jnp.concatenate([rows, jnp.zeros((2, lanes - index.shape[1]), jnp.float32)], axis=1)


def to_column(ref):
    count = ref.shape[1]
    rows = jnp.concatenate([index_digits(ref, count), jnp.zeros((6, count), jnp.float32)])
    unit = lax.broadcasted_iota(jnp.int32, (count, count), 0)
    unit = unit == lax.broadcasted_iota(jnp.int32, (count, count), 1)
    digits = dot_t(unit.astype(jnp.bfloat16), rows.astype(jnp.bfloat16))
    return (DIGIT * digits[:, 0:1] + digits[:, 1:2]).astype(jnp.int32)


def halo_kernel(first, *refs):
    if first:
        nodes, halo, edges, send, recv, *outs, coarse, block = refs
        count, width = edges.shape
        block[0:count, :] = edges[...]
        digits = [index_digits(ref, width) for ref in (send, recv)]
        digits.append(jnp.zeros((16 - 4, width), jnp.float32))
        block[count : count + 16, :] = jnp.concatenate(digits).astype(jnp.bfloat16)
    else:
        own, other, halo, *outs, coarse, nodes = refs
        join_halves(nodes, own, other)
    to_prev, to_next, to_far = outs
    core = core_index()
    count = nodes.shape[0]
    hr, cp = halo.shape[1] // 2, coarse.shape[0]
    hh, ch = hr // 2, cp // 2
    index = to_column(halo)
    mine = [jnp.where(core == 0, x[:hh], x[hh:]) for x in (index[:hr], index[hr:])]
    table = nodes[...]
    rows = dot(pick_rows(jnp.concatenate(mine), count), table).astype(jnp.bfloat16)
    every = STRIDE * lax.broadcasted_iota(jnp.int32, (cp, 1), 0)
    coarse[...] = dot(pick_rows(every, count), table).astype(jnp.bfloat16)
    mine = coarse[pl.ds(pl.multiple_of(core * ch, ch), ch), :]
    to_prev[pl.ds(0, hh), :] = rows[:hh]
    to_next[pl.ds(0, hh), :] = rows[hh:]
    for out, skip in ((to_prev, hh), (to_next, hh), (to_far, 0)):
        out[pl.ds(skip, ch), :] = mine
        if first:
            out[pl.ds(skip + ch, block.shape[0]), :] = block[...]


def prepare_kernel(plans, cut, n_small, *refs):
    n_out = len(plans) + 5 + (1 if cut else 0)
    source, given, outs = refs[:4], refs[4 : 4 + n_small], refs[4 + n_small :][:n_out]
    refs = refs[4 + n_small + n_out :]
    small, made, sems = refs[:n_small], refs[n_small:-1], refs[-1]
    started = []

    def start(src, dst):
        copy = pltpu.make_async_copy(src, dst, sems.at[len(started)])
        copy.start()
        started.append(copy)
        return copy

    arriving = [start(src, dst) for src, dst in zip(given, small)]
    loads = []
    for plan, pack in zip(plans, made):
        at, parts = 0, []
        for which, layer, first, last in plan:
            spot = pack.at[:, at : at + last - first]
            parts.append(start(source[which].at[layer, :, first:last], spot))
            at += last - first
        loads.append(parts)
    for copy in arriving:
        copy.wait()
    edge_b1, node_b1, nodes, halo, edges, send, recv = small
    hidden = edge_b1.shape[1]
    rows = [edge_b1[...].astype(jnp.float32), node_b1[...].astype(jnp.float32)]
    rows.append(jnp.zeros((16 - 2 * STEPS, hidden), jnp.float32))
    at = made[0].shape[1] - LANES
    made[0][0:16, at : at + hidden] = jnp.concatenate(rows).astype(jnp.bfloat16)
    n_packs = len(plans) + (1 if cut else 0)
    halo_kernel(True, nodes, halo, edges, send, recv, *made[n_packs:])
    stores = [start(src, dst) for src, dst in zip(made[n_packs:], outs[n_packs:])]
    for parts, src, dst in zip(loads, made, outs):
        for copy in parts:
            copy.wait()
        stores.append(start(src, dst))
    if cut:
        last = made[len(plans) - 1]
        group = lax.axis_index("groups")
        made[len(plans)][...] = jnp.where(group == 0, last[:, :cut], last[:, cut:])
        stores.append(start(made[len(plans)], outs[len(plans)]))
    for copy in stores:
        copy.wait()


def gather_kernel(tile, nodes, send, recv, sent, received):
    count = nodes.shape[0]

    def body(t, carry):
        rows = pl.ds(pl.multiple_of(t * tile, tile), tile)
        table = nodes[...]
        sent[rows, :] = dot(pick_rows(send[rows, :], count), table).astype(jnp.bfloat16)
        safe = jnp.minimum(recv[rows, :], count - 1)
        received[rows, :] = dot(pick_rows(safe, count), table).astype(jnp.bfloat16)
        return carry

    loop(send.shape[0] // tile, body)


def bias_rows_of(bias_ref, line, n_groups):
    per = bias_ref.shape[1] // n_groups
    return [bias_ref[line : line + 1, g * per : (g + 1) * per] for g in range(n_groups)]


def fine_kernel(tile, sizes, spots, layer, *refs):
    count, hr, cp, parts, cores = sizes
    it = iter(refs)
    fine, sent, received, send, recv_row, gain_ref = (next(it) for _ in range(6))
    prev, nxt = ((next(it), next(it)) for _ in range(2))
    groups = take_groups(it, spots, cores)
    bias_in = None if layer == 0 else next(it)
    new_fine = next(it)
    bias_out = next(it) if layer == 0 else None
    aggs = [next(it), next(it)]
    halo_tab = next(it)

    core = core_index()
    width = gain_ref.shape[-1]
    hh = hr // 2
    for side, pair in ((0, prev), (hr, nxt)):
        for who, ref in zip((core, 1 - core), pair):
            halo_tab[pl.ds(pl.multiple_of(side + who * hh, hh), hh), :] = ref[pl.ds(0, hh), :]

    if layer == 0:
        spot = 0
        for shards in groups:
            for _, [(pack, _, at)] in shards:
                hidden = pack.shape[0]
                rows = pack[0:16, at : at + hidden].astype(jnp.float32)
                bias_out[:, spot : spot + hidden] = rows[:8]
                spot += hidden
    biases = bias_rows_of(bias_out if layer == 0 else bias_in, layer, len(groups))
    gain = gain_ref[layer : layer + 1, :].astype(jnp.float32)

    def body(t, carry):
        rows = pl.ds(pl.multiple_of(t * tile, tile), tile)
        border = dot(pick_rows(send[rows, :] - count, 2 * hr), halo_tab[...])
        senders = (sent[rows, :].astype(jnp.float32) + border).astype(jnp.bfloat16)
        old = fine[rows, :]
        x = jnp.concatenate([old, senders, received[rows, :]], axis=1)
        y = mlp(x, groups, biases, gain)
        new_fine[rows, :] = (old.astype(jnp.float32) + y).astype(jnp.bfloat16)
        return carry

    loop(fine.shape[0] // tile, body)
    for out, half in zip(aggs, (1 - core, core)):
        place = place_in_half((count // 2, recv_row[...] - half * (count // 2)))
        sum_rows(out, 0, [place], [new_fine[...]])


def coarse_target(state, width, me, cp):
    lane = lax.broadcasted_iota(jnp.int32, (8, LANES), 1)
    weights = jnp.where(lane == 2, float(DIGIT), jnp.where(lane == 3, 1.0, 0.0)).astype(jnp.bfloat16)
    near = dot_t(weights, state[:, width : width + LANES])[:1, :].astype(jnp.int32) - me * cp
    return jnp.where((near >= 0) & (near < cp), near * STRIDE, -1)


def place_in_half(row):
    count, row = row
    group, rest = lax.shift_right_logical(row, 3), row & (STRIDE - 1)
    fine_rows = count - count // STRIDE
    place = jnp.where(rest == 0, fine_rows + group, (STRIDE - 1) * group + rest - 1)
    return jnp.where((row >= 0) & (row < count), place, -1)


def sum_rows(out, first, places, latents):
    total = None
    for place, latent in zip(places, latents):
        rows = lax.broadcasted_iota(jnp.int32, (out.shape[0], place.shape[1]), 0) + first
        part = dot((rows == place).astype(jnp.bfloat16), latent)
        total = part if total is None else total + part
    out[...] = total.astype(out.dtype)


def coarse_kernel(tile, sizes, spots, layer, *refs):
    count, hr, cp, parts, cores = sizes
    it = iter(refs)
    new_fine, recv_row, coarse_own, gain_ref, bias_ref = (next(it) for _ in range(5))
    given = next(it)
    arrived = [(next(it), next(it)) for _ in range(parts - 1)]
    groups = take_groups(it, spots, cores)
    state, *aggs, coarse_tab = it

    core, me = core_index(), lax.axis_index("mesh")
    width = gain_ref.shape[-1]
    hh, ch, nh = hr // 2, cp // 2, count // 2

    coarse_tab[pl.ds(pl.multiple_of(me * cp, cp), cp), :] = coarse_own[...]
    for i, pair in enumerate(arrived):
        owner = lax.rem(me + parts - 1 - i, parts)
        skip = hh if i in (0, parts - 2) or (parts == RELAYED and layer == 0) else 0
        for who, ref in zip((core, 1 - core), pair):
            spot = pl.multiple_of(owner * cp + who * ch, ch)
            coarse_tab[pl.ds(spot, ch), :] = ref[pl.ds(skip, ch), 0:width]
    if layer == 0:
        per = given.shape[0] - 16
        lane = lax.broadcasted_iota(jnp.int32, (per, width), 1)
        unit = (lane == lax.broadcasted_iota(jnp.int32, (per, width), 0)).astype(jnp.bfloat16)
        blocks = [(given, 0)]
        for i, (ref, _) in enumerate(arrived):
            near = i in (0, parts - 2) or parts == RELAYED
            blocks.append((ref, ch + (hh if near else 0)))
        for i, (ref, skip) in enumerate(blocks):
            rows = pl.ds(i * per, per)
            state[rows, :width] = ref[pl.ds(skip, per), :]
            digits = ref[pl.ds(skip + per, 16), :].astype(jnp.float32)
            digits = jnp.concatenate([digits, jnp.zeros((LANES - 16, width), jnp.float32)])
            state[rows, width:] = dot_t(unit, digits.astype(jnp.bfloat16)).astype(jnp.bfloat16)
    else:
        state[...] = given[...]

    biases = bias_rows_of(bias_ref, layer, len(groups))
    gain = gain_ref[layer : layer + 1, :].astype(jnp.float32)

    def body(t, carry):
        rows = pl.ds(pl.multiple_of(t * tile, tile), tile)
        old = state[rows, :width]
        digits = state[rows, width : width + LANES].astype(jnp.float32)
        ends = []
        for j in range(2):
            index = DIGIT * digits[:, 2 * j : 2 * j + 1] + digits[:, 2 * j + 1 : 2 * j + 2]
            picked = pick_rows(index.astype(jnp.int32), coarse_tab.shape[0])
            ends.append(dot(picked, coarse_tab[...]).astype(jnp.bfloat16))
        y = mlp(jnp.concatenate([old] + ends, axis=1), groups, biases, gain)
        state[rows, :width] = (old.astype(jnp.float32) + y).astype(jnp.bfloat16)
        return carry

    loop(state.shape[0] // tile, body)
    target = coarse_target(state, width, me, cp)
    latents = [new_fine[...], state[:, :width]]
    for out, half in zip(aggs, (1 - core, core)):
        places = [place_in_half((nh, at - half * nh)) for at in (recv_row[...], target)]
        sum_rows(out, nh - ch, places, latents)


def node_kernel(tile, layer, cores, spots, n_sums, cut, *refs):
    it = iter(refs)
    nodes, bias_ref, gain_ref = (next(it) for _ in range(3))
    sums = [[next(it) for _ in range(n)] for n in n_sums]
    if cut:
        groups = take_groups(it, spots, 2)
        parts = [(next(it), next(it)) for _ in range(2)]
    else:
        groups = take_groups(it, spots, cores)
    out, agg_ref, *far = it
    if cut:
        group = lax.axis_index("groups")
        for ref, (mine, other) in zip(far, parts):
            ref[:, pl.ds(pl.multiple_of(group * cut, LANES), cut)] = mine[...]
            ref[:, pl.ds(pl.multiple_of((1 - group) * cut, LANES), cut)] = other[...]
        groups.append([[[(ref, at, to) for _, at, to in pieces] for pieces in spots] for ref in far])
    nh = out.shape[0]
    agg = []
    for terms in sums:
        total = terms[0][...].astype(jnp.float32)
        for more in terms[1:]:
            total = total + more[...].astype(jnp.float32)
        agg.append(total.astype(jnp.bfloat16))
    if len(agg) > 1:
        row = lax.broadcasted_iota(jnp.int32, (nh, 1), 0)
        order = pick_rows(place_in_half((nh, row)), nh)
        agg = [dot(order, jnp.concatenate(agg)).astype(jnp.bfloat16)]
    agg_ref[...] = agg[0]
    biases = bias_rows_of(bias_ref, STEPS + layer, len(groups))
    gain = gain_ref[layer : layer + 1, :].astype(jnp.float32)
    core = core_index()
    half = nodes.shape[0] // 2
    for t in range(nh // tile):
        rows = pl.ds(t * tile, tile)
        old = nodes[pl.ds(pl.multiple_of(core * half + t * tile, tile), tile), :]
        x = jnp.concatenate([old, agg_ref[rows, :]], axis=1)
        y = mlp(x, groups, biases, gain)
        out[rows, :] = (old.astype(jnp.float32) + y).astype(jnp.bfloat16)


def divisor(count, most, unit=16):
    best = unit
    for size in range(unit, min(most, count) + 1, unit):
        if count % size == 0:
            best = size
    return best


def local(
    nodes,
    fine_edges,
    fine_send,
    fine_recv,
    halo_send,
    coarse_edges,
    coarse_send,
    coarse_recv,
    edge_w1,
    edge_b1,
    edge_w2,
    edge_gain,
    node_w1,
    node_b1,
    node_w2,
    node_gain,
):
    count, width = nodes.shape
    hr = halo_send.shape[0] // 2
    cp = count // STRIDE
    nh = count // 2
    fine_count = fine_edges.shape[0]
    parts = lax.axis_size("mesh")
    cores = lax.axis_size("feat")
    core = core_index()

    def swap(x):
        return lax.ppermute(x, "feat", [(i, i ^ 1) for i in range(cores)])

    def across(x):
        return lax.ppermute(x, "feat", [(i, i ^ 2) for i in range(cores)])

    def shift(x, by):
        return lax.ppermute(x, "mesh", [(i, (i + by) % parts) for i in range(parts)])

    def both(x):
        return [x, swap(x)]

    def after(x, *earlier):
        return lax.optimization_barrier((x, earlier))[0]

    two = cores == 4

    def spread(pack, *earlier):
        if two:
            return across(after(pack, *earlier) if earlier else pack)
        return lax.all_gather(pack, "feat", axis=0)

    def shards(pack, far):
        if two:
            return both(pack) + both(far)
        return [far[i] for i in range(cores)]

    k, kn = edge_w1.shape[2], node_w1.shape[2]
    w_hidden = edge_w1.shape[1]
    stream = ((2, 0, kn), (3, 0, width), (1, 1, width), (0, 1, k), (2, 1, kn), (3, 1, width))
    starts = [0]
    for _, _, lanes in stream:
        starts.append(starts[-1] + lanes)
    cuts = [0, starts[2], starts[4], starts[-1]]

    def pieces(which):
        first, last = starts[which], starts[which + 1]
        found = []
        for pack, (lo, hi) in enumerate(zip(cuts, cuts[1:])):
            if max(lo, first) < min(hi, last):
                found.append((pack, max(lo, first) - lo, min(hi, last) - lo))
        return found

    plans = [[] for _ in cuts[1:]]
    for which, (source, layer, _) in enumerate(stream):
        done = 0
        for pack, at, to in pieces(which):
            plans[pack].append((source, layer, done, done + to - at))
            done += to - at
    halo_row = halo_send.reshape(1, 2 * hr)
    own_coarse = coarse_edges.shape[0]
    coarse_count = own_coarse * parts
    plans = [[(0, 0, 0, k), (1, 0, 0, width)], *plans]
    lanes = [k + width + LANES] + [hi - lo for lo, hi in zip(cuts, cuts[1:])]
    cut = lanes[-1] // 2 if two and lax.axis_size("groups") == 2 else 0
    block = own_coarse + 16
    near, far = hr // 2 + cp // 2 + block, cp // 2 + block
    shapes = [(w_hidden, n) for n in lanes] + ([(w_hidden, cut)] if cut else [])
    shapes += [(near, width), (near, width), (far, width), (cp, width), (block, width)]
    small = [edge_b1, node_b1, nodes, halo_row, coarse_edges]
    small += [x.reshape(1, own_coarse) for x in (coarse_send, coarse_recv)]
    n_copies = len(small) + sum(len(p) for p in plans) + len(shapes)
    first_pack, *packs = call(
        functools.partial(prepare_kernel, plans, cut, len(small)),
        tuple(bf16(*shape) for shape in shapes),
        [edge_w1, edge_w2, node_w1, node_w2, *small],
        scratch=[pltpu.VMEM(x.shape, x.dtype) for x in small]
        + [pltpu.VMEM(shape, jnp.bfloat16) for shape in shapes]
        + [pltpu.SemaphoreType.DMA((n_copies,))],
        memory=[pl.ANY] * (4 + len(small)),
        out_memory=pl.ANY,
        limit=3 * VMEM_BYTES,
        name="weights_and_halo_rows",
    )
    to_prev, to_next, to_far, coarse_own, block = packs[-5:]
    cut_part = packs[-6] if cut else None
    packs = packs[: len(plans) - 1]

    def choose(shards_of, w_in, w_out):
        used = sorted({pack for which in (w_in, w_out) for pack, _, _ in pieces(which)})
        spots = [[(used.index(p), at, to) for p, at, to in pieces(w)] for w in (w_in, w_out)]
        return [x for shard in zip(*(shards_of[p] for p in used)) for x in shard], spots

    send_col = fine_send.reshape(fine_count, 1)
    recv_col = fine_recv.reshape(fine_count, 1)
    recv_row = fine_recv.reshape(1, fine_count)
    tile = divisor(fine_count, 768)
    ctile = divisor(coarse_count, 384)
    hidden = w_hidden * cores
    sizes = (count, hr, cp, parts, cores)
    bias_rows = None

    def node_rows_out(own, other):
        near, far = hr // 2 + cp // 2, cp // 2
        return call(
            functools.partial(halo_kernel, False),
            (bf16(near, width), bf16(near, width), bf16(far, width), bf16(cp, width), bf16(count, width)),
            [own, other, halo_row],
            name="halo_rows",
        )

    def exchange(to_prev, to_next, to_far, relayed=False):
        return [
            shift({1: to_next, parts - 1: to_prev}.get(by, to_far), by)
            for by in range(1, parts)
            if by in (1, parts - 1) or not relayed
        ]

    def far_rows(moved):
        return [shift(moved[0], 1)] if parts == RELAYED else moved[1:-1]

    def gather(nodes):
        return call(
            functools.partial(gather_kernel, tile),
            (bf16(fine_count, width), bf16(fine_count, width)),
            [nodes, send_col, recv_col],
            flops=4 * fine_count * count * width,
            name="gather_rows",
        )

    def fine_update(s, fine, sent, received, halo, weights, spots):
        outs = [bf16(fine_count, width)]
        if s == 0:
            outs.append(jax.ShapeDtypeStruct((8, hidden), jnp.float32))
        fine_rows = nh - cp // 2
        outs += [bf16(fine_rows, width), jax.ShapeDtypeStruct((fine_rows, width), jnp.float32)]
        return call(
            functools.partial(fine_kernel, tile, sizes, spots, s),
            tuple(outs),
            [fine, sent, received, send_col, recv_row, edge_gain] + halo + weights + ([bias_rows] if s else []),
            scratch=[pltpu.VMEM((2 * hr, width), jnp.bfloat16)],
            flops=8 * fine_count * width * hidden,
            name="fine_edges",
        )

    def coarse_update(s, new_fine, coarse_own, state, arrived, weights, spots):
        aggs = [bf16(cp // 2, width), jax.ShapeDtypeStruct((cp // 2, width), jnp.float32)]
        return call(
            functools.partial(coarse_kernel, ctile, sizes, spots, s),
            (bf16(coarse_count, width + LANES), *aggs),
            [new_fine, recv_row, coarse_own, edge_gain, bias_rows, state] + arrived + weights,
            scratch=[pltpu.VMEM((parts * cp, width), jnp.bfloat16)],
            flops=COARSE_FLOPS[s],
            name="coarse_edges_and_sums",
        )

    def node_update(s, nodes, sums, weights, spots, cut=0):
        far = [pltpu.VMEM((w_hidden, 2 * cut), jnp.bfloat16)] * 2 if cut else []
        rows = sum(part[0].shape[0] for part in sums)
        return both(
            call(
                functools.partial(node_kernel, rows, s, cores, spots, [len(part) for part in sums], cut),
                bf16(rows, width),
                [nodes, bias_rows, node_gain] + [x for part in sums for x in part] + weights,
                scratch=[pltpu.VMEM((rows, width), jnp.bfloat16), *far],
                name="node_update",
            )
        )

    def core_sum(agg_own, agg_other):
        return call(add_kernel, bf16(*agg_own.shape), [agg_own, swap(agg_other)], name="core_sum")

    def chip_sums(partial):
        if two:
            return [partial, across(partial)]
        every = lax.all_gather(partial, "feat", axis=0)
        every = every.reshape(cores // 2, 2, *partial.shape).astype(jnp.float32)
        return [lax.dynamic_index_in_dim(every.sum(axis=0), core, 0, keepdims=False)]

    def halo_of(moved, swapped):
        return [moved[0], swapped[0], moved[-1], swapped[-1]]

    def pairs(moved, swapped):
        return [x for pair in zip(moved, swapped) for x in pair]

    far_first = spread(first_pack)
    moved = exchange(to_prev, to_next, to_far, parts == RELAYED)
    send_col, recv_col, recv_row, *packs = after(
        (send_col, recv_col, recv_row, *packs), to_prev
    )
    sent, received = gather(nodes)
    moved[0], moved[-1], far_first = after((moved[0], moved[-1], far_first), sent)
    relayed = far_rows(moved)
    swapped = {i: swap(moved[i]) for i in (0, -1)}
    weights, spots = shards(first_pack, far_first), (((0, 0, k),), ((0, k, k + width),))
    far = spread(packs[0], far_first)
    fine_edges, bias_rows, other, own = fine_update(
        0, fine_edges, sent, received, halo_of(moved, swapped), weights, spots
    )
    other, far, *relayed = after((other, far, *relayed))
    swapped = [swapped[0], *(swap(m) for m in relayed), swapped[-1]]
    moved = [moved[0], *relayed, moved[-1]]
    partial = core_sum(own, other)
    fine_edges, far = after((fine_edges, far), partial)
    packs_of = [shards(packs[0], far)]
    fine_part = chip_sums(partial)
    state, other, own = coarse_update(
        0, fine_edges, coarse_own, block, pairs(moved, swapped), weights, spots
    )
    sums = [fine_part, chip_sums(core_sum(own, other))]
    far = spread(packs[1], sums)
    halves = node_update(0, nodes, sums, *choose(packs_of, 0, 1))

    to_prev, to_next, to_far, coarse_own, nodes = node_rows_out(*halves)
    moved = exchange(to_prev, to_next, to_far)
    sent, received = gather(nodes)
    *moved, far = after((*moved, far), sent)
    packs_of.append(shards(packs[1], far))
    swapped = [swap(m) for m in moved]
    far = across(after(cut_part, far)) if cut else spread(packs[2], far)
    weights, spots = choose(packs_of, 3, 2)
    fine_edges, other, own = fine_update(
        1, fine_edges, sent, received, halo_of(moved, swapped), weights, spots
    )
    other, far = after((other, far))
    partial = core_sum(own, other)
    fine_part = chip_sums(partial)
    state, other, own = coarse_update(
        1, fine_edges, coarse_own, state, pairs(moved, swapped), weights, spots
    )
    if cut:
        mine = both(far)
        others = lax.ppermute(far, "groups", [(0, 1), (1, 0)])
        own, others = after((own, others))
        weights = both(packs[2]) + pairs(mine, both(others))
        spots = [[(0, at - starts[4], at - starts[4] + n)] for at, n in zip(starts[4:], (kn, width))]
    else:
        packs_of.append(shards(packs[2], far))
        weights, spots = choose(packs_of, 4, 5)
    sums = [fine_part, chip_sums(core_sum(own, other))]
    halves = node_update(1, nodes, sums, weights, spots, cut)
    return call(join_kernel, bf16(count, width), halves, name="nodes_out")


def solution(mesh):
    placed = (
        P(("groups", "mesh"), None),
        P(("groups", "mesh", "feat"), None),
        P(("groups", "mesh", "feat")),
        P(("groups", "mesh", "feat")),
        P(("groups", "mesh")),
        P(("groups", "mesh", "feat"), None),
        P(("groups", "mesh", "feat")),
        P(("groups", "mesh", "feat")),
        P(None, "feat", None),
        P(None, "feat"),
        P(None, "feat", None),
        P(),
        P(None, "feat", None),
        P(None, "feat"),
        P(None, "feat", None),
        P(),
    )
    return jax.shard_map(
        local, mesh=mesh, in_specs=placed, out_specs=P(("groups", "mesh"), None), check_vma=False
    )
```

```python
import functools

import jax
import jax.numpy as jnp
from jax import lax
from jax.experimental import pallas as pl
from jax.experimental.pallas import tpu as pltpu
from jax.sharding import PartitionSpec as P

STEPS = 2
STRIDE = 8
LANES = 128
COARSE_FLOPS = (0, 0)
RELAYED = 4
DIGIT = 64
VMEM_BYTES = 20 * 1024 * 1024


def dot(a, b):
    return jnp.dot(a, b, preferred_element_type=jnp.float32)


def dot_t(a, b):
    return lax.dot_general(a, b, (((1,), (1,)), ((), ())), preferred_element_type=jnp.float32)


def pick_rows(index, count):
    spots = lax.broadcasted_iota(jnp.int32, (index.shape[0], count), 1)
    return (spots == index).astype(jnp.bfloat16)


def silu(x):
    return x * (0.5 * jnp.tanh(0.5 * x) + 0.5)


def layer_norm(values, gain):
    centred = values - jnp.mean(values, axis=-1, keepdims=True)
    row_var = jnp.mean(centred * centred, axis=-1, keepdims=True)
    return centred * lax.rsqrt(row_var + 1e-05) * gain


def along_lanes(pieces):
    return jnp.concatenate([pack[:, at:to] for pack, at, to in pieces], axis=1)


def mlp(x, groups, biases, gain):
    total = None
    for shards, bias in zip(groups, biases):
        w_in = jnp.concatenate([along_lanes(pieces) for pieces, _ in shards])
        w_out = jnp.concatenate([along_lanes(pieces) for _, pieces in shards])
        act = silu(dot_t(x, w_in) + bias).astype(jnp.bfloat16)
        part = dot(act, w_out)
        total = part if total is None else total + part
    return layer_norm(total, gain)


def take_groups(it, spots, cores):
    n_packs = 1 + max(pack for pieces in spots for pack, _, _ in pieces)
    groups = []
    for _ in range(cores // 2):
        shards = []
        for _ in range(2):
            refs = [next(it) for _ in range(n_packs)]
            shards.append([[(refs[pack], at, to) for pack, at, to in pieces] for pieces in spots])
        groups.append(shards)
    return groups


def loop(steps, body):
    lax.fori_loop(0, steps, body, 0, unroll=2 if steps % 2 == 0 else 1)


def call(kernel, out_shape, args, scratch=(), flops=0, nbytes=0, memory=None, out_memory=pltpu.VMEM, limit=VMEM_BYTES, name=None):
    in_specs = [pl.BlockSpec(memory_space=m) for m in memory or [pltpu.VMEM] * len(args)]
    out_specs = jax.tree.map(lambda _: pl.BlockSpec(memory_space=out_memory), out_shape)
    return pl.pallas_call(
        kernel,
        out_shape=out_shape,
        in_specs=in_specs,
        out_specs=out_specs,
        scratch_shapes=list(scratch),
        compiler_params=pltpu.CompilerParams(vmem_limit_bytes=limit),
        cost_estimate=pl.CostEstimate(flops=flops, bytes_accessed=nbytes, transcendentals=0),
        name=name,
    )(*args)


def bf16(*shape):
    return jax.ShapeDtypeStruct(shape, jnp.bfloat16)


def core_index():
    return lax.rem(lax.axis_index("feat"), 2)


def join_halves(out, own, other):
    core, nh = core_index(), own.shape[0]
    out[pl.ds(pl.multiple_of(core * nh, nh), nh), :] = own[...]
    out[pl.ds(pl.multiple_of((1 - core) * nh, nh), nh), :] = other[...]


def join_kernel(own, other, out, sems):
    core, nh = core_index(), own.shape[0]
    copies = []
    for i, (half, ref) in enumerate(((core, own), (1 - core, other))):
        spot = out.at[pl.ds(pl.multiple_of(half * nh, nh), nh), :]
        copies.append(pltpu.make_async_copy(ref, spot, sems.at[i]))
        copies[i].start()
    for copy in copies:
        copy.wait()


def add_kernel(own, arrived, out):
    out[...] = (own[...] + arrived[...].astype(jnp.float32)).astype(out.dtype)


def index_digits(ref, lanes):
    index = ref[...]
    high = lax.shift_right_logical(index, DIGIT.bit_length() - 1)
    rows = jnp.concatenate([high, index & (DIGIT - 1)]).astype(jnp.float32)
    if lanes == index.shape[1]:
        return rows
    return jnp.concatenate([rows, jnp.zeros((2, lanes - index.shape[1]), jnp.float32)], axis=1)


def to_column(ref):
    count = ref.shape[1]
    rows = jnp.concatenate([index_digits(ref, count), jnp.zeros((6, count), jnp.float32)])
    unit = lax.broadcasted_iota(jnp.int32, (count, count), 0)
    unit = unit == lax.broadcasted_iota(jnp.int32, (count, count), 1)
    digits = dot_t(unit.astype(jnp.bfloat16), rows.astype(jnp.bfloat16))
    return (DIGIT * digits[:, 0:1] + digits[:, 1:2]).astype(jnp.int32)


def halo_kernel(first, *refs):
    if first:
        nodes, halo, edges, send, recv, to_prev, to_next, *far, coarse, block = refs
        count, width = edges.shape
        block[0:count, :] = edges[...]
        digits = [index_digits(ref, width) for ref in (send, recv)]
        digits.append(jnp.zeros((16 - 4, width), jnp.float32))
        block[count : count + 16, :] = jnp.concatenate(digits).astype(jnp.bfloat16)
    else:
        own, other, halo, to_prev, to_next, *far, coarse, nodes = refs
        join_halves(nodes, own, other)
    core = core_index()
    count = nodes.shape[0]
    hr, cp = halo.shape[1] // 2, coarse.shape[0]
    hh, ch = hr // 2, cp // 2
    index = to_column(halo)
    mine = [jnp.where(core == 0, x[:hh], x[hh:]) for x in (index[:hr], index[hr:])]
    table = nodes[...]
    rows = dot(pick_rows(jnp.concatenate(mine), count), table).astype(jnp.bfloat16)
    every = STRIDE * lax.broadcasted_iota(jnp.int32, (cp, 1), 0)
    coarse[...] = dot(pick_rows(every, count), table).astype(jnp.bfloat16)
    mine = coarse[pl.ds(pl.multiple_of(core * ch, ch), ch), :]
    to_prev[pl.ds(0, hh), :] = rows[:hh]
    to_next[pl.ds(0, hh), :] = rows[hh:]
    for out, skip in [(to_prev, hh), (to_next, hh)] + [(ref, 0) for ref in far]:
        out[pl.ds(skip, ch), :] = mine
        if first:
            out[pl.ds(skip + ch, block.shape[0]), :] = block[...]


def prepare_kernel(plans, halves, cut, n_small, *refs):
    n_out = len(refs) - 4 - n_small - 1
    n_out = (n_out - n_small) // 2
    source, given, outs = refs[:4], refs[4 : 4 + n_small], refs[4 + n_small :][:n_out]
    refs = refs[4 + n_small + n_out :]
    small, made, sems = refs[:n_small], refs[n_small:-1], refs[-1]
    started = []

    def start(src, dst):
        copy = pltpu.make_async_copy(src, dst, sems.at[len(started)])
        copy.start()
        started.append(copy)
        return copy

    arriving = [start(src, dst) for src, dst in zip(given, small)]
    loads = []
    for plan, pack in zip(plans, made):
        parts = []
        for which, layer, at in plan:
            part = source[which].at[layer]
            spot = pack.at[:, at : at + part.shape[1]]
            parts.append(start(part, spot))
        loads.append(parts)
    for copy in arriving:
        copy.wait()
    edge_b1, node_b1, nodes, halo, edges, send, recv = small
    hidden = edge_b1.shape[1]
    rows = [edge_b1[...].astype(jnp.float32), node_b1[...].astype(jnp.float32)]
    rows.append(jnp.zeros((16 - 2 * STEPS, hidden), jnp.float32))
    at = made[0].shape[1] - LANES
    made[0][0:16, at : at + hidden] = jnp.concatenate(rows).astype(jnp.bfloat16)
    n_packs = len(plans)
    halo_kernel(True, nodes, halo, edges, send, recv, *made[n_packs:])
    stores = [start(src, dst) for src, dst in zip(made[n_packs:], outs[n_packs:])]
    group = lax.axis_index("groups")
    for i, parts in enumerate(loads):
        for copy in parts:
            copy.wait()
        if cut and i in halves:
            whole = made[halves[i]]
            made[i][:, :cut] = jnp.where(group == 0, whole[:, :cut], whole[:, cut:])
        stores.append(start(made[i], outs[i]))
    for copy in stores:
        copy.wait()


def part_kernel(pack, out):
    out[...] = pack[:, : out.shape[1]]


def gather_kernel(tile, nodes, send, recv, *refs):
    carried, (sent, received) = refs[: len(refs) - 2], refs[len(refs) - 2 :]
    count = nodes.shape[0]
    if carried:
        carried[1][...] = carried[0][...]

    def body(t, carry):
        rows = pl.ds(pl.multiple_of(t * tile, tile), tile)
        table = nodes[...]
        sent[rows, :] = dot(pick_rows(send[rows, :], count), table).astype(jnp.bfloat16)
        safe = jnp.minimum(recv[rows, :], count - 1)
        received[rows, :] = dot(pick_rows(safe, count), table).astype(jnp.bfloat16)
        return carry

    loop(send.shape[0] // tile, body)


def bias_rows_of(bias_ref, line, n_groups):
    per = bias_ref.shape[1] // n_groups
    return [bias_ref[line : line + 1, g * per : (g + 1) * per] for g in range(n_groups)]


def half_sums(out, half, nh, new_fine, recv_row):
    sum_rows(out, 0, [place_in_half((nh, recv_row[...] - half * nh))], [new_fine[...]])


def own_sums_kernel(nh, new_fine, recv_row, out):
    half_sums(out, core_index(), nh, new_fine, recv_row)


def fine_kernel(tile, sizes, spots, layer, *refs):
    count, hr, cp, parts, cores = sizes
    it = iter(refs)
    fine, sent, received, send, recv_row, gain_ref = (next(it) for _ in range(6))
    prev, nxt = ((next(it), next(it)) for _ in range(2))
    groups = take_groups(it, spots, cores)
    bias_in = None if layer == 0 else next(it)
    new_fine = next(it)
    bias_out = next(it) if layer == 0 else None
    agg_other, halo_tab = it

    core = core_index()
    width = gain_ref.shape[-1]
    hh = hr // 2
    for side, pair in ((0, prev), (hr, nxt)):
        for who, ref in zip((core, 1 - core), pair):
            halo_tab[pl.ds(pl.multiple_of(side + who * hh, hh), hh), :] = ref[pl.ds(0, hh), :]

    if layer == 0:
        spot = 0
        for shards in groups:
            for _, [(pack, _, at)] in shards:
                hidden = pack.shape[0]
                rows = pack[0:16, at : at + hidden].astype(jnp.float32)
                bias_out[:, spot : spot + hidden] = rows[:8]
                spot += hidden
    biases = bias_rows_of(bias_out if layer == 0 else bias_in, layer, len(groups))
    gain = gain_ref[layer : layer + 1, :].astype(jnp.float32)

    def body(t, carry):
        rows = pl.ds(pl.multiple_of(t * tile, tile), tile)
        border = dot(pick_rows(send[rows, :] - count, 2 * hr), halo_tab[...])
        senders = (sent[rows, :].astype(jnp.float32) + border).astype(jnp.bfloat16)
        old = fine[rows, :]
        x = jnp.concatenate([old, senders, received[rows, :]], axis=1)
        y = mlp(x, groups, biases, gain)
        new_fine[rows, :] = (old.astype(jnp.float32) + y).astype(jnp.bfloat16)
        return carry

    loop(fine.shape[0] // tile, body)
    half_sums(agg_other, 1 - core, count // 2, new_fine, recv_row)


def coarse_target(state, width, me, cp):
    lane = lax.broadcasted_iota(jnp.int32, (8, LANES), 1)
    weights = jnp.where(lane == 2, float(DIGIT), jnp.where(lane == 3, 1.0, 0.0)).astype(jnp.bfloat16)
    near = dot_t(weights, state[:, width : width + LANES])[:1, :].astype(jnp.int32) - me * cp
    return jnp.where((near >= 0) & (near < cp), near * STRIDE, -1)


def place_in_half(row):
    count, row = row
    group, rest = lax.shift_right_logical(row, 3), row & (STRIDE - 1)
    fine_rows = count - count // STRIDE
    place = jnp.where(rest == 0, fine_rows + group, (STRIDE - 1) * group + rest - 1)
    return jnp.where((row >= 0) & (row < count), place, -1)


def sum_rows(out, first, places, latents):
    total = None
    for place, latent in zip(places, latents):
        rows = lax.broadcasted_iota(jnp.int32, (out.shape[0], place.shape[1]), 0) + first
        part = dot((rows == place).astype(jnp.bfloat16), latent)
        total = part if total is None else total + part
    out[...] = total.astype(out.dtype)


def coarse_kernel(tile, sizes, spots, layer, *refs):
    count, hr, cp, parts, cores = sizes
    it = iter(refs)
    new_fine, recv_row, coarse_own, gain_ref, bias_ref = (next(it) for _ in range(5))
    given = next(it)
    arrived = [(next(it), next(it)) for _ in range(parts - 1)]
    groups = take_groups(it, spots, cores)
    state, *aggs, coarse_tab = it

    core, me = core_index(), lax.axis_index("mesh")
    width = gain_ref.shape[-1]
    hh, ch, nh = hr // 2, cp // 2, count // 2

    coarse_tab[pl.ds(pl.multiple_of(me * cp, cp), cp), :] = coarse_own[...]
    for i, pair in enumerate(arrived):
        owner = lax.rem(me + parts - 1 - i, parts)
        skip = hh if i in (0, parts - 2) or parts == RELAYED else 0
        for who, ref in zip((core, 1 - core), pair):
            spot = pl.multiple_of(owner * cp + who * ch, ch)
            coarse_tab[pl.ds(spot, ch), :] = ref[pl.ds(skip, ch), 0:width]
    if layer == 0:
        per = given.shape[0] - 16
        lane = lax.broadcasted_iota(jnp.int32, (per, width), 1)
        unit = (lane == lax.broadcasted_iota(jnp.int32, (per, width), 0)).astype(jnp.bfloat16)
        blocks = [(given, 0)]
        for i, (ref, _) in enumerate(arrived):
            near = i in (0, parts - 2) or parts == RELAYED
            blocks.append((ref, ch + (hh if near else 0)))
        for i, (ref, skip) in enumerate(blocks):
            rows = pl.ds(i * per, per)
            state[rows, :width] = ref[pl.ds(skip, per), :]
            digits = ref[pl.ds(skip + per, 16), :].astype(jnp.float32)
            digits = jnp.concatenate([digits, jnp.zeros((LANES - 16, width), jnp.float32)])
            state[rows, width:] = dot_t(unit, digits.astype(jnp.bfloat16)).astype(jnp.bfloat16)
    else:
        state[...] = given[...]

    biases = bias_rows_of(bias_ref, layer, len(groups))
    gain = gain_ref[layer : layer + 1, :].astype(jnp.float32)

    def body(t, carry):
        rows = pl.ds(pl.multiple_of(t * tile, tile), tile)
        old = state[rows, :width]
        digits = state[rows, width : width + LANES].astype(jnp.float32)
        ends = []
        for j in range(2):
            index = DIGIT * digits[:, 2 * j : 2 * j + 1] + digits[:, 2 * j + 1 : 2 * j + 2]
            picked = pick_rows(index.astype(jnp.int32), coarse_tab.shape[0])
            ends.append(dot(picked, coarse_tab[...]).astype(jnp.bfloat16))
        y = mlp(jnp.concatenate([old] + ends, axis=1), groups, biases, gain)
        state[rows, :width] = (old.astype(jnp.float32) + y).astype(jnp.bfloat16)
        return carry

    loop(state.shape[0] // tile, body)
    target = coarse_target(state, width, me, cp)
    latents = [new_fine[...], state[:, :width]]
    for out, half in zip(aggs, (1 - core, core)):
        places = [place_in_half((nh, at - half * nh)) for at in (recv_row[...], target)]
        sum_rows(out, nh - ch, places, latents)


def node_kernel(tile, layer, cores, spots, n_sums, cut, *refs):
    it = iter(refs)
    nodes, bias_ref, gain_ref = (next(it) for _ in range(3))
    sums = [[next(it) for _ in range(n)] for n in n_sums]
    if cut:
        groups = take_groups(it, spots, 2)
        parts = [(next(it), next(it)) for _ in range(2)]
    else:
        groups = take_groups(it, spots, cores)
    out, agg_ref, *far = it
    if cut:
        group = lax.axis_index("groups")
        for ref, (mine, other) in zip(far, parts):
            ref[:, pl.ds(pl.multiple_of(group * cut, LANES), cut)] = mine[:, :cut]
            ref[:, pl.ds(pl.multiple_of((1 - group) * cut, LANES), cut)] = other[...]
        groups.append([[[(ref, at, to) for _, at, to in pieces] for pieces in spots] for ref in far])
    nh = out.shape[0]
    agg = []
    for terms in sums:
        total = terms[0][...].astype(jnp.float32)
        for more in terms[1:]:
            total = total + more[...].astype(jnp.float32)
        agg.append(total.astype(jnp.bfloat16))
    if len(agg) > 1:
        row = lax.broadcasted_iota(jnp.int32, (nh, 1), 0)
        order = pick_rows(place_in_half((nh, row)), nh)
        agg = [dot(order, jnp.concatenate(agg)).astype(jnp.bfloat16)]
    agg_ref[...] = agg[0]
    biases = bias_rows_of(bias_ref, STEPS + layer, len(groups))
    gain = gain_ref[layer : layer + 1, :].astype(jnp.float32)
    core = core_index()
    half = nodes.shape[0] // 2
    for t in range(nh // tile):
        rows = pl.ds(t * tile, tile)
        old = nodes[pl.ds(pl.multiple_of(core * half + t * tile, tile), tile), :]
        x = jnp.concatenate([old, agg_ref[rows, :]], axis=1)
        y = mlp(x, groups, biases, gain)
        out[rows, :] = (old.astype(jnp.float32) + y).astype(jnp.bfloat16)


def divisor(count, most, unit=16):
    best = unit
    for size in range(unit, min(most, count) + 1, unit):
        if count % size == 0:
            best = size
    return best


def local(
    nodes,
    fine_edges,
    fine_send,
    fine_recv,
    halo_send,
    coarse_edges,
    coarse_send,
    coarse_recv,
    edge_w1,
    edge_b1,
    edge_w2,
    edge_gain,
    node_w1,
    node_b1,
    node_w2,
    node_gain,
):
    count, width = nodes.shape
    hr = halo_send.shape[0] // 2
    cp = count // STRIDE
    nh = count // 2
    fine_count = fine_edges.shape[0]
    parts = lax.axis_size("mesh")
    cores = lax.axis_size("feat")
    core = core_index()

    def swap(x):
        return lax.ppermute(x, "feat", [(i, i ^ 1) for i in range(cores)])

    def across(x):
        return lax.ppermute(x, "feat", [(i, i ^ 2) for i in range(cores)])

    def shift(x, by):
        return lax.ppermute(x, "mesh", [(i, (i + by) % parts) for i in range(parts)])

    def both(x):
        return [x, swap(x)]

    def after(xs):
        return lax.optimization_barrier(tuple(xs))

    two = cores == 4

    def spread(pack):
        return across(pack) if two else lax.all_gather(pack, "feat", axis=0)

    def shards(pack, far):
        if two:
            return both(pack) + both(far)
        return [far[i] for i in range(cores)]

    k, kn = edge_w1.shape[2], node_w1.shape[2]
    w_hidden = edge_w1.shape[1]
    halo_row = halo_send.reshape(1, 2 * hr)
    own_coarse = coarse_edges.shape[0]
    coarse_count = own_coarse * parts
    lanes = kn + width
    cut = lanes // 2 if two and lax.axis_size("groups") == 2 else 0
    plans = [
        [(0, 0, 0), (1, 0, k)],
        [(2, 0, 0), (3, 0, kn)],
        [(2, 1, 0), (3, 1, kn)],
        [(1, 1, cut)],
        [(0, 1, 0)],
    ] + ([[]] if cut else [])
    halves = {3: 1, 5: 2}
    block = own_coarse + 16
    near, far = hr // 2 + cp // 2 + block, cp // 2 + block
    widths = [k + width + LANES, lanes, lanes, cut + width, k] + ([cut] if cut else [])
    shapes = [(w_hidden, n) for n in widths]
    direct = parts != RELAYED
    shapes += [(near, width), (near, width)] + [(far, width)] * direct
    shapes += [(cp, width), (block, width)]
    small = [edge_b1, node_b1, nodes, halo_row, coarse_edges]
    small += [x.reshape(1, own_coarse) for x in (coarse_send, coarse_recv)]
    n_copies = len(small) + sum(len(p) for p in plans) + len(shapes)
    made = call(
        functools.partial(prepare_kernel, plans, halves, cut, len(small)),
        tuple(bf16(*shape) for shape in shapes),
        [edge_w1, edge_w2, node_w1, node_w2, *small],
        scratch=[pltpu.VMEM(x.shape, x.dtype) for x in small]
        + [pltpu.VMEM(shape, jnp.bfloat16) for shape in shapes]
        + [pltpu.SemaphoreType.DMA((n_copies,))],
        memory=[pl.ANY] * (4 + len(small)),
        out_memory=pl.ANY,
        limit=3 * VMEM_BYTES,
        name="weights_and_halo_rows",
    )
    first_pack, node0, node1, mixed, edge1, *node1_half = made[: len(widths)]
    *rows_out, coarse_own, block = made[len(widths) :]
    node_spots = (((0, 0, kn),), ((0, kn, lanes),))

    send_col = fine_send.reshape(fine_count, 1)
    recv_col = fine_recv.reshape(fine_count, 1)
    recv_row = fine_recv.reshape(1, fine_count)
    tile = divisor(fine_count, 768)
    ctile = divisor(coarse_count, 384)
    hidden = w_hidden * cores
    sizes = (count, hr, cp, parts, cores)
    bias_rows = None

    def node_rows_out(own, other):
        near, far = bf16(hr // 2 + cp // 2, width), bf16(cp // 2, width)
        return call(
            functools.partial(halo_kernel, False),
            (near, near, *[far] * direct, bf16(cp, width), bf16(count, width)),
            [own, other, halo_row],
            name="halo_rows",
        )

    def exchange(to_prev, to_next, *to_far):
        between = [shift(to_far[0], by) for by in range(2, parts - 1)] if to_far else []
        return [shift(to_next, 1), *between, shift(to_prev, parts - 1)]

    def far_rows(moved):
        return [shift(moved[0], 1)] if parts == RELAYED else moved[1:-1]

    def gather(nodes, *carried):
        return call(
            functools.partial(gather_kernel, tile),
            (*(bf16(*x.shape) for x in carried), bf16(fine_count, width), bf16(fine_count, width)),
            [nodes, send_col, recv_col, *carried],
            flops=4 * fine_count * count * width,
            name="gather_rows",
        )

    def fine_update(s, fine, sent, received, halo, weights, spots):
        outs = [bf16(fine_count, width)]
        if s == 0:
            outs.append(jax.ShapeDtypeStruct((8, hidden), jnp.float32))
        fine_rows = nh - cp // 2
        outs.append(bf16(fine_rows, width))
        return call(
            functools.partial(fine_kernel, tile, sizes, spots, s),
            tuple(outs),
            [fine, sent, received, send_col, recv_row, edge_gain] + halo + weights + ([bias_rows] if s else []),
            scratch=[pltpu.VMEM((2 * hr, width), jnp.bfloat16)],
            flops=8 * fine_count * width * hidden,
            name="fine_edges",
        )

    def own_sums(new_fine):
        return call(
            functools.partial(own_sums_kernel, nh),
            jax.ShapeDtypeStruct((nh - cp // 2, width), jnp.float32),
            [new_fine, recv_row],
            name="own_sums",
        )

    def coarse_update(s, new_fine, coarse_own, state, arrived, weights, spots):
        aggs = [bf16(cp // 2, width), jax.ShapeDtypeStruct((cp // 2, width), jnp.float32)]
        return call(
            functools.partial(coarse_kernel, ctile, sizes, spots, s),
            (bf16(coarse_count, width + LANES), *aggs),
            [new_fine, recv_row, coarse_own, edge_gain, bias_rows, state] + arrived + weights,
            scratch=[pltpu.VMEM((parts * cp, width), jnp.bfloat16)],
            flops=COARSE_FLOPS[s],
            name="coarse_edges_and_sums",
        )

    def node_update(s, nodes, sums, weights, spots, cut=0):
        far = [pltpu.VMEM((w_hidden, 2 * cut), jnp.bfloat16)] * 2 if cut else []
        rows = sum(part[0].shape[0] for part in sums)
        return both(
            call(
                functools.partial(node_kernel, rows, s, cores, spots, [len(part) for part in sums], cut),
                bf16(rows, width),
                [nodes, bias_rows, node_gain] + [x for part in sums for x in part] + weights,
                scratch=[pltpu.VMEM((rows, width), jnp.bfloat16), *far],
                name="node_update",
            )
        )

    def core_sum(agg_own, agg_other):
        return call(add_kernel, bf16(*agg_own.shape), [agg_own, swap(agg_other)], name="core_sum")

    def chip_sums(partial):
        if two:
            return [partial, across(partial)]
        every = lax.all_gather(partial, "feat", axis=0)
        every = every.reshape(cores // 2, 2, *partial.shape).astype(jnp.float32)
        return [lax.dynamic_index_in_dim(every.sum(axis=0), core, 0, keepdims=False)]

    def halo_of(moved, swapped):
        return [moved[0], swapped[0], moved[-1], swapped[-1]]

    def pairs(moved, swapped):
        return [x for pair in zip(moved, swapped) for x in pair]

    def other_group(x):
        return lax.ppermute(x, "groups", [(0, 1), (1, 0)])

    far_first = spread(first_pack)
    moved = exchange(*rows_out)
    send_col, recv_col, recv_row = after((send_col, recv_col, recv_row))
    if two:
        near, sent, received = gather(nodes, swap(first_pack))
    else:
        sent, received = gather(nodes)
    moved[0], moved[-1], far_first, sent = after((moved[0], moved[-1], far_first, sent))
    relayed = far_rows(moved)
    swapped = {i: swap(moved[i]) for i in (0, -1)}
    weights = [first_pack, near, *both(far_first)] if two else shards(first_pack, far_first)
    spots = (((0, 0, k),), ((0, k, k + width),))
    far = spread(mixed)
    fine_edges, bias_rows, other = fine_update(
        0, fine_edges, sent, received, halo_of(moved, swapped), weights, spots
    )
    other, far, *relayed = after((other, far, *relayed))
    swapped = [swapped[0], *(swap(m) for m in relayed), swapped[-1]]
    moved = [moved[0], *relayed, moved[-1]]
    partial = core_sum(own_sums(fine_edges), other)
    mixed = shards(mixed, far)
    fine_part = chip_sums(partial)
    state, other, own = coarse_update(
        0, fine_edges, coarse_own, block, pairs(moved, swapped), weights, spots
    )
    if cut:
        others = other_group(call(part_kernel, bf16(w_hidden, cut), [far], name="part"))
        own, others = after((own, others))
        weights = both(node0) + pairs(mixed[2:], both(others))
    else:
        weights = shards(node0, spread(node0))
    sums = [fine_part, chip_sums(core_sum(own, other))]
    sums[1][-1], edge1 = after((sums[1][-1], edge1))
    far = spread(edge1)
    halves = node_update(0, nodes, sums, weights, node_spots, cut)

    *rows_out, coarse_own, nodes = node_rows_out(*halves)
    moved = exchange(*rows_out)
    sent, received = gather(nodes)
    *moved, far, sent = after((*moved, far, sent))
    weights = pairs(shards(edge1, far), mixed)
    spots = (((0, 0, k),), ((1, cut, cut + width),))
    relayed = far_rows(moved)
    swapped = {i: swap(moved[i]) for i in (0, -1)}
    far = across(node1_half[0]) if cut else spread(node1)
    fine_edges, other = fine_update(
        1, fine_edges, sent, received, halo_of(moved, swapped), weights, spots
    )
    other, far, *relayed = after((other, far, *relayed))
    swapped = [swapped[0], *(swap(m) for m in relayed), swapped[-1]]
    moved = [moved[0], *relayed, moved[-1]]
    partial = core_sum(own_sums(fine_edges), other)
    fine_part = chip_sums(partial)
    state, other, own = coarse_update(
        1, fine_edges, coarse_own, state, pairs(moved, swapped), weights, spots
    )
    if cut:
        others = other_group(far)
        own, others = after((own, others))
        weights = both(node1) + pairs(both(far), both(others))
    else:
        weights = shards(node1, far)
    sums = [fine_part, chip_sums(core_sum(own, other))]
    halves = node_update(1, nodes, sums, weights, node_spots, cut)
    return call(
        join_kernel,
        bf16(count, width),
        halves,
        scratch=[pltpu.SemaphoreType.DMA((2,))],
        out_memory=pl.ANY,
        name="nodes_out",
    )


def solution(mesh):
    placed = (
        P(("groups", "mesh"), None),
        P(("groups", "mesh", "feat"), None),
        P(("groups", "mesh", "feat")),
        P(("groups", "mesh", "feat")),
        P(("groups", "mesh")),
        P(("groups", "mesh", "feat"), None),
        P(("groups", "mesh", "feat")),
        P(("groups", "mesh", "feat")),
        P(None, "feat", None),
        P(None, "feat"),
        P(None, "feat", None),
        P(),
        P(None, "feat", None),
        P(None, "feat"),
        P(None, "feat", None),
        P(),
    )
    return jax.shard_map(
        local, mesh=mesh, in_specs=placed, out_specs=P(("groups", "mesh"), None), check_vma=False
    )
```

```python
import functools

import jax
import jax.numpy as jnp
from jax import lax
from jax.experimental import pallas as pl
from jax.experimental.pallas import tpu as pltpu
from jax.sharding import PartitionSpec as P

STEPS = 2
STRIDE = 8
LANES = 128
COARSE_FLOPS = (0, 0)
RELAYED = 4
DIGIT = 64
VMEM_BYTES = 20 * 1024 * 1024


def dot(a, b):
    return jnp.dot(a, b, preferred_element_type=jnp.float32)


def dot_t(a, b):
    return lax.dot_general(a, b, (((1,), (1,)), ((), ())), preferred_element_type=jnp.float32)


def pick_rows(index, count):
    spots = lax.broadcasted_iota(jnp.int32, (index.shape[0], count), 1)
    return (spots == index).astype(jnp.bfloat16)


def silu(x):
    return x * (0.5 * jnp.tanh(0.5 * x) + 0.5)


def layer_norm(values, gain):
    centred = values - jnp.mean(values, axis=-1, keepdims=True)
    row_var = jnp.mean(centred * centred, axis=-1, keepdims=True)
    return centred * lax.rsqrt(row_var + 1e-05) * gain


def along_lanes(pieces):
    return jnp.concatenate([pack[:, at:to] for pack, at, to in pieces], axis=1)


def mlp(x, groups, biases, gain):
    total = None
    for shards, bias in zip(groups, biases):
        w_in = jnp.concatenate([along_lanes(pieces) for pieces, _ in shards])
        w_out = jnp.concatenate([along_lanes(pieces) for _, pieces in shards])
        act = silu(dot_t(x, w_in) + bias).astype(jnp.bfloat16)
        part = dot(act, w_out)
        total = part if total is None else total + part
    return layer_norm(total, gain)


def take_groups(it, spots, cores):
    n_packs = 1 + max(pack for pieces in spots for pack, _, _ in pieces)
    groups = []
    for _ in range(cores // 2):
        shards = []
        for _ in range(2):
            refs = [next(it) for _ in range(n_packs)]
            shards.append([[(refs[pack], at, to) for pack, at, to in pieces] for pieces in spots])
        groups.append(shards)
    return groups


def loop(steps, body):
    lax.fori_loop(0, steps, body, 0, unroll=2 if steps % 2 == 0 else 1)


def call(kernel, out_shape, args, scratch=(), flops=0, nbytes=0, memory=None, out_memory=pltpu.VMEM, limit=VMEM_BYTES, name=None):
    in_specs = [pl.BlockSpec(memory_space=m) for m in memory or [pltpu.VMEM] * len(args)]
    out_specs = jax.tree.map(lambda _: pl.BlockSpec(memory_space=out_memory), out_shape)
    return pl.pallas_call(
        kernel,
        out_shape=out_shape,
        in_specs=in_specs,
        out_specs=out_specs,
        scratch_shapes=list(scratch),
        compiler_params=pltpu.CompilerParams(vmem_limit_bytes=limit),
        cost_estimate=pl.CostEstimate(flops=flops, bytes_accessed=nbytes, transcendentals=0),
        name=name,
    )(*args)


def bf16(*shape):
    return jax.ShapeDtypeStruct(shape, jnp.bfloat16)


def core_index():
    return lax.rem(lax.axis_index("feat"), 2)


def join_halves(out, own, other):
    core, nh = core_index(), own.shape[0]
    out[pl.ds(pl.multiple_of(core * nh, nh), nh), :] = own[...]
    out[pl.ds(pl.multiple_of((1 - core) * nh, nh), nh), :] = other[...]


def join_kernel(own, other, out, sems):
    core, nh = core_index(), own.shape[0]
    copies = []
    for i, (half, ref) in enumerate(((core, own), (1 - core, other))):
        spot = out.at[pl.ds(pl.multiple_of(half * nh, nh), nh), :]
        copies.append(pltpu.make_async_copy(ref, spot, sems.at[i]))
        copies[i].start()
    for copy in copies:
        copy.wait()


def add_kernel(own, arrived, out):
    out[...] = (own[...] + arrived[...].astype(jnp.float32)).astype(out.dtype)


def index_digits(ref, lanes):
    index = ref[...]
    high = lax.shift_right_logical(index, DIGIT.bit_length() - 1)
    rows = jnp.concatenate([high, index & (DIGIT - 1)]).astype(jnp.float32)
    if lanes == index.shape[1]:
        return rows
    return jnp.concatenate([rows, jnp.zeros((2, lanes - index.shape[1]), jnp.float32)], axis=1)


def to_column(ref):
    count = ref.shape[1]
    rows = jnp.concatenate([index_digits(ref, count), jnp.zeros((6, count), jnp.float32)])
    unit = lax.broadcasted_iota(jnp.int32, (count, count), 0)
    unit = unit == lax.broadcasted_iota(jnp.int32, (count, count), 1)
    digits = dot_t(unit.astype(jnp.bfloat16), rows.astype(jnp.bfloat16))
    return (DIGIT * digits[:, 0:1] + digits[:, 1:2]).astype(jnp.int32)


def halo_kernel(first, *refs):
    if first:
        nodes, halo, edges, send, recv, to_prev, to_next, *far, coarse, block = refs
        count, width = edges.shape
        block[0:count, :] = edges[...]
        digits = [index_digits(ref, width) for ref in (send, recv)]
        digits.append(jnp.zeros((16 - 4, width), jnp.float32))
        block[count : count + 16, :] = jnp.concatenate(digits).astype(jnp.bfloat16)
    else:
        own, other, halo, to_prev, to_next, *far, coarse, nodes = refs
        join_halves(nodes, own, other)
    core = core_index()
    count = nodes.shape[0]
    hr, cp = halo.shape[1] // 2, coarse.shape[0]
    hh, ch = hr // 2, cp // 2
    index = to_column(halo)
    mine = [jnp.where(core == 0, x[:hh], x[hh:]) for x in (index[:hr], index[hr:])]
    table = nodes[...]
    rows = dot(pick_rows(jnp.concatenate(mine), count), table).astype(jnp.bfloat16)
    every = STRIDE * lax.broadcasted_iota(jnp.int32, (cp, 1), 0)
    coarse[...] = dot(pick_rows(every, count), table).astype(jnp.bfloat16)
    mine = coarse[pl.ds(pl.multiple_of(core * ch, ch), ch), :]
    to_prev[pl.ds(0, hh), :] = rows[:hh]
    to_next[pl.ds(0, hh), :] = rows[hh:]
    for out, skip in [(to_prev, hh), (to_next, hh)] + [(ref, 0) for ref in far]:
        out[pl.ds(skip, ch), :] = mine
        if first:
            out[pl.ds(skip + ch, block.shape[0]), :] = block[...]


class Copies:
    def __init__(self, sems):
        self.sems, self.started = sems, []

    def start(self, src, dst):
        copy = pltpu.make_async_copy(src, dst, self.sems.at[len(self.started)])
        copy.start()
        self.started.append(copy)
        return copy


def first_kernel(n_in, n_out, *refs):
    edge_w1, edge_w2, *given = refs[:n_in]
    outs = refs[n_in : n_in + n_out]
    small, made, sems = refs[n_in + n_out :][: len(given)], refs[-1 - n_out : -1], refs[-1]
    copies = Copies(sems)
    arriving = [copies.start(src, dst) for src, dst in zip(given, small)]
    pack, k = made[0], edge_w1.shape[2]
    loads = [
        copies.start(edge_w1.at[0], pack.at[:, 0:k]),
        copies.start(edge_w2.at[0], pack.at[:, k : k + edge_w2.shape[2]]),
    ]
    for copy in arriving:
        copy.wait()
    edge_b1, node_b1, nodes, halo, edges, send, recv = small
    hidden = edge_b1.shape[1]
    rows = [edge_b1[...].astype(jnp.float32), node_b1[...].astype(jnp.float32)]
    rows.append(jnp.zeros((16 - 2 * STEPS, hidden), jnp.float32))
    at = pack.shape[1] - LANES
    pack[0:16, at : at + hidden] = jnp.concatenate(rows).astype(jnp.bfloat16)
    halo_kernel(True, nodes, halo, edges, send, recv, *made[1:])
    for copy in loads:
        copy.wait()
    for copy in [copies.start(src, dst) for src, dst in zip(made, outs)]:
        copy.wait()


def later_kernel(plans, halves, *refs):
    source, outs, made, sems = refs[:4], refs[4 : 4 + len(plans)], refs[4 + len(plans) : -1], refs[-1]
    copies = Copies(sems)
    loads = []
    for plan, pack in zip(plans, made):
        parts = []
        for which, layer, at in plan:
            part = source[which].at[layer]
            parts.append(copies.start(part, pack.at[:, at : at + part.shape[1]]))
        loads.append(parts)
    group = lax.axis_index("groups")
    stores = []
    for i, parts in enumerate(loads):
        for copy in parts:
            copy.wait()
        for which, at in halves.get(i, ()):
            whole = made[which]
            lanes = whole.shape[1] // 2
            part = jnp.where(group == 0, whole[:, :lanes], whole[:, lanes:])
            made[i][:, at : at + lanes] = part
        stores.append(copies.start(made[i], outs[i]))
    for copy in stores:
        copy.wait()


def parts_kernel(pack, first, last):
    first[...] = pack[:, : first.shape[1]]
    last[...] = pack[:, first.shape[1] :]


def tail_kernel(rows, out):
    out[...] = rows[pl.ds(rows.shape[0] - out.shape[0], out.shape[0]), :]


def gather_kernel(tile, nodes, send, recv, *refs):
    carried, (sent, received) = refs[: len(refs) - 2], refs[len(refs) - 2 :]
    count = nodes.shape[0]
    if carried:
        carried[1][...] = carried[0][...]

    def body(t, carry):
        rows = pl.ds(pl.multiple_of(t * tile, tile), tile)
        table = nodes[...]
        sent[rows, :] = dot(pick_rows(send[rows, :], count), table).astype(jnp.bfloat16)
        safe = jnp.minimum(recv[rows, :], count - 1)
        received[rows, :] = dot(pick_rows(safe, count), table).astype(jnp.bfloat16)
        return carry

    loop(send.shape[0] // tile, body)


def bias_rows_of(bias_ref, line, n_groups):
    per = bias_ref.shape[1] // n_groups
    return [bias_ref[line : line + 1, g * per : (g + 1) * per] for g in range(n_groups)]


def far_weights(halved, k, w_in, parts, w_out):
    lanes = halved
    group = lax.axis_index("groups")
    for ref, pair in zip(w_out, parts):
        for who, part in zip((group, 1 - group), pair):
            spot = pl.ds(pl.multiple_of(who * lanes, LANES), lanes)
            ref[:, spot] = part[:, part.shape[1] - lanes :]
    return [[[(w, 0, k)], [(ref, 0, ref.shape[1])]] for w, ref in zip(w_in, w_out)]


def half_sums(out, half, nh, new_fine, recv_row):
    sum_rows(out, 0, [place_in_half((nh, recv_row[...] - half * nh))], [new_fine[...]])


def own_sums_kernel(nh, new_fine, recv_row, out):
    half_sums(out, core_index(), nh, new_fine, recv_row)


def fine_kernel(tile, sizes, spots, layer, halved, *refs):
    count, hr, cp, parts, cores = sizes
    it = iter(refs)
    fine, sent, received, send, recv_row, gain_ref = (next(it) for _ in range(6))
    prev, nxt = ((next(it), next(it)) for _ in range(2))
    groups = take_groups(it, spots, 2 if halved else cores)
    far_in = [next(it) for _ in range(2 if halved else 0)]
    parts = [(next(it), next(it)) for _ in far_in]
    bias_in = None if layer == 0 else next(it)
    new_fine = next(it)
    bias_out = next(it) if layer == 0 else None
    agg_other, halo_tab, *far_out = it

    core = core_index()
    width = gain_ref.shape[-1]
    hh = hr // 2
    for side, pair in ((0, prev), (hr, nxt)):
        for who, ref in zip((core, 1 - core), pair):
            halo_tab[pl.ds(pl.multiple_of(side + who * hh, hh), hh), :] = ref[pl.ds(0, hh), :]

    if layer == 0:
        spot = 0
        for shards in groups:
            for _, [(pack, _, at)] in shards:
                hidden = pack.shape[0]
                rows = pack[0:16, at : at + hidden].astype(jnp.float32)
                bias_out[:, spot : spot + hidden] = rows[:8]
                spot += hidden
    if halved:
        groups.append(far_weights(halved, 3 * width, far_in, parts, far_out))
    biases = bias_rows_of(bias_out if layer == 0 else bias_in, layer, len(groups))
    gain = gain_ref[layer : layer + 1, :].astype(jnp.float32)

    def body(t, carry):
        rows = pl.ds(pl.multiple_of(t * tile, tile), tile)
        border = dot(pick_rows(send[rows, :] - count, 2 * hr), halo_tab[...])
        senders = (sent[rows, :].astype(jnp.float32) + border).astype(jnp.bfloat16)
        old = fine[rows, :]
        x = jnp.concatenate([old, senders, received[rows, :]], axis=1)
        y = mlp(x, groups, biases, gain)
        new_fine[rows, :] = (old.astype(jnp.float32) + y).astype(jnp.bfloat16)
        return carry

    loop(fine.shape[0] // tile, body)
    half_sums(agg_other, 1 - core, count // 2, new_fine, recv_row)


def coarse_target(state, width, me, cp):
    lane = lax.broadcasted_iota(jnp.int32, (8, LANES), 1)
    weights = jnp.where(lane == 2, float(DIGIT), jnp.where(lane == 3, 1.0, 0.0)).astype(jnp.bfloat16)
    near = dot_t(weights, state[:, width : width + LANES])[:1, :].astype(jnp.int32) - me * cp
    return jnp.where((near >= 0) & (near < cp), near * STRIDE, -1)


def place_in_half(row):
    count, row = row
    group, rest = lax.shift_right_logical(row, 3), row & (STRIDE - 1)
    fine_rows = count - count // STRIDE
    place = jnp.where(rest == 0, fine_rows + group, (STRIDE - 1) * group + rest - 1)
    return jnp.where((row >= 0) & (row < count), place, -1)


def sum_rows(out, first, places, latents):
    total = None
    for place, latent in zip(places, latents):
        rows = lax.broadcasted_iota(jnp.int32, (out.shape[0], place.shape[1]), 0) + first
        part = dot((rows == place).astype(jnp.bfloat16), latent)
        total = part if total is None else total + part
    out[...] = total.astype(out.dtype)


def coarse_kernel(tile, sizes, spots, layer, halved, *refs):
    count, hr, cp, parts, cores = sizes
    it = iter(refs)
    new_fine, recv_row, coarse_own, gain_ref, bias_ref = (next(it) for _ in range(5))
    given = next(it)
    arrived = [(next(it), next(it)) for _ in range(parts - 1)]
    groups = take_groups(it, spots, 2 if halved else cores)
    far_in = [next(it) for _ in range(2 if halved else 0)]
    halves = [(next(it), next(it)) for _ in far_in]
    state, *aggs = (next(it) for _ in range(3))
    coarse_tab, *far_out = it

    core, me = core_index(), lax.axis_index("mesh")
    width = gain_ref.shape[-1]
    hh, ch, nh = hr // 2, cp // 2, count // 2
    if halved:
        groups.append(far_weights(halved, 3 * width, far_in, halves, far_out))

    coarse_tab[pl.ds(pl.multiple_of(me * cp, cp), cp), :] = coarse_own[...]
    for i, pair in enumerate(arrived):
        owner = lax.rem(me + parts - 1 - i, parts)
        skip = hh if i in (0, parts - 2) else 0
        for who, ref in zip((core, 1 - core), pair):
            spot = pl.multiple_of(owner * cp + who * ch, ch)
            coarse_tab[pl.ds(spot, ch), :] = ref[pl.ds(skip, ch), 0:width]
    if layer == 0:
        per = given.shape[0] - 16
        lane = lax.broadcasted_iota(jnp.int32, (per, width), 1)
        unit = (lane == lax.broadcasted_iota(jnp.int32, (per, width), 0)).astype(jnp.bfloat16)
        blocks = [(given, 0)]
        for i, (ref, _) in enumerate(arrived):
            blocks.append((ref, ch + (hh if i in (0, parts - 2) else 0)))
        for i, (ref, skip) in enumerate(blocks):
            rows = pl.ds(i * per, per)
            state[rows, :width] = ref[pl.ds(skip, per), :]
            digits = ref[pl.ds(skip + per, 16), :].astype(jnp.float32)
            digits = jnp.concatenate([digits, jnp.zeros((LANES - 16, width), jnp.float32)])
            state[rows, width:] = dot_t(unit, digits.astype(jnp.bfloat16)).astype(jnp.bfloat16)
    else:
        state[...] = given[...]

    biases = bias_rows_of(bias_ref, layer, len(groups))
    gain = gain_ref[layer : layer + 1, :].astype(jnp.float32)

    def body(t, carry):
        rows = pl.ds(pl.multiple_of(t * tile, tile), tile)
        old = state[rows, :width]
        digits = state[rows, width : width + LANES].astype(jnp.float32)
        ends = []
        for j in range(2):
            index = DIGIT * digits[:, 2 * j : 2 * j + 1] + digits[:, 2 * j + 1 : 2 * j + 2]
            picked = pick_rows(index.astype(jnp.int32), coarse_tab.shape[0])
            ends.append(dot(picked, coarse_tab[...]).astype(jnp.bfloat16))
        y = mlp(jnp.concatenate([old] + ends, axis=1), groups, biases, gain)
        state[rows, :width] = (old.astype(jnp.float32) + y).astype(jnp.bfloat16)
        return carry

    loop(state.shape[0] // tile, body)
    target = coarse_target(state, width, me, cp)
    latents = [new_fine[...], state[:, :width]]
    for out, half in zip(aggs, (1 - core, core)):
        places = [place_in_half((nh, at - half * nh)) for at in (recv_row[...], target)]
        sum_rows(out, nh - ch, places, latents)


def node_kernel(tile, layer, cores, spots, n_sums, cut, *refs):
    it = iter(refs)
    nodes, bias_ref, gain_ref = (next(it) for _ in range(3))
    sums = [[next(it) for _ in range(n)] for n in n_sums]
    if cut:
        groups = take_groups(it, spots, 2)
        parts = [(next(it), next(it)) for _ in range(2)]
    else:
        groups = take_groups(it, spots, cores)
    out, agg_ref, *far = it
    if cut:
        group = lax.axis_index("groups")
        for ref, (mine, other) in zip(far, parts):
            ref[:, pl.ds(pl.multiple_of(group * cut, LANES), cut)] = mine[:, :cut]
            ref[:, pl.ds(pl.multiple_of((1 - group) * cut, LANES), cut)] = other[:, :cut]
        groups.append([[[(ref, at, to) for _, at, to in pieces] for pieces in spots] for ref in far])
    nh = out.shape[0]
    agg = []
    for terms in sums:
        total = terms[0][...].astype(jnp.float32)
        for more in terms[1:]:
            total = total + more[...].astype(jnp.float32)
        agg.append(total.astype(jnp.bfloat16))
    if len(agg) > 1:
        row = lax.broadcasted_iota(jnp.int32, (nh, 1), 0)
        order = pick_rows(place_in_half((nh, row)), nh)
        agg = [dot(order, jnp.concatenate(agg)).astype(jnp.bfloat16)]
    agg_ref[...] = agg[0]
    biases = bias_rows_of(bias_ref, STEPS + layer, len(groups))
    gain = gain_ref[layer : layer + 1, :].astype(jnp.float32)
    core = core_index()
    half = nodes.shape[0] // 2
    for t in range(nh // tile):
        rows = pl.ds(t * tile, tile)
        old = nodes[pl.ds(pl.multiple_of(core * half + t * tile, tile), tile), :]
        x = jnp.concatenate([old, agg_ref[rows, :]], axis=1)
        y = mlp(x, groups, biases, gain)
        out[rows, :] = (old.astype(jnp.float32) + y).astype(jnp.bfloat16)


def divisor(count, most, unit=16):
    best = unit
    for size in range(unit, min(most, count) + 1, unit):
        if count % size == 0:
            best = size
    return best


def local(
    nodes,
    fine_edges,
    fine_send,
    fine_recv,
    halo_send,
    coarse_edges,
    coarse_send,
    coarse_recv,
    edge_w1,
    edge_b1,
    edge_w2,
    edge_gain,
    node_w1,
    node_b1,
    node_w2,
    node_gain,
):
    count, width = nodes.shape
    hr = halo_send.shape[0] // 2
    cp = count // STRIDE
    nh = count // 2
    fine_count = fine_edges.shape[0]
    parts = lax.axis_size("mesh")
    cores = lax.axis_size("feat")
    core = core_index()

    def swap(x):
        return lax.ppermute(x, "feat", [(i, i ^ 1) for i in range(cores)])

    def across(x):
        return lax.ppermute(x, "feat", [(i, i ^ 2) for i in range(cores)])

    def shift(x, by):
        return lax.ppermute(x, "mesh", [(i, (i + by) % parts) for i in range(parts)])

    def both(x):
        return [x, swap(x)]

    def after(xs):
        return lax.optimization_barrier(tuple(xs))

    two = cores == 4

    def spread(pack):
        return across(pack) if two else lax.all_gather(pack, "feat", axis=0)

    def shards(pack, far):
        if two:
            return both(pack) + both(far)
        return [far[i] for i in range(cores)]

    k, kn = edge_w1.shape[2], node_w1.shape[2]
    w_hidden = edge_w1.shape[1]
    halo_row = halo_send.reshape(1, 2 * hr)
    own_coarse = coarse_edges.shape[0]
    coarse_count = own_coarse * parts
    lanes = kn + width
    cut = lanes // 2 if two and lax.axis_size("groups") == 2 else 0
    plans = [
        [(2, 0, 0), (3, 0, kn)],
        [(2, 1, 0), (3, 1, kn)],
        [(1, 1, 0)],
        [(0, 1, 0)],
    ] + ([[], []] if cut else [])
    halves = {4: ((0, 0), (2, cut)), 5: ((1, 0),)} if cut else {}

    def copying(kernel, args, scratch, shapes, n_copies, name):
        return call(
            kernel,
            tuple(bf16(*shape) for shape in shapes),
            args,
            scratch=scratch
            + [pltpu.VMEM(shape, jnp.bfloat16) for shape in shapes]
            + [pltpu.SemaphoreType.DMA((n_copies,))],
            memory=[pl.ANY] * len(args),
            out_memory=pl.ANY,
            limit=3 * VMEM_BYTES,
            name=name,
        )

    block = own_coarse + 16
    near, far = hr // 2 + cp // 2 + block, cp // 2 + block
    direct = parts != RELAYED
    shapes = [(w_hidden, k + width + LANES), (near, width), (near, width)]
    shapes += [(far, width)] * direct + [(cp, width), (block, width)]
    small = [edge_b1, node_b1, nodes, halo_row, coarse_edges]
    small += [x.reshape(1, own_coarse) for x in (coarse_send, coarse_recv)]
    first_pack, *rows_out, coarse_own, block = copying(
        functools.partial(first_kernel, 2 + len(small), len(shapes)),
        [edge_w1, edge_w2, *small],
        [pltpu.VMEM(x.shape, x.dtype) for x in small],
        shapes,
        len(small) + 2 + len(shapes),
        "first_weights_and_rows",
    )
    widths = [lanes, lanes, width, k] + ([cut + width // 2, cut] if cut else [])
    later = copying(
        functools.partial(later_kernel, plans, halves),
        [edge_w1, edge_w2, node_w1, node_w2],
        [],
        [(w_hidden, n) for n in widths],
        sum(len(p) for p in plans) + len(widths),
        "later_weights",
    )
    node_spots = (((0, 0, kn),), ((0, kn, lanes),))

    send_col = fine_send.reshape(fine_count, 1)
    recv_col = fine_recv.reshape(fine_count, 1)
    recv_row = fine_recv.reshape(1, fine_count)
    tile = divisor(fine_count, 768)
    ctile = divisor(coarse_count, 384)
    hidden = w_hidden * cores
    sizes = (count, hr, cp, parts, cores)
    bias_rows = None

    def node_rows_out(own, other):
        near, far = bf16(hr // 2 + cp // 2, width), bf16(cp // 2, width)
        return call(
            functools.partial(halo_kernel, False),
            (near, near, *[far] * direct, bf16(cp, width), bf16(count, width)),
            [own, other, halo_row],
            name="halo_rows",
        )

    def exchange(to_prev, to_next, *to_far):
        between = [shift(to_far[0], by) for by in range(2, parts - 1)] if to_far else []
        return [shift(to_next, 1), *between, shift(to_prev, parts - 1)]

    def far_rows(moved):
        if parts != RELAYED:
            return moved[1:-1]
        rows = moved[0].shape[0] - hr // 2
        return [shift(call(tail_kernel, bf16(rows, width), [moved[0]], name="far_rows"), 1)]

    def gather(nodes, *carried):
        return call(
            functools.partial(gather_kernel, tile),
            (*(bf16(*x.shape) for x in carried), bf16(fine_count, width), bf16(fine_count, width)),
            [nodes, send_col, recv_col, *carried],
            flops=4 * fine_count * count * width,
            name="gather_rows",
        )

    def fine_update(s, fine, sent, received, halo, weights, spots, halved=0):
        outs = [bf16(fine_count, width)]
        if s == 0:
            outs.append(jax.ShapeDtypeStruct((8, hidden), jnp.float32))
        fine_rows = nh - cp // 2
        outs.append(bf16(fine_rows, width))
        return call(
            functools.partial(fine_kernel, tile, sizes, spots, s, halved),
            tuple(outs),
            [fine, sent, received, send_col, recv_row, edge_gain] + halo + weights + ([bias_rows] if s else []),
            scratch=[pltpu.VMEM((2 * hr, width), jnp.bfloat16)]
            + ([pltpu.VMEM((w_hidden, width), jnp.bfloat16)] * 2 if halved else []),
            flops=8 * fine_count * width * hidden,
            name="fine_edges",
        )

    def own_sums(new_fine):
        return call(
            functools.partial(own_sums_kernel, nh),
            jax.ShapeDtypeStruct((nh - cp // 2, width), jnp.float32),
            [new_fine, recv_row],
            name="own_sums",
        )

    def coarse_update(s, new_fine, coarse_own, state, arrived, weights, spots, halved=0):
        aggs = [bf16(cp // 2, width), jax.ShapeDtypeStruct((cp // 2, width), jnp.float32)]
        return call(
            functools.partial(coarse_kernel, ctile, sizes, spots, s, halved),
            (bf16(coarse_count, width + LANES), *aggs),
            [new_fine, recv_row, coarse_own, edge_gain, bias_rows, state] + arrived + weights,
            scratch=[pltpu.VMEM((parts * cp, width), jnp.bfloat16)]
            + ([pltpu.VMEM((w_hidden, width), jnp.bfloat16)] * 2 if halved else []),
            flops=COARSE_FLOPS[s],
            name="coarse_edges_and_sums",
        )

    def node_update(s, nodes, sums, weights, spots, cut=0):
        far = [pltpu.VMEM((w_hidden, 2 * cut), jnp.bfloat16)] * 2 if cut else []
        rows = sum(part[0].shape[0] for part in sums)
        return both(
            call(
                functools.partial(node_kernel, rows, s, cores, spots, [len(part) for part in sums], cut),
                bf16(rows, width),
                [nodes, bias_rows, node_gain] + [x for part in sums for x in part] + weights,
                scratch=[pltpu.VMEM((rows, width), jnp.bfloat16), *far],
                name="node_update",
            )
        )

    def core_sum(agg_own, agg_other):
        return call(add_kernel, bf16(*agg_own.shape), [agg_own, swap(agg_other)], name="core_sum")

    def chip_sums(partial):
        if two:
            return [partial, across(partial)]
        every = lax.all_gather(partial, "feat", axis=0)
        every = every.reshape(cores // 2, 2, *partial.shape).astype(jnp.float32)
        return [lax.dynamic_index_in_dim(every.sum(axis=0), core, 0, keepdims=False)]

    def halo_of(moved, swapped):
        return [moved[0], swapped[0], moved[-1], swapped[-1]]

    def pairs(moved, swapped):
        return [x for pair in zip(moved, swapped) for x in pair]

    def other_group(x):
        return lax.ppermute(x, "groups", [(0, 1), (1, 0)])

    far_first = spread(first_pack)
    moved = exchange(*rows_out)
    send_col, recv_col, recv_row, *later = after(
        (send_col, recv_col, recv_row, *later, rows_out[0])
    )[:-1]
    node0, node1, edge1_w2, edge1, *sent_halves = later
    if two:
        near, sent, received = gather(nodes, swap(first_pack))
    else:
        sent, received = gather(nodes)
    moved[0], moved[-1], far_first, sent = after((moved[0], moved[-1], far_first, sent))
    relayed = far_rows(moved)
    swapped = {i: swap(moved[i]) for i in (0, -1)}
    weights = [first_pack, near, *both(far_first)] if two else shards(first_pack, far_first)
    spots = (((0, 0, k),), ((0, k, k + width),))
    far = across(sent_halves[0]) if cut else spread(edge1_w2)
    fine_edges, bias_rows, other = fine_update(
        0, fine_edges, sent, received, halo_of(moved, swapped), weights, spots
    )
    other, far, *relayed = after((other, far, *relayed))
    swapped = [swapped[0], *(swap(m) for m in relayed), swapped[-1]]
    moved = [moved[0], *relayed, moved[-1]]
    partial = core_sum(own_sums(fine_edges), other)
    fine_part = chip_sums(partial)
    state, other, own = coarse_update(
        0, fine_edges, coarse_own, block, pairs(moved, swapped), weights, spots
    )
    if cut:
        node_part, edge_part = call(
            parts_kernel, (bf16(w_hidden, cut), bf16(w_hidden, width // 2)), [far], name="parts"
        )
        others = other_group(node_part)
        own, others = after((own, others))
    sums = [fine_part, chip_sums(core_sum(own, other))]
    if cut:
        weights = both(node0) + pairs(both(far), both(others))
    else:
        weights = shards(node0, spread(node0))
    sums[1][-1], edge1 = after((sums[1][-1], edge1))
    mixed = far
    far = spread(edge1)
    halves = node_update(0, nodes, sums, weights, node_spots, cut)

    *rows_out, coarse_own, nodes = node_rows_out(*halves)
    moved = exchange(*rows_out)
    sent, received = gather(nodes)
    if cut:
        edge_part = other_group(edge_part)
        *moved, far, sent, edge_part = after((*moved, far, sent, edge_part))
    else:
        *moved, far, sent = after((*moved, far, sent))
    halved = width // 2 if cut else 0
    if cut:
        w2_parts = pairs(both(mixed), both(edge_part))
        weights = pairs(both(edge1), both(edge1_w2)) + both(far) + w2_parts
    else:
        weights = pairs(shards(edge1, far), shards(edge1_w2, mixed))
    spots = (((0, 0, k),), ((1, 0, width),))
    relayed = far_rows(moved)
    swapped = {i: swap(moved[i]) for i in (0, -1)}
    far = across(sent_halves[1]) if cut else spread(node1)
    fine_edges, other = fine_update(
        1, fine_edges, sent, received, halo_of(moved, swapped), weights, spots, halved
    )
    other, far, *relayed = after((other, far, *relayed))
    swapped = [swapped[0], *(swap(m) for m in relayed), swapped[-1]]
    moved = [moved[0], *relayed, moved[-1]]
    partial = core_sum(own_sums(fine_edges), other)
    fine_part = chip_sums(partial)
    state, other, own = coarse_update(
        1, fine_edges, coarse_own, state, pairs(moved, swapped), weights, spots, halved
    )
    if cut:
        others = other_group(far)
        own, others = after((own, others))
        weights = both(node1) + pairs(both(far), both(others))
    else:
        weights = shards(node1, far)
    sums = [fine_part, chip_sums(core_sum(own, other))]
    halves = node_update(1, nodes, sums, weights, node_spots, cut)
    return call(
        join_kernel,
        bf16(count, width),
        halves,
        scratch=[pltpu.SemaphoreType.DMA((2,))],
        out_memory=pl.ANY,
        name="nodes_out",
    )


def solution(mesh):
    placed = (
        P(("groups", "mesh"), None),
        P(("groups", "mesh", "feat"), None),
        P(("groups", "mesh", "feat")),
        P(("groups", "mesh", "feat")),
        P(("groups", "mesh")),
        P(("groups", "mesh", "feat"), None),
        P(("groups", "mesh", "feat")),
        P(("groups", "mesh", "feat")),
        P(None, "feat", None),
        P(None, "feat"),
        P(None, "feat", None),
        P(),
        P(None, "feat", None),
        P(None, "feat"),
        P(None, "feat", None),
        P(),
    )
    return jax.shard_map(
        local, mesh=mesh, in_specs=placed, out_specs=P(("groups", "mesh"), None), check_vma=False
    )
```

```python
import functools

import jax
import jax.numpy as jnp
from jax import lax
from jax.experimental import pallas as pl
from jax.experimental.pallas import tpu as pltpu
from jax.sharding import PartitionSpec as P

STEPS = 2
STRIDE = 8
LANES = 128
COARSE_FLOPS = (0, 0)
RELAYED = 4
DIGIT = 64
VMEM_BYTES = 20 * 1024 * 1024


def dot(a, b):
    return jnp.dot(a, b, preferred_element_type=jnp.float32)


def dot_t(a, b):
    return lax.dot_general(a, b, (((1,), (1,)), ((), ())), preferred_element_type=jnp.float32)


def pick_rows(index, count):
    spots = lax.broadcasted_iota(jnp.int32, (index.shape[0], count), 1)
    return (spots == index).astype(jnp.bfloat16)


def silu(x):
    half = 0.5 * x
    return half * jnp.tanh(half) + half


def layer_norm(values, gain):
    centred = values - jnp.mean(values, axis=-1, keepdims=True)
    row_var = jnp.mean(centred * centred, axis=-1, keepdims=True)
    return centred * lax.rsqrt(row_var + 1e-05) * gain


def along_lanes(pieces):
    return jnp.concatenate([pack[:, at:to] for pack, at, to in pieces], axis=1)


def mlp(x, groups, biases, gain):
    total = None
    for shards, bias in zip(groups, biases):
        w_in = jnp.concatenate([along_lanes(pieces) for pieces, _ in shards])
        w_out = jnp.concatenate([along_lanes(pieces) for _, pieces in shards])
        act = silu(dot_t(x, w_in) + bias).astype(jnp.bfloat16)
        part = dot(act, w_out)
        total = part if total is None else total + part
    return layer_norm(total, gain)


def take_groups(it, spots, cores):
    n_packs = 1 + max(pack for pieces in spots for pack, _, _ in pieces)
    groups = []
    for _ in range(cores // 2):
        shards = []
        for _ in range(2):
            refs = [next(it) for _ in range(n_packs)]
            shards.append([[(refs[pack], at, to) for pack, at, to in pieces] for pieces in spots])
        groups.append(shards)
    return groups


def loop(steps, body):
    lax.fori_loop(0, steps, body, 0, unroll=2 if steps % 2 == 0 else 1)


def call(kernel, out_shape, args, scratch=(), flops=0, nbytes=0, memory=None, out_memory=pltpu.VMEM, limit=VMEM_BYTES, name=None):
    in_specs = [pl.BlockSpec(memory_space=m) for m in memory or [pltpu.VMEM] * len(args)]
    out_specs = jax.tree.map(lambda _: pl.BlockSpec(memory_space=out_memory), out_shape)
    return pl.pallas_call(
        kernel,
        out_shape=out_shape,
        in_specs=in_specs,
        out_specs=out_specs,
        scratch_shapes=list(scratch),
        compiler_params=pltpu.CompilerParams(vmem_limit_bytes=limit),
        cost_estimate=pl.CostEstimate(flops=flops, bytes_accessed=nbytes, transcendentals=0),
        name=name,
    )(*args)


def bf16(*shape):
    return jax.ShapeDtypeStruct(shape, jnp.bfloat16)


def core_index():
    return lax.rem(lax.axis_index("feat"), 2)


def join_halves(out, own, other):
    core, nh = core_index(), own.shape[0]
    out[pl.ds(pl.multiple_of(core * nh, nh), nh), :] = own[...]
    out[pl.ds(pl.multiple_of((1 - core) * nh, nh), nh), :] = other[...]


def join_kernel(own, other, out, sems):
    core, nh = core_index(), own.shape[0]
    copies = []
    for i, (half, ref) in enumerate(((core, own), (1 - core, other))):
        spot = out.at[pl.ds(pl.multiple_of(half * nh, nh), nh), :]
        copies.append(pltpu.make_async_copy(ref, spot, sems.at[i]))
        copies[i].start()
    for copy in copies:
        copy.wait()


def add_kernel(own, arrived, out):
    out[...] = (own[...] + arrived[...].astype(jnp.float32)).astype(out.dtype)


def index_digits(ref, lanes):
    index = ref[...]
    high = lax.shift_right_logical(index, DIGIT.bit_length() - 1)
    rows = jnp.concatenate([high, index & (DIGIT - 1)]).astype(jnp.float32)
    if lanes == index.shape[1]:
        return rows
    return jnp.concatenate([rows, jnp.zeros((2, lanes - index.shape[1]), jnp.float32)], axis=1)


def to_column(ref):
    count = ref.shape[1]
    rows = jnp.concatenate([index_digits(ref, count), jnp.zeros((6, count), jnp.float32)])
    unit = lax.broadcasted_iota(jnp.int32, (count, count), 0)
    unit = unit == lax.broadcasted_iota(jnp.int32, (count, count), 1)
    digits = dot_t(unit.astype(jnp.bfloat16), rows.astype(jnp.bfloat16))
    return (DIGIT * digits[:, 0:1] + digits[:, 1:2]).astype(jnp.int32)


def halo_kernel(first, *refs):
    if first:
        nodes, halo, edges, send, recv, to_prev, to_next, *far, coarse, block = refs
        count, width = edges.shape
        block[0:count, :] = edges[...]
        digits = [index_digits(ref, width) for ref in (send, recv)]
        digits.append(jnp.zeros((16 - 4, width), jnp.float32))
        block[count : count + 16, :] = jnp.concatenate(digits).astype(jnp.bfloat16)
    else:
        own, other, halo, to_prev, to_next, *far, coarse, nodes = refs
        join_halves(nodes, own, other)
    core = core_index()
    count = nodes.shape[0]
    hr, cp = halo.shape[1] // 2, coarse.shape[0]
    hh, ch = hr // 2, cp // 2
    index = to_column(halo)
    mine = [jnp.where(core == 0, x[:hh], x[hh:]) for x in (index[:hr], index[hr:])]
    table = nodes[...]
    rows = dot(pick_rows(jnp.concatenate(mine), count), table).astype(jnp.bfloat16)
    every = STRIDE * lax.broadcasted_iota(jnp.int32, (cp, 1), 0)
    coarse[...] = dot(pick_rows(every, count), table).astype(jnp.bfloat16)
    mine = coarse[pl.ds(pl.multiple_of(core * ch, ch), ch), :]
    to_prev[pl.ds(0, hh), :] = rows[:hh]
    to_next[pl.ds(0, hh), :] = rows[hh:]
    for out, skip in [(to_prev, hh), (to_next, hh)] + [(ref, 0) for ref in far]:
        out[pl.ds(skip, ch), :] = mine
        if first:
            out[pl.ds(skip + ch, block.shape[0]), :] = block[...]


class Copies:
    def __init__(self, sems):
        self.sems, self.started = sems, []

    def start(self, src, dst):
        copy = pltpu.make_async_copy(src, dst, self.sems.at[len(self.started)])
        copy.start()
        self.started.append(copy)
        return copy


def first_kernel(n_in, n_out, *refs):
    edge_w1, edge_w2, *given = refs[:n_in]
    outs = refs[n_in : n_in + n_out]
    small, made, sems = refs[n_in + n_out :][: len(given)], refs[-1 - n_out : -1], refs[-1]
    copies = Copies(sems)
    arriving = [copies.start(src, dst) for src, dst in zip(given, small)]
    pack, k = made[0], edge_w1.shape[2]
    loads = [
        copies.start(edge_w1.at[0], pack.at[:, 0:k]),
        copies.start(edge_w2.at[0], pack.at[:, k : k + edge_w2.shape[2]]),
    ]
    for copy in arriving:
        copy.wait()
    edge_b1, node_b1, nodes, halo, edges, send, recv = small
    hidden = edge_b1.shape[1]
    rows = [edge_b1[...].astype(jnp.float32), node_b1[...].astype(jnp.float32)]
    rows.append(jnp.zeros((16 - 2 * STEPS, hidden), jnp.float32))
    at = pack.shape[1] - LANES
    pack[0:16, at : at + hidden] = jnp.concatenate(rows).astype(jnp.bfloat16)
    halo_kernel(True, nodes, halo, edges, send, recv, *made[1:])
    for copy in loads:
        copy.wait()
    for copy in [copies.start(src, dst) for src, dst in zip(made, outs)]:
        copy.wait()


def later_kernel(plans, halves, *refs):
    source, outs, made, sems = refs[:4], refs[4 : 4 + len(plans)], refs[4 + len(plans) : -1], refs[-1]
    copies = Copies(sems)
    loads = []
    for plan, pack in zip(plans, made):
        parts = []
        for which, layer, at in plan:
            part = source[which].at[layer]
            parts.append(copies.start(part, pack.at[:, at : at + part.shape[1]]))
        loads.append(parts)
    group = lax.axis_index("groups")
    stores = []
    for i, parts in enumerate(loads):
        for copy in parts:
            copy.wait()
        for which, at in halves.get(i, ()):
            whole = made[which]
            lanes = whole.shape[1] // 2
            part = jnp.where(group == 0, whole[:, :lanes], whole[:, lanes:])
            made[i][:, at : at + lanes] = part
        stores.append(copies.start(made[i], outs[i]))
    for copy in stores:
        copy.wait()


def parts_kernel(pack, first, last):
    first[...] = pack[:, : first.shape[1]]
    last[...] = pack[:, first.shape[1] :]


def tail_kernel(rows, out):
    out[...] = rows[pl.ds(rows.shape[0] - out.shape[0], out.shape[0]), :]


def gather_kernel(tile, nodes, send, recv, *refs):
    carried, (sent, received) = refs[: len(refs) - 2], refs[len(refs) - 2 :]
    count = nodes.shape[0]
    if carried:
        carried[1][...] = carried[0][...]

    def body(t, carry):
        rows = pl.ds(pl.multiple_of(t * tile, tile), tile)
        table = nodes[...]
        sent[rows, :] = dot(pick_rows(send[rows, :], count), table).astype(jnp.bfloat16)
        safe = jnp.minimum(recv[rows, :], count - 1)
        received[rows, :] = dot(pick_rows(safe, count), table).astype(jnp.bfloat16)
        return carry

    loop(send.shape[0] // tile, body)


def bias_rows_of(bias_ref, line, n_groups):
    per = bias_ref.shape[1] // n_groups
    return [bias_ref[line : line + 1, g * per : (g + 1) * per] for g in range(n_groups)]


def far_weights(halved, k, w_in, parts, w_out):
    lanes = halved
    group = lax.axis_index("groups")
    for ref, pair in zip(w_out, parts):
        for who, part in zip((group, 1 - group), pair):
            spot = pl.ds(pl.multiple_of(who * lanes, LANES), lanes)
            ref[:, spot] = part[:, part.shape[1] - lanes :]
    return [[[(w, 0, k)], [(ref, 0, ref.shape[1])]] for w, ref in zip(w_in, w_out)]


def half_sums(out, half, nh, new_fine, recv_row):
    sum_rows(out, 0, [place_in_half((nh, recv_row[...] - half * nh))], [new_fine[...]])


def own_sums_kernel(nh, new_fine, recv_row, out):
    half_sums(out, core_index(), nh, new_fine, recv_row)


def fine_kernel(tile, sizes, spots, layer, halved, *refs):
    count, hr, cp, parts, cores = sizes
    it = iter(refs)
    fine, sent, received, send, recv_row, gain_ref = (next(it) for _ in range(6))
    prev, nxt = ((next(it), next(it)) for _ in range(2))
    groups = take_groups(it, spots, 2 if halved else cores)
    far_in = [next(it) for _ in range(2 if halved else 0)]
    parts = [(next(it), next(it)) for _ in far_in]
    bias_in = None if layer == 0 else next(it)
    new_fine = next(it)
    bias_out = next(it) if layer == 0 else None
    agg_other, halo_tab, *far_out = it

    core = core_index()
    width = gain_ref.shape[-1]
    hh = hr // 2
    for side, pair in ((0, prev), (hr, nxt)):
        for who, ref in zip((core, 1 - core), pair):
            halo_tab[pl.ds(pl.multiple_of(side + who * hh, hh), hh), :] = ref[pl.ds(0, hh), :]

    if layer == 0:
        spot = 0
        for shards in groups:
            for _, [(pack, _, at)] in shards:
                hidden = pack.shape[0]
                rows = pack[0:16, at : at + hidden].astype(jnp.float32)
                bias_out[:, spot : spot + hidden] = rows[:8]
                spot += hidden
    if halved:
        groups.append(far_weights(halved, 3 * width, far_in, parts, far_out))
    biases = bias_rows_of(bias_out if layer == 0 else bias_in, layer, len(groups))
    gain = gain_ref[layer : layer + 1, :].astype(jnp.float32)

    def body(t, carry):
        rows = pl.ds(pl.multiple_of(t * tile, tile), tile)
        border = dot(pick_rows(send[rows, :] - count, 2 * hr), halo_tab[...])
        senders = (sent[rows, :].astype(jnp.float32) + border).astype(jnp.bfloat16)
        old = fine[rows, :]
        x = jnp.concatenate([old, senders, received[rows, :]], axis=1)
        y = mlp(x, groups, biases, gain)
        new_fine[rows, :] = (old.astype(jnp.float32) + y).astype(jnp.bfloat16)
        return carry

    loop(fine.shape[0] // tile, body)
    half_sums(agg_other, 1 - core, count // 2, new_fine, recv_row)


def coarse_target(state, width, me, cp):
    lane = lax.broadcasted_iota(jnp.int32, (8, LANES), 1)
    weights = jnp.where(lane == 2, float(DIGIT), jnp.where(lane == 3, 1.0, 0.0)).astype(jnp.bfloat16)
    near = dot_t(weights, state[:, width : width + LANES])[:1, :].astype(jnp.int32) - me * cp
    return jnp.where((near >= 0) & (near < cp), near * STRIDE, -1)


def place_in_half(row):
    count, row = row
    group, rest = lax.shift_right_logical(row, 3), row & (STRIDE - 1)
    fine_rows = count - count // STRIDE
    place = jnp.where(rest == 0, fine_rows + group, (STRIDE - 1) * group + rest - 1)
    return jnp.where((row >= 0) & (row < count), place, -1)


def sum_rows(out, first, places, latents):
    total = None
    for place, latent in zip(places, latents):
        rows = lax.broadcasted_iota(jnp.int32, (out.shape[0], place.shape[1]), 0) + first
        part = dot((rows == place).astype(jnp.bfloat16), latent)
        total = part if total is None else total + part
    out[...] = total.astype(out.dtype)


def coarse_kernel(tile, sizes, spots, layer, halved, *refs):
    count, hr, cp, parts, cores = sizes
    it = iter(refs)
    new_fine, recv_row, coarse_own, gain_ref, bias_ref = (next(it) for _ in range(5))
    given = next(it)
    arrived = [(next(it), next(it)) for _ in range(parts - 1)]
    groups = take_groups(it, spots, 2 if halved else cores)
    far_in = [next(it) for _ in range(2 if halved else 0)]
    halves = [(next(it), next(it)) for _ in far_in]
    state, *aggs = (next(it) for _ in range(3))
    coarse_tab, *far_out = it

    core, me = core_index(), lax.axis_index("mesh")
    width = gain_ref.shape[-1]
    hh, ch, nh = hr // 2, cp // 2, count // 2
    if halved:
        groups.append(far_weights(halved, 3 * width, far_in, halves, far_out))

    coarse_tab[pl.ds(pl.multiple_of(me * cp, cp), cp), :] = coarse_own[...]
    for i, pair in enumerate(arrived):
        owner = lax.rem(me + parts - 1 - i, parts)
        skip = hh if i in (0, parts - 2) else 0
        for who, ref in zip((core, 1 - core), pair):
            spot = pl.multiple_of(owner * cp + who * ch, ch)
            coarse_tab[pl.ds(spot, ch), :] = ref[pl.ds(skip, ch), 0:width]
    if layer == 0:
        per = given.shape[0] - 16
        lane = lax.broadcasted_iota(jnp.int32, (per, width), 1)
        unit = (lane == lax.broadcasted_iota(jnp.int32, (per, width), 0)).astype(jnp.bfloat16)
        blocks = [(given, 0)]
        for i, (ref, _) in enumerate(arrived):
            blocks.append((ref, ch + (hh if i in (0, parts - 2) else 0)))
        for i, (ref, skip) in enumerate(blocks):
            rows = pl.ds(i * per, per)
            state[rows, :width] = ref[pl.ds(skip, per), :]
            digits = ref[pl.ds(skip + per, 16), :].astype(jnp.float32)
            digits = jnp.concatenate([digits, jnp.zeros((LANES - 16, width), jnp.float32)])
            state[rows, width:] = dot_t(unit, digits.astype(jnp.bfloat16)).astype(jnp.bfloat16)
    else:
        state[...] = given[...]

    biases = bias_rows_of(bias_ref, layer, len(groups))
    gain = gain_ref[layer : layer + 1, :].astype(jnp.float32)

    def body(t, carry):
        rows = pl.ds(pl.multiple_of(t * tile, tile), tile)
        old = state[rows, :width]
        digits = state[rows, width : width + LANES].astype(jnp.float32)
        ends = []
        for j in range(2):
            index = DIGIT * digits[:, 2 * j : 2 * j + 1] + digits[:, 2 * j + 1 : 2 * j + 2]
            picked = pick_rows(index.astype(jnp.int32), coarse_tab.shape[0])
            ends.append(dot(picked, coarse_tab[...]).astype(jnp.bfloat16))
        y = mlp(jnp.concatenate([old] + ends, axis=1), groups, biases, gain)
        state[rows, :width] = (old.astype(jnp.float32) + y).astype(jnp.bfloat16)
        return carry

    loop(state.shape[0] // tile, body)
    target = coarse_target(state, width, me, cp)
    latents = [new_fine[...], state[:, :width]]
    for out, half in zip(aggs, (1 - core, core)):
        places = [place_in_half((nh, at - half * nh)) for at in (recv_row[...], target)]
        sum_rows(out, nh - ch, places, latents)


def node_kernel(tile, layer, cores, spots, n_sums, cut, *refs):
    it = iter(refs)
    nodes, bias_ref, gain_ref = (next(it) for _ in range(3))
    sums = [[next(it) for _ in range(n)] for n in n_sums]
    if cut:
        groups = take_groups(it, spots, 2)
        parts = [(next(it), next(it)) for _ in range(2)]
    else:
        groups = take_groups(it, spots, cores)
    out, agg_ref, *far = it
    if cut:
        group = lax.axis_index("groups")
        for ref, (mine, other) in zip(far, parts):
            ref[:, pl.ds(pl.multiple_of(group * cut, LANES), cut)] = mine[:, :cut]
            ref[:, pl.ds(pl.multiple_of((1 - group) * cut, LANES), cut)] = other[:, :cut]
        groups.append([[[(ref, at, to) for _, at, to in pieces] for pieces in spots] for ref in far])
    nh = out.shape[0]
    agg = []
    for terms in sums:
        total = terms[0][...].astype(jnp.float32)
        for more in terms[1:]:
            total = total + more[...].astype(jnp.float32)
        agg.append(total.astype(jnp.bfloat16))
    if len(agg) > 1:
        row = lax.broadcasted_iota(jnp.int32, (nh, 1), 0)
        order = pick_rows(place_in_half((nh, row)), nh)
        agg = [dot(order, jnp.concatenate(agg)).astype(jnp.bfloat16)]
    agg_ref[...] = agg[0]
    biases = bias_rows_of(bias_ref, STEPS + layer, len(groups))
    gain = gain_ref[layer : layer + 1, :].astype(jnp.float32)
    core = core_index()
    half = nodes.shape[0] // 2
    for t in range(nh // tile):
        rows = pl.ds(t * tile, tile)
        old = nodes[pl.ds(pl.multiple_of(core * half + t * tile, tile), tile), :]
        x = jnp.concatenate([old, agg_ref[rows, :]], axis=1)
        y = mlp(x, groups, biases, gain)
        out[rows, :] = (old.astype(jnp.float32) + y).astype(jnp.bfloat16)


def divisor(count, most, unit=16):
    best = unit
    for size in range(unit, min(most, count) + 1, unit):
        if count % size == 0:
            best = size
    return best


def local(
    nodes,
    fine_edges,
    fine_send,
    fine_recv,
    halo_send,
    coarse_edges,
    coarse_send,
    coarse_recv,
    edge_w1,
    edge_b1,
    edge_w2,
    edge_gain,
    node_w1,
    node_b1,
    node_w2,
    node_gain,
):
    count, width = nodes.shape
    hr = halo_send.shape[0] // 2
    cp = count // STRIDE
    nh = count // 2
    fine_count = fine_edges.shape[0]
    parts = lax.axis_size("mesh")
    cores = lax.axis_size("feat")
    core = core_index()

    def swap(x):
        return lax.ppermute(x, "feat", [(i, i ^ 1) for i in range(cores)])

    def across(x):
        return lax.ppermute(x, "feat", [(i, i ^ 2) for i in range(cores)])

    def shift(x, by):
        return lax.ppermute(x, "mesh", [(i, (i + by) % parts) for i in range(parts)])

    def both(x):
        return [x, swap(x)]

    def after(xs):
        return lax.optimization_barrier(tuple(xs))

    two = cores == 4

    def spread(pack):
        return across(pack) if two else lax.all_gather(pack, "feat", axis=0)

    def shards(pack, far):
        if two:
            return both(pack) + both(far)
        return [far[i] for i in range(cores)]

    k, kn = edge_w1.shape[2], node_w1.shape[2]
    w_hidden = edge_w1.shape[1]
    halo_row = halo_send.reshape(1, 2 * hr)
    own_coarse = coarse_edges.shape[0]
    coarse_count = own_coarse * parts
    lanes = kn + width
    cut = lanes // 2 if two and lax.axis_size("groups") == 2 else 0
    plans = [
        [(2, 0, 0), (3, 0, kn)],
        [(2, 1, 0), (3, 1, kn)],
        [(1, 1, 0)],
        [(0, 1, 0)],
    ] + ([[], []] if cut else [])
    halves = {4: ((0, 0), (2, cut)), 5: ((1, 0),)} if cut else {}

    def copying(kernel, args, scratch, shapes, n_copies, name):
        return call(
            kernel,
            tuple(bf16(*shape) for shape in shapes),
            args,
            scratch=scratch
            + [pltpu.VMEM(shape, jnp.bfloat16) for shape in shapes]
            + [pltpu.SemaphoreType.DMA((n_copies,))],
            memory=[pl.ANY] * len(args),
            out_memory=pl.ANY,
            limit=3 * VMEM_BYTES,
            name=name,
        )

    block = own_coarse + 16
    near, far = hr // 2 + cp // 2 + block, cp // 2 + block
    direct = parts != RELAYED
    shapes = [(w_hidden, k + width + LANES), (near, width), (near, width)]
    shapes += [(far, width)] * direct + [(cp, width), (block, width)]
    small = [edge_b1, node_b1, nodes, halo_row, coarse_edges]
    small += [x.reshape(1, own_coarse) for x in (coarse_send, coarse_recv)]
    first_pack, *rows_out, coarse_own, block = copying(
        functools.partial(first_kernel, 2 + len(small), len(shapes)),
        [edge_w1, edge_w2, *small],
        [pltpu.VMEM(x.shape, x.dtype) for x in small],
        shapes,
        len(small) + 2 + len(shapes),
        "first_weights_and_rows",
    )
    widths = [lanes, lanes, width, k] + ([cut + width // 2, cut] if cut else [])
    later = copying(
        functools.partial(later_kernel, plans, halves),
        [edge_w1, edge_w2, node_w1, node_w2],
        [],
        [(w_hidden, n) for n in widths],
        sum(len(p) for p in plans) + len(widths),
        "later_weights",
    )
    node_spots = (((0, 0, kn),), ((0, kn, lanes),))

    send_col = fine_send.reshape(fine_count, 1)
    recv_col = fine_recv.reshape(fine_count, 1)
    recv_row = fine_recv.reshape(1, fine_count)
    tile = divisor(fine_count, 768)
    ctile = divisor(coarse_count, 384)
    hidden = w_hidden * cores
    sizes = (count, hr, cp, parts, cores)
    bias_rows = None

    def node_rows_out(own, other):
        near, far = bf16(hr // 2 + cp // 2, width), bf16(cp // 2, width)
        return call(
            functools.partial(halo_kernel, False),
            (near, near, *[far] * direct, bf16(cp, width), bf16(count, width)),
            [own, other, halo_row],
            name="halo_rows",
        )

    def exchange(to_prev, to_next, *to_far):
        between = [shift(to_far[0], by) for by in range(2, parts - 1)] if to_far else []
        return [shift(to_next, 1), *between, shift(to_prev, parts - 1)]

    def far_rows(moved):
        if parts != RELAYED:
            return moved[1:-1]
        rows = moved[0].shape[0] - hr // 2
        return [shift(call(tail_kernel, bf16(rows, width), [moved[0]], name="far_rows"), 1)]

    def gather(nodes, *carried):
        return call(
            functools.partial(gather_kernel, tile),
            (*(bf16(*x.shape) for x in carried), bf16(fine_count, width), bf16(fine_count, width)),
            [nodes, send_col, recv_col, *carried],
            flops=4 * fine_count * count * width,
            name="gather_rows",
        )

    def fine_update(s, fine, sent, received, halo, weights, spots, halved=0):
        outs = [bf16(fine_count, width)]
        if s == 0:
            outs.append(jax.ShapeDtypeStruct((8, hidden), jnp.float32))
        fine_rows = nh - cp // 2
        outs.append(bf16(fine_rows, width))
        return call(
            functools.partial(fine_kernel, tile, sizes, spots, s, halved),
            tuple(outs),
            [fine, sent, received, send_col, recv_row, edge_gain] + halo + weights + ([bias_rows] if s else []),
            scratch=[pltpu.VMEM((2 * hr, width), jnp.bfloat16)]
            + ([pltpu.VMEM((w_hidden, width), jnp.bfloat16)] * 2 if halved else []),
            flops=8 * fine_count * width * hidden,
            name="fine_edges",
        )

    def own_sums(new_fine):
        return call(
            functools.partial(own_sums_kernel, nh),
            jax.ShapeDtypeStruct((nh - cp // 2, width), jnp.float32),
            [new_fine, recv_row],
            name="own_sums",
        )

    def coarse_update(s, new_fine, coarse_own, state, arrived, weights, spots, halved=0):
        aggs = [bf16(cp // 2, width), jax.ShapeDtypeStruct((cp // 2, width), jnp.float32)]
        return call(
            functools.partial(coarse_kernel, ctile, sizes, spots, s, halved),
            (bf16(coarse_count, width + LANES), *aggs),
            [new_fine, recv_row, coarse_own, edge_gain, bias_rows, state] + arrived + weights,
            scratch=[pltpu.VMEM((parts * cp, width), jnp.bfloat16)]
            + ([pltpu.VMEM((w_hidden, width), jnp.bfloat16)] * 2 if halved else []),
            flops=COARSE_FLOPS[s],
            name="coarse_edges_and_sums",
        )

    def node_update(s, nodes, sums, weights, spots, cut=0):
        far = [pltpu.VMEM((w_hidden, 2 * cut), jnp.bfloat16)] * 2 if cut else []
        rows = sum(part[0].shape[0] for part in sums)
        return both(
            call(
                functools.partial(node_kernel, rows, s, cores, spots, [len(part) for part in sums], cut),
                bf16(rows, width),
                [nodes, bias_rows, node_gain] + [x for part in sums for x in part] + weights,
                scratch=[pltpu.VMEM((rows, width), jnp.bfloat16), *far],
                name="node_update",
            )
        )

    def core_sum(agg_own, agg_other):
        return call(add_kernel, bf16(*agg_own.shape), [agg_own, swap(agg_other)], name="core_sum")

    def chip_sums(partial):
        if two:
            return [partial, across(partial)]
        every = lax.all_gather(partial, "feat", axis=0)
        every = every.reshape(cores // 2, 2, *partial.shape).astype(jnp.float32)
        return [lax.dynamic_index_in_dim(every.sum(axis=0), core, 0, keepdims=False)]

    def halo_of(moved, swapped):
        return [moved[0], swapped[0], moved[-1], swapped[-1]]

    def pairs(moved, swapped):
        return [x for pair in zip(moved, swapped) for x in pair]

    def other_group(x):
        return lax.ppermute(x, "groups", [(0, 1), (1, 0)])

    far_first = spread(first_pack)
    moved = exchange(*rows_out)
    send_col, recv_col, recv_row, *later = after(
        (send_col, recv_col, recv_row, *later, rows_out[0])
    )[:-1]
    node0, node1, edge1_w2, edge1, *sent_halves = later
    if two:
        near, sent, received = gather(nodes, swap(first_pack))
    else:
        sent, received = gather(nodes)
    moved[0], moved[-1], far_first, sent = after((moved[0], moved[-1], far_first, sent))
    relayed = far_rows(moved)
    swapped = {i: swap(moved[i]) for i in (0, -1)}
    weights = [first_pack, near, *both(far_first)] if two else shards(first_pack, far_first)
    spots = (((0, 0, k),), ((0, k, k + width),))
    far = across(sent_halves[0]) if cut else spread(edge1_w2)
    fine_edges, bias_rows, other = fine_update(
        0, fine_edges, sent, received, halo_of(moved, swapped), weights, spots
    )
    other, far, *relayed = after((other, far, *relayed))
    swapped = [swapped[0], *(swap(m) for m in relayed), swapped[-1]]
    moved = [moved[0], *relayed, moved[-1]]
    partial = core_sum(own_sums(fine_edges), other)
    fine_part = chip_sums(partial)
    state, other, own = coarse_update(
        0, fine_edges, coarse_own, block, pairs(moved, swapped), weights, spots
    )
    if cut:
        node_part, edge_part = call(
            parts_kernel, (bf16(w_hidden, cut), bf16(w_hidden, width // 2)), [far], name="parts"
        )
        others = other_group(node_part)
        own, others = after((own, others))
    sums = [fine_part, chip_sums(core_sum(own, other))]
    if cut:
        weights = both(node0) + pairs(both(far), both(others))
    else:
        weights = shards(node0, spread(node0))
    sums[1][-1], edge1 = after((sums[1][-1], edge1))
    mixed = far
    far = spread(edge1)
    halves = node_update(0, nodes, sums, weights, node_spots, cut)

    *rows_out, coarse_own, nodes = node_rows_out(*halves)
    moved = exchange(*rows_out)
    sent, received = gather(nodes)
    if cut:
        edge_part = other_group(edge_part)
        *moved, far, sent, edge_part = after((*moved, far, sent, edge_part))
    else:
        *moved, far, sent = after((*moved, far, sent))
    halved = width // 2 if cut else 0
    if cut:
        w2_parts = pairs(both(mixed), both(edge_part))
        weights = pairs(both(edge1), both(edge1_w2)) + both(far) + w2_parts
    else:
        weights = pairs(shards(edge1, far), shards(edge1_w2, mixed))
    spots = (((0, 0, k),), ((1, 0, width),))
    relayed = far_rows(moved)
    swapped = {i: swap(moved[i]) for i in (0, -1)}
    far = across(sent_halves[1]) if cut else spread(node1)
    fine_edges, other = fine_update(
        1, fine_edges, sent, received, halo_of(moved, swapped), weights, spots, halved
    )
    other, far, *relayed = after((other, far, *relayed))
    swapped = [swapped[0], *(swap(m) for m in relayed), swapped[-1]]
    moved = [moved[0], *relayed, moved[-1]]
    partial = core_sum(own_sums(fine_edges), other)
    fine_part = chip_sums(partial)
    state, other, own = coarse_update(
        1, fine_edges, coarse_own, state, pairs(moved, swapped), weights, spots, halved
    )
    if cut:
        others = other_group(far)
        own, others = after((own, others))
        weights = both(node1) + pairs(both(far), both(others))
    else:
        weights = shards(node1, far)
    sums = [fine_part, chip_sums(core_sum(own, other))]
    halves = node_update(1, nodes, sums, weights, node_spots, cut)
    return call(
        join_kernel,
        bf16(count, width),
        halves,
        scratch=[pltpu.SemaphoreType.DMA((2,))],
        out_memory=pl.ANY,
        name="nodes_out",
    )


def solution(mesh):
    placed = (
        P(("groups", "mesh"), None),
        P(("groups", "mesh", "feat"), None),
        P(("groups", "mesh", "feat")),
        P(("groups", "mesh", "feat")),
        P(("groups", "mesh")),
        P(("groups", "mesh", "feat"), None),
        P(("groups", "mesh", "feat")),
        P(("groups", "mesh", "feat")),
        P(None, "feat", None),
        P(None, "feat"),
        P(None, "feat", None),
        P(),
        P(None, "feat", None),
        P(None, "feat"),
        P(None, "feat", None),
        P(),
    )
    return jax.shard_map(
        local, mesh=mesh, in_specs=placed, out_specs=P(("groups", "mesh"), None), check_vma=False
    )
```
